32 devices in a mesh: group: 4 (over y, x), dp: 8 (over z, core).
Axes of the slice: x: 2, y: 2, z: 4, core: 2. Of those that a mesh axis runs over, the one named last changes fastest.
Arguments:
- train_images: float32 [256, 32, 32, 3], P(('group', 'dp')), may hold values from -6 to 6
- train_labels: int32 [256], P(('group', 'dp')), may hold values from 0 to 9
- flip_flags: int32 [256], P(('group', 'dp')), may hold values 0 or 1
- class_ids: int32 [256], P(('group', 'dp')), may hold values from 0 to 9
- clip_mask: int32 [256], P(('group', 'dp')), may hold values 0 or 1
- norm_flag: int32 [4], P('group'), may hold values from 0 to 1, as said below
- val_images: float32 [128, 32, 32, 3], P(('group', 'dp')), may hold values from -6 to 6
- val_labels: int32 [128], P(('group', 'dp')), may hold values from 0 to 9
- stem: float32 [3, 3, 3, 64], replicated, may hold values from -1.25 to 1.25
- convs: float32 [2, 3, 3, 64, 64], replicated, may hold values from -0.25 to 0.25
- norms: float32 [3, 2, 64], replicated, may hold values from -2.5 to 2.5
- head: float32 [65, 10], replicated, may hold values from -0.75 to 0.75
- m_stem: float32 [4, 3, 3, 3, 64], P('group'), may hold values from -0.00390625 to 0.00390625
- v_stem: float32 [4, 3, 3, 3, 64], P('group'), may hold values from 6e-09 to 2.4e-08
- m_convs: float32 [4, 2, 3, 3, 64, 64], P('group'), may hold values from -0.0034179688 to 0.0034179688
- v_convs: float32 [4, 2, 3, 3, 64, 64], P('group'), may hold values from 4e-09 to 1.6e-08
- m_norms: float32 [4, 3, 2, 64], P('group'), may hold values from -0.013671875 to 0.013671875
- v_norms: float32 [4, 3, 2, 64], P('group'), may hold values from 6.4e-08 to 2.56e-07
- m_head: float32 [4, 65, 10], P('group'), may hold values from -0.078125 to 0.078125
- v_head: float32 [4, 65, 10], P('group'), may hold values from 2.5e-06 to 1e-05
- mom_stem: float32 [3, 3, 3, 64], replicated, may hold values from -0.75 to 0.75
- mom_convs: float32 [2, 3, 3, 64, 64], replicated, may hold values from -0.75 to 0.75
- mom_norms: float32 [3, 2, 64], replicated, may hold values from -0.75 to 0.75
- mom_head: float32 [65, 10], replicated, may hold values from -0.75 to 0.75
Outputs:
- new_stem: float32 [3, 3, 3, 64], replicated
- new_convs: float32 [2, 3, 3, 64, 64], replicated
- new_norms: float32 [3, 2, 64], replicated
- new_head: float32 [65, 10], replicated
- low_stem: bfloat16 [3, 3, 3, 64], replicated
- low_convs: bfloat16 [2, 3, 3, 64, 64], replicated
- low_norms: bfloat16 [3, 2, 64], replicated
- low_head: bfloat16 [65, 10], replicated
- first_stem: float32 [4, 3, 3, 3, 64], P('group')
- first_convs: float32 [4, 2, 3, 3, 64, 64], P('group')
- first_norms: float32 [4, 3, 2, 64], P('group')
- first_head: float32 [4, 65, 10], P('group')
- second_stem: float32 [4, 3, 3, 3, 64], P('group')
- second_convs: float32 [4, 2, 3, 3, 64, 64], P('group')
- second_norms: float32 [4, 3, 2, 64], P('group')
- second_head: float32 [4, 65, 10], P('group')
- outer_stem: float32 [3, 3, 3, 64], replicated
- outer_convs: float32 [2, 3, 3, 64, 64], replicated
- outer_norms: float32 [3, 2, 64], replicated
- outer_head: float32 [65, 10], replicated
- group_loss: float32 [4], P('group')
The draws below stay inside these ranges and needn't reach their ends.
Inputs may be any that keep to these rules, and one draw needn't show every extreme that they name: `norm_flag`: both values occur in every draw.
All inputs are finite; a program needn't handle non-finite values. No bound on the sum of `flip_flags` or of `clip_mask` on one device may be relied on, other than what follows from the above.
Results may differ from the reference program's by a relative error of at most 0.001.
Values sent between devices are 32-bit elements; how exact they have to be, the bound alone decides.
No kernel may reach another device: no remote copies, remote signals or barrier semaphores. Data moves between devices by JAX's collectives and lax.ppermute only.
A program may use at most 192 MiB of HBM per device.

```python
import math
import jax
import jax.numpy as jnp
from jax import lax

C = 64
CLASSES = 10
SIDE = 32
STEP = 10
GROUPS = 4
TRAIN_ALL = 256
VAL_ALL = 128


def draw_norm_flag(key, part):
    start = jax.random.randint(jax.random.fold_in(key, 1), (), 0, GROUPS)
    bits = jax.random.randint(jax.random.fold_in(key, 2), (GROUPS,), 0, 2)
    place = (jnp.arange(GROUPS) - start) % GROUPS
    return jnp.where(place == 0, 0, jnp.where(place == 1, 1, bits)).astype(jnp.int32)


def with_ends(result, own_key, least, largest):
    spot = [jax.random.randint(jax.random.fold_in(own_key, axis), (), 0, length) for axis, length in enumerate(result.shape)]
    longest = result.shape.index(max(result.shape))
    next_to = spot[:longest] + [(spot[longest] + 1) % result.shape[longest]] + spot[longest + 1:]
    return result.at[tuple(spot)].set(least).at[tuple(next_to)].set(largest)


def steps_of(key, extent, split, low, top_value):
    factor_of = 1.0
    for position, blocks in split:
        steps = jax.random.uniform(jax.random.fold_in(jax.random.fold_in(key, 6), position), (blocks,), jnp.float32, low / len(split), top_value / len(split))
        factor_of = factor_of * jnp.repeat(jnp.exp(steps), extent[position] // blocks).reshape((-1,) + (1,) * (len(extent) - 1 - position))
    return factor_of


def centred(rng, dims, spread, limit, pieces=(), held_as=jnp.bfloat16):
    entries = jax.random.normal(rng, dims, jnp.float32) * spread
    if len(pieces) > 0:
        entries = steps_of(rng, dims, pieces, -0.22, 0.18) * entries
    return jnp.clip(entries, min=-limit, max=limit).astype(held_as)


def setup_inputs(seed: int = 0) -> dict:
    streams_of = jax.random.split(jax.random.key(seed), 25)
    train_images = centred(streams_of[0], (TRAIN_ALL, SIDE, SIDE, 3), 1.0, 6.0, ((0, 32),), jnp.float32)
    train_labels = with_ends(jax.random.randint(streams_of[1], (TRAIN_ALL,), 0, CLASSES), jax.random.fold_in(streams_of[1], 1), 0, CLASSES - 1).astype(jnp.int32)
    flip_flags = with_ends((jax.random.randint(streams_of[2], (TRAIN_ALL,), 0, 5) < 2).astype(jnp.int32), jax.random.fold_in(streams_of[2], 1), 0, 1)
    class_ids = with_ends(jax.random.randint(streams_of[3], (TRAIN_ALL,), 0, CLASSES), jax.random.fold_in(streams_of[3], 1), 0, CLASSES - 1).astype(jnp.int32)
    clip_mask = with_ends((jax.random.randint(streams_of[4], (TRAIN_ALL,), 0, 4) < 3).astype(jnp.int32), jax.random.fold_in(streams_of[4], 1), 0, 1)
    norm_flag = draw_norm_flag(jax.random.fold_in(streams_of[24], 71), 0)
    val_images = centred(streams_of[6], (VAL_ALL, SIDE, SIDE, 3), 1.0, 6.0, ((0, 32),), jnp.float32)
    val_labels = with_ends(jax.random.randint(streams_of[7], (VAL_ALL,), 0, CLASSES), jax.random.fold_in(streams_of[7], 1), 0, CLASSES - 1).astype(jnp.int32)
    stem = centred(streams_of[8], (3, 3, 3, C), 27 ** -0.5, 1.25, (), jnp.float32)
    convs = centred(streams_of[9], (2, 3, 3, C, C), (9 * C) ** -0.5, 0.25, (), jnp.float32)
    norms = centred(streams_of[10], (3, 2, C), 0.5, 2.5, (), jnp.float32)
    head = centred(streams_of[11], (C + 1, CLASSES), C ** -0.5, 0.75, (), jnp.float32)
    m_stem = centred(streams_of[12], (GROUPS, 3, 3, 3, C), 0.00027, 0.00390625, ((0, 4),), jnp.float32)
    v_stem = jnp.clip(jnp.exp(math.log(2.4000000209412065e-08) - 1.3862944 * jax.random.uniform(streams_of[13], (GROUPS, 3, 3, 3, C), jnp.float32) ** steps_of(streams_of[13], (GROUPS, 3, 3, 3, C), ((0, 4),), -0.2, 0.2)), 6.000000052353016e-09, 2.4000000209412065e-08)
    m_convs = centred(streams_of[14], (GROUPS, 2, 3, 3, C, C), 0.00022, 0.0034179688, ((0, 4),), jnp.float32)
    v_convs = jnp.clip(jnp.exp(math.log(1.5999999547489097e-08) - 1.3862944 * jax.random.uniform(streams_of[15], (GROUPS, 2, 3, 3, C, C), jnp.float32) ** steps_of(streams_of[15], (GROUPS, 2, 3, 3, C, C), ((0, 4),), -0.2, 0.2)), 3.999999886872274e-09, 1.5999999547489097e-08)
    m_norms = centred(streams_of[16], (GROUPS, 3, 2, C), 0.0009, 0.013671875, ((0, 4),), jnp.float32)
    v_norms = jnp.clip(jnp.exp(math.log(2.5599999275982555e-07) - 1.3862944 * jax.random.uniform(streams_of[17], (GROUPS, 3, 2, C), jnp.float32) ** steps_of(streams_of[17], (GROUPS, 3, 2, C), ((0, 4),), -0.2, 0.2)), 6.399999818995639e-08, 2.5599999275982555e-07)
    m_head = centred(streams_of[18], (GROUPS, C + 1, CLASSES), 0.0055, 0.078125, ((0, 4),), jnp.float32)
    v_head = jnp.clip(jnp.exp(math.log(9.999999747378752e-06) - 1.3862944 * jax.random.uniform(streams_of[19], (GROUPS, C + 1, CLASSES), jnp.float32) ** steps_of(streams_of[19], (GROUPS, C + 1, CLASSES), ((0, 4),), -0.2, 0.2)), 2.499999936844688e-06, 9.999999747378752e-06)
    mom_stem = centred(streams_of[20], (3, 3, 3, C), 0.05, 0.75, (), jnp.float32)
    mom_convs = centred(streams_of[21], (2, 3, 3, C, C), 0.05, 0.75, (), jnp.float32)
    mom_norms = centred(streams_of[22], (3, 2, C), 0.05, 0.75, (), jnp.float32)
    mom_head = centred(streams_of[23], (C + 1, CLASSES), 0.05, 0.75, (), jnp.float32)
    return dict(train_images=train_images, train_labels=train_labels, flip_flags=flip_flags, class_ids=class_ids, clip_mask=clip_mask, norm_flag=norm_flag, val_images=val_images, val_labels=val_labels, stem=stem, convs=convs, norms=norms, head=head, m_stem=m_stem, v_stem=v_stem, m_convs=m_convs, v_convs=v_convs, m_norms=m_norms, v_norms=v_norms, m_head=m_head, v_head=v_head, mom_stem=mom_stem, mom_convs=mom_convs, mom_norms=mom_norms, mom_head=mom_head)


@jax.custom_vjp
def low(v):
    return lax.optimization_barrier(v.astype(jnp.bfloat16)).astype(jnp.float32)

@jax.custom_vjp
def low_back(v):
    return v

def low_keep(v):
    return (low(v), None)

def low_pass(kept, grad):
    return (grad,)

def back_keep(v):
    return (v, None)

def back_low(kept, grad):
    return (low(grad),)
low.defvjp(low_keep, low_pass)
low_back.defvjp(back_keep, back_low)
HIGH = lax.Precision.HIGHEST
BN_EPS = 1e-05
ALPHA = 0.1

def conv(x, w):
    return lax.conv_general_dilated(x, w, (1, 1), 'SAME', dimension_numbers=('NHWC', 'HWIO', 'NHWC'), precision=HIGH)

def batch_norm(a, norm_gain, bias):
    mean = lax.optimization_barrier(jnp.mean(a, axis=(0, 1, 2)))
    var = lax.optimization_barrier(jnp.mean((a - mean) * (a - mean), axis=(0, 1, 2)))
    return norm_gain * (a - mean) * lax.rsqrt(var + BN_EPS) + bias

def network(params, images):
    stem, convs, norms, head = params
    h0 = jax.nn.relu(batch_norm(conv(images, stem), norms[0, 0], norms[0, 1]))
    h1 = jax.nn.relu(batch_norm(conv(h0, convs[0]), norms[1, 0], norms[1, 1]))
    z = jax.nn.relu(batch_norm(conv(h1, convs[1]), norms[2, 0], norms[2, 1]) + h0)
    pooled = lax.optimization_barrier(jnp.mean(z, axis=(1, 2)))
    return jnp.dot(pooled, head[:-1], precision=HIGH) + head[-1]

def cross(logits, labels):
    onehot = (labels[:, None] == jnp.arange(CLASSES)[None, :]).astype(jnp.float32)
    return jax.nn.logsumexp(logits, axis=-1) - lax.optimization_barrier(jnp.sum(onehot * logits, axis=-1))

def group_step(images, labels, flips, ids, clip, flag, vimages, vlabels, params):
    noisy = jnp.where(flips == 1, ids, labels)
    onehot = (noisy[:, None] == jnp.arange(CLASSES)[None, :]).astype(jnp.float32)
    element_count = images.shape[0]
    counts = lax.optimization_barrier(jnp.sum(onehot, axis=0))
    class_weight = element_count / (CLASSES * (counts + 1.0))
    per = lax.optimization_barrier(jnp.sum(onehot * class_weight, axis=1))

    def train_terms(p):
        return per * cross(network(p, images), noisy)

    def val_loss(p):
        return jnp.mean(cross(network(p, vimages), vlabels))

    def virtual(eps):
        _, pull = jax.vjp(lambda p: jnp.sum(eps * train_terms(p)), params)
        grads = pull(jnp.float32(1.0))[0]
        return val_loss(jax.tree.map(lambda a, b: a - ALPHA * b, params, grads))
    _, pull_eps = jax.vjp(virtual, jnp.zeros((element_count,), jnp.float32))
    score = pull_eps(jnp.float32(1.0))[0]
    clipf = clip.astype(jnp.float32)
    raw = clipf * jnp.maximum(-score, 0.0)
    total = jnp.sum(raw)
    magnitude = jnp.sum(clipf * jnp.abs(score))
    weights = jnp.where(flag == 1, raw / (jnp.maximum(total, 0.25 * magnitude) + 1e-06), 1.0 / element_count)
    loss, pull = jax.vjp(lambda p: jnp.sum(weights * train_terms(p)), params)
    return (loss, pull(jnp.float32(1.0))[0])

def reference(train_images, train_labels, flip_flags, class_ids, clip_mask, norm_flag, val_images, val_labels, stem, convs, norms, head, m_stem, v_stem, m_convs, v_convs, m_norms, v_norms, m_head, v_head, mom_stem, mom_convs, mom_norms, mom_head):
    params = (stem, convs, norms, head)
    firsts_in = (m_stem, m_convs, m_norms, m_head)
    seconds_in = (v_stem, v_convs, v_norms, v_head)
    moms = (mom_stem, mom_convs, mom_norms, mom_head)
    tg = TRAIN_ALL // GROUPS
    vg = VAL_ALL // GROUPS
    losses, firsts, seconds = ([], [[], [], [], []], [[], [], [], []])
    delta_sum = [jnp.zeros_like(p) for p in params]
    for g in range(GROUPS):
        t0, v0 = (g * tg, g * vg)
        loss, grads = group_step(train_images[t0:t0 + tg], train_labels[t0:t0 + tg], flip_flags[t0:t0 + tg], class_ids[t0:t0 + tg], clip_mask[t0:t0 + tg], norm_flag[g], val_images[v0:v0 + vg], val_labels[v0:v0 + vg], params)
        losses.append(loss)
        for k in range(4):
            first = 0.9 * firsts_in[k][g] + 0.1 * grads[k]
            second = 0.999 * seconds_in[k][g] + 0.001 * grads[k] * grads[k]
            step = first / (1.0 - 0.9 ** STEP) / (jnp.sqrt(second / (1.0 - 0.999 ** STEP)) + 1e-08) + 0.01 * params[k]
            delta_sum[k] = delta_sum[k] + 0.05 * step
            firsts[k].append(first)
            seconds[k].append(second)
    news, outers = ([], [])
    for k in range(4):
        avg = delta_sum[k] / GROUPS
        outer = 0.9 * moms[k] + avg
        news.append(params[k] - 0.7 * (avg + 0.9 * outer))
        outers.append(outer)
    lows = [a.astype(jnp.bfloat16) for a in news]
    fs = [jnp.stack(a) for a in firsts]
    ss = [jnp.stack(a) for a in seconds]
    return (news[0], news[1], news[2], news[3], lows[0], lows[1], lows[2], lows[3], fs[0], fs[1], fs[2], fs[3], ss[0], ss[1], ss[2], ss[3], outers[0], outers[1], outers[2], outers[3], jnp.stack(losses))
```

```python
import functools

import jax
import jax.numpy as jnp
from jax import lax
from jax.experimental import pallas as pl
from jax.experimental.pallas import tpu as pltpu
from jax.sharding import PartitionSpec as P

STEP = 10
BN_EPS = 1e-05
ALPHA = 0.1
F32 = jnp.float32
BF16 = jnp.bfloat16
HIGH = lax.Precision.HIGHEST
VMEM_BYTES = 56 * 1024 * 1024


TERMS = {
    1: ((0, 0),),
    2: ((1, 0), (0, 1), (0, 0)),
    3: ((2, 0), (1, 1), (0, 2), (1, 0), (0, 1), (0, 0)),
}


def mxu(a, b):
    return lax.dot_general(a, b, (((1,), (0,)), ((), ())), preferred_element_type=F32)


def mxu_t(a, b):
    return lax.dot_general(a, b, (((0,), (0,)), ((), ())), preferred_element_type=F32)


def split(x, n):
    parts = []
    for k in range(n):
        p = x.astype(BF16)
        parts.append(p)
        if k + 1 < n:
            x = x - p.astype(F32)
    return parts


def dup(v):
    return v + pltpu.roll(v, v.shape[-1] // 2, v.ndim - 1)


def low_half(shape):
    return lax.broadcasted_iota(jnp.int32, shape, len(shape) - 1) < shape[-1] // 2


def edges(rows, side):
    y = lax.rem(lax.broadcasted_iota(jnp.int32, (rows, 128), 0), side)
    return y == 0, y == side - 1


def down(x, top):
    return jnp.where(top, 0.0, pltpu.roll(x, 1, 0))


def up(x, bottom):
    return jnp.where(bottom, 0.0, pltpu.roll(x, x.shape[0] - 1, 0))


def row_sum(x):
    return jnp.sum(x, axis=0, keepdims=True)


def zero_ends(wide, k):
    last, rows = wide.shape[1] - 1, wide.shape[2]
    wide[k, last, :, 128:192] = jnp.zeros((rows, 64), BF16)
    wide[k, 0, :, 192:256] = jnp.zeros((rows, 64), BF16)


def put(wide, xp, parts):
    for k, part in enumerate(parts):
        wide[k, xp, :, 0:128] = part
        if xp > 0:
            wide[k, xp - 1, :, 128:192] = part[:, 0:64]
        if xp + 1 < wide.shape[1]:
            wide[k, xp + 1, :, 192:256] = part[:, 64:128]


def conv_block(pairs, top, bottom):
    z = None
    for a, b in pairs:
        t = mxu(a, b)
        z = t if z is None else z + t
    return down(z[:, 0:128], top) + z[:, 128:256] + up(z[:, 256:384], bottom)


def pair_form(t0, t1, t2):
    lt = low_half(t0.shape)
    return jnp.concatenate(
        [
            jnp.where(lt, t1, t0),
            jnp.where(lt, t2, t1),
            jnp.where(lt, 0.0, t2),
            jnp.where(lt, t0, 0.0),
        ],
        axis=0,
    )


def fold_pair(acc, out, base=0):
    for dy in range(3):
        b = acc[:, 128 * dy : 128 * dy + 128]
        even, odd, nxt, prv = b[0:64], b[64:128], b[128:192], b[192:256]
        lt = low_half(even.shape)
        taps = (jnp.where(lt, prv, even), jnp.where(lt, even, odd), jnp.where(lt, odd, nxt))
        for dx in range(3):
            r = base + 64 * (3 * dy + dx)
            out[r : r + 64] = dup(taps[dx])


def tap_distance(side, xp):
    xin = lax.broadcasted_iota(jnp.int32, (side, 128), 0)
    parity = jnp.where(low_half((side, 128)), 0, 1)
    return xin - 2 * xp - parity + 1


def stem_band(stem, side, xp):
    d = tap_distance(side, xp)
    blocks = []
    for dy in range(3):
        for c in range(4):
            if c == 3:
                blocks.append(jnp.zeros((side, 128), F32))
                continue
            s = [stem[12 * dx + 4 * dy + c : 12 * dx + 4 * dy + c + 1] for dx in range(3)]
            blocks.append(
                jnp.where(d == 0, s[0], jnp.where(d == 1, s[1], jnp.where(d == 2, s[2], 0.0)))
            )
    return jnp.concatenate(blocks, axis=0)


def stem_rows(img, top, bottom):
    lane = lax.broadcasted_iota(jnp.int32, img.shape, 1)
    img = jnp.where(lane < 96, img, 0.0)
    return jnp.concatenate([down(img, top), img, up(img, bottom)], axis=1)


def fold_stem(accs, side):
    rows = []
    for dx in range(3):
        for k in range(12):
            rows.append(dup(row_sum(accs[dx][side * k : side * k + side])))
    return jnp.concatenate(rows + [jnp.zeros((4, 128), F32)], axis=0)


def stem_fold_step(accs, f, side, xp):
    d = tap_distance(side, xp)
    d = jnp.concatenate([d] * 12, axis=0)
    return [a + jnp.where(d == dx, f, 0.0) for dx, a in enumerate(accs)]


def label_onehot(img, images, classes):
    lab = img.reshape(images, img.shape[0] // images, 128)[:, 0, :]
    lane = lax.broadcasted_iota(jnp.int32, (images, 128), 1)
    lab = jnp.sum(jnp.where(lane == 96, lab, 0.0), axis=1, keepdims=True)
    return jnp.where((lane.astype(F32) == lab) & (lane < classes), 1.0, 0.0)


def combine(blocks, count):
    each = count / len(blocks)
    total = sum(b[0:1] for b in blocks)
    mean = total / count
    m2 = sum(b[1:2] + each * jnp.square(b[0:1] / each - mean) for b in blocks)
    return mean, lax.rsqrt(m2 / count + BN_EPS)


def stack_rows(rows, n=8):
    rows = list(rows)
    return jnp.concatenate(rows + [jnp.zeros((n - len(rows), 128), F32)], axis=0)


def centred_sums(a, s, count):
    mean = s / count
    m2 = jnp.zeros((1, 128), F32)
    for xp in range(a.shape[0]):
        d = a[xp] - mean
        m2 = m2 + row_sum(d * d)
    return dup(m2)


def k_weights(wd, wt, w1, w2, t1, t2):
    for k, (out, back) in enumerate(((w1, t1), (w2, t2))):
        for dy in range(3):
            sl = slice(128 * dy, 128 * dy + 128)
            for src, dst, n in ((wd, out, 3), (wt, back, 2)):
                blk = pair_form(*[src[k, 3 * dy + dx] for dx in range(3)])
                for i, p in enumerate(split(blk, n)):
                    dst[i, :, sl] = p


def k_pack(img, lab, out):
    for n in range(img.shape[0]):
        side = img.shape[2]
        out[side * n : side * n + side] = jnp.concatenate(
            [img[n, 0], img[n, 1], img[n, 2], jnp.broadcast_to(lab[n : n + 1], (side, 32))], axis=1
        )


def k_stem(n, side, classes, img, stem, a0, st):
    rows = img.shape[0]
    pairs = a0.shape[0]
    top, bottom = edges(rows, side)
    lhs = split(stem_rows(img[...], top, bottom), n)
    s = jnp.zeros((1, 128), F32)
    st_stem = stem[...]
    for xp in range(0, pairs, 2):
        band = jnp.concatenate(
            [stem_band(st_stem, side, xp), stem_band(st_stem, side, xp + 1)], axis=1
        )
        rhs = split(band, n)
        z = None
        for i, j in TERMS[n]:
            t = mxu(lhs[i], rhs[j])
            z = t if z is None else z + t
        a0[xp] = z[:, 0:128]
        a0[xp + 1] = z[:, 128:256]
        s = s + row_sum(z[:, 0:128]) + row_sum(z[:, 128:256])
    s = dup(s)
    m2 = centred_sums(a0, s, rows * pairs * 2)
    counts = row_sum(label_onehot(img[...], rows // side, classes))
    st[...] = stack_rows([s, m2, counts])


def k_conv(n, side, nb, layer, count, *refs):
    a_in, nv = refs[0], refs[1]
    blocks, w = refs[2 : 2 + nb], refs[2 + nb]
    a_out, st, vec, wide = refs[3 + nb :]
    pairs, rows = a_in.shape[0], a_in.shape[1]
    top, bottom = edges(rows, side)
    bl = [b[...] for b in blocks]
    mean, r = combine(bl, count)
    gain, bias = nv[2 * layer : 2 * layer + 1], nv[2 * layer + 1 : 2 * layer + 2]
    counts = sum(b[2:3] for b in bl)
    vec[...] = stack_rows([mean, r, gain, bias, counts])
    for k in range(n):
        zero_ends(wide, k)

    def prep(xp):
        h = jnp.maximum(gain * ((a_in[xp] - mean) * r) + bias, 0.0)
        put(wide, xp, split(h, n))

    prep(0)
    s = jnp.zeros((1, 128), F32)
    for xp in range(pairs):
        if xp + 1 < pairs:
            prep(xp + 1)
        out = conv_block([(wide[i, xp], w[j]) for i, j in TERMS[n]], top, bottom)
        a_out[xp] = out
        s = s + row_sum(out)
    s = dup(s)
    m2 = centred_sums(a_out, s, rows * pairs * 2)
    st[...] = stack_rows([s, m2])


def bn(a, vec):
    xh = (a - vec[0:1]) * vec[1:2]
    return xh, vec[2:3] * xh + vec[3:4]


def k_head(val, side, nb, count, classes, group_count, *refs):
    a2, a0, vec0r, nv, img, hp, hpt, hb = refs[:8]
    blocks = refs[8 : 8 + nb]
    clip = refs[8 + nb]
    mz, vec2r, info, extra = refs[9 + nb :]
    pairs, rows = a2.shape[0], a2.shape[1]
    images = rows // side
    mean, r = combine([b[...] for b in blocks], count)
    vec2 = stack_rows([mean, r, nv[4:5], nv[5:6]])
    vec2r[...] = vec2
    vec0 = vec0r[...]
    zs = jnp.zeros((images, 128), F32)
    ms = jnp.zeros((images, 128), F32)
    xs = jnp.zeros((images, 128), F32)
    for xp in range(pairs):
        xh2, y2 = bn(a2[xp], vec2)
        z = y2 + jnp.maximum(bn(a0[xp], vec0)[1], 0.0)
        on = z > 0
        m = jnp.where(on, 1.0, 0.0)
        mz[xp] = m.astype(BF16)
        zs = zs + jnp.sum(jnp.where(on, z, 0.0).reshape(images, side, 128), axis=1)
        ms = ms + jnp.sum(m.reshape(images, side, 128), axis=1)
        xs = xs + jnp.sum(jnp.where(on, xh2, 0.0).reshape(images, side, 128), axis=1)
    area = side * pairs * 2
    lt = low_half((images, 128))
    pooled, ms, xs = dup(zs) / area, dup(ms), dup(xs)
    logits = lax.dot(pooled, hp[...], precision=HIGH) + hb[0:1]
    lane = lax.broadcasted_iota(jnp.int32, (images, 128), 1)
    ok = lane < classes
    top = jnp.max(jnp.where(ok, logits, -3e38), axis=1, keepdims=True)
    e = jnp.where(ok, jnp.exp(jnp.where(ok, logits - top, 0.0)), 0.0)
    tot = jnp.sum(e, axis=1, keepdims=True)
    onehot = label_onehot(img[...], images, classes)
    pm = e / tot - onehot
    ce = jnp.log(tot) + top - jnp.sum(onehot * logits, axis=1, keepdims=True)
    g = lax.dot(pm, hpt[...], precision=HIGH)
    if val:
        n_val = group_count
        gp = g / (n_val * area)
        info[...] = gp
        head = lax.dot_general(
            pooled, pm / n_val, (((0,), (0,)), ((), ())), precision=HIGH
        )
        extra[0:64] = head[0:64]
        extra[64:72] = stack_rows([row_sum(pm) / n_val])
        extra[72:80] = stack_rows([row_sum(gp * ms), row_sum(gp * xs)])
    else:
        cw = group_count / (classes * (vec0[4:5] + 1.0))
        per = jnp.sum(onehot * cw, axis=1, keepdims=True)
        uw = jnp.where(lt, g * ms, g * xs)
        pc = jnp.where(lane == 0, per, jnp.where(lane == 1, clip[...], 0.0))
        extra[0:images] = uw
        extra[images : 2 * images] = pc
        for k, v in enumerate((g, ms, xs, pooled, pm, jnp.broadcast_to(ce, (images, 128)))):
            info[k] = v


def k_static(side, img, a0, vec0r, out):
    pairs, rows = a0.shape[0], a0.shape[1]
    top, bottom = edges(rows, side)
    vec0 = vec0r[...]
    lhs = split(stem_rows(img[...], top, bottom), 2)
    px, ps = stem_static(side, pairs, lhs, lambda xp: (a0[xp] - vec0[0:1]) * vec0[1:2], 2)
    out[0:40] = px
    out[40:80] = ps


def stem_grad(side, pairs, lhs, rhs_of, n):
    accs = [jnp.zeros((lhs[0].shape[1], 128), F32)] * 3
    for xp in range(0, pairs, 2):
        rhs = split(jnp.concatenate([rhs_of(xp), rhs_of(xp + 1)], axis=1), n)
        f = None
        for i, j in TERMS[n]:
            t = mxu_t(lhs[i], rhs[j])
            f = t if f is None else f + t
        accs = stem_fold_step(accs, f[:, 0:128], side, xp)
        accs = stem_fold_step(accs, f[:, 128:256], side, xp + 1)
    return fold_stem(accs, side)


def stem_static(side, pairs, lhs, rhs_of, n):
    px = stem_grad(side, pairs, lhs, rhs_of, n)
    sums = 0.0
    for part in lhs:
        sums = sums + jnp.sum(part.astype(F32), axis=0, keepdims=True)
    col = jnp.transpose(jnp.broadcast_to(sums, (8, sums.shape[1])))[:, 0:1]
    xin = lax.rem(lax.broadcasted_iota(jnp.int32, col.shape, 0), side)
    rows = []
    for dx in range(3):
        keep = xin <= side - 2 if dx == 0 else (xin >= 1 if dx == 2 else xin >= 0)
        c = jnp.where(keep, col, 0.0)
        for k in range(12):
            rows.append(jnp.broadcast_to(row_sum(c[side * k : side * k + side]), (1, 128)))
    ps = jnp.concatenate(rows + [jnp.zeros((4, 128), F32)], axis=0)
    return px, ps


def back_conv2(n, side, gp, vec2, s1, s2, count, a2, mz, a1, vec1, wt, wide, dy1, keep, extra):
    pairs, rows = a2.shape[0], a2.shape[1]
    images = rows // side
    top, bottom = edges(rows, side)
    for k in range(n):
        zero_ends(wide, k)
    k2 = vec2[2:3] * vec2[1:2]
    c0, c1 = k2 * s1 / count, k2 * s2 / count
    gk = gp * k2
    gk = jnp.broadcast_to(gk[:, None, :], (images, side, 128)).reshape(rows, 128)

    def prep(xp):
        xh2 = (a2[xp] - vec2[0:1]) * vec2[1:2]
        back = mz[xp].astype(F32) * gk - c0 - xh2 * c1
        parts = split(back, n)
        put(wide, xp, parts)
        extra(xp, back, parts)

    prep(0)
    q1 = jnp.zeros((1, 128), F32)
    q2 = jnp.zeros((1, 128), F32)
    for xp in range(pairs):
        if xp + 1 < pairs:
            prep(xp + 1)
        dh = conv_block([(wide[i, xp], wt[j]) for i, j in TERMS[n]], top, bottom)
        xh1, y1 = bn(a1[xp], vec1)
        dy = jnp.where(y1 > 0, dh, 0.0)
        dy1[xp] = dy
        q1 = q1 + row_sum(dy)
        q2 = q2 + row_sum(dy * xh1)
    return dup(q1), dup(q2)


def shifted(back, top, bottom):
    return jnp.concatenate([up(back, bottom), back, down(back, top)], axis=1)


def k_val_back2(side, nb, count, *refs):
    a2, mz, a1, vec2r, vec1r, gp, wt, wide1 = refs[:8]
    blocks = refs[8 : 8 + nb]
    dy1, st, g2 = refs[8 + nb : 11 + nb]
    wide, acc = refs[11 + nb :]
    rows = a2.shape[1]
    top, bottom = edges(rows, side)
    s1 = sum(b[72:73] for b in blocks)
    s2 = sum(b[73:74] for b in blocks)
    acc[...] = jnp.zeros(acc.shape, F32)

    def extra(xp, back, parts):
        acc[...] += mxu_t(wide1[0, xp], shifted(back, top, bottom).astype(BF16))

    q1, q2 = back_conv2(
        1, side, gp[...], vec2r[...], s1, s2, count, a2, mz, a1, vec1r[...], wt, wide, dy1, None, extra
    )
    fold_pair(acc[...], g2)
    st[...] = stack_rows([q1, q2, s1, s2])


def back_conv1(n, side, gp, vec1, vec0, s1, s2, count, dy1, a1, a0, mz, wt, wide, dy0, extra):
    pairs, rows = a1.shape[0], a1.shape[1]
    images = rows // side
    top, bottom = edges(rows, side)
    for k in range(n):
        zero_ends(wide, k)
    k1 = vec1[2:3] * vec1[1:2]
    c0, c1 = k1 * s1 / count, k1 * s2 / count
    gpr = jnp.broadcast_to(gp[:, None, :], (images, side, 128)).reshape(rows, 128)

    def prep(xp):
        xh1 = (a1[xp] - vec1[0:1]) * vec1[1:2]
        back = dy1[xp] * k1 - c0 - xh1 * c1
        parts = split(back, n)
        put(wide, xp, parts)
        extra(xp, back, parts)

    prep(0)
    q1 = jnp.zeros((1, 128), F32)
    q2 = jnp.zeros((1, 128), F32)
    for xp in range(pairs):
        if xp + 1 < pairs:
            prep(xp + 1)
        dh = conv_block([(wide[i, xp], wt[j]) for i, j in TERMS[n]], top, bottom)
        xh0, y0 = bn(a0[xp], vec0)
        dy = jnp.where(y0 > 0, dh + mz[xp].astype(F32) * gpr, 0.0)
        dy0[xp] = dy
        q1 = q1 + row_sum(dy)
        q2 = q2 + row_sum(dy * xh0)
    return dup(q1), dup(q2)


def k_val_back1(side, nb, count, *refs):
    dy1, a1, a0, mz, vec1r, vec0r, gp, wt, wide0, img = refs[:10]
    blocks = refs[10 : 10 + nb]
    g1, small = refs[10 + nb : 12 + nb]
    wide, acc, dy0 = refs[12 + nb :]
    pairs, rows = a1.shape[0], a1.shape[1]
    top, bottom = edges(rows, side)
    s1 = sum(b[0:1] for b in blocks)
    s2 = sum(b[1:2] for b in blocks)
    acc[...] = jnp.zeros(acc.shape, F32)
    vec0 = vec0r[...]

    def extra(xp, back, parts):
        acc[...] += mxu_t(wide0[0, xp], shifted(back, top, bottom).astype(BF16))

    q1, q2 = back_conv1(
        1, side, gp[...], vec1r[...], vec0, s1, s2, count, dy1, a1, a0, mz, wt, wide, dy0, extra
    )
    fold_pair(acc[...], g1)
    lhs = split(stem_rows(img[...], top, bottom), 1)
    small[0:40] = stem_grad(side, pairs, lhs, lambda xp: dy0[xp], 1)
    px, ps = stem_static(side, pairs, lhs, lambda xp: (a0[xp] - vec0[0:1]) * vec0[1:2], 1)
    small[40:80] = px
    small[80:120] = ps
    small[120:128] = stack_rows([q1, q2])


def k_tan1(side, nb, nv_blocks, count, count_val, *refs):
    img, a0, a1, vec0r, vec1r, w1, wide0, vvec0r = refs[:8]
    refs = refs[8:]
    stat = refs[:nb]
    refs = refs[nb:]
    smalls, g1s, sts = refs[:nv_blocks], refs[nv_blocks : 2 * nv_blocks], refs[2 * nv_blocks : 3 * nv_blocks]
    t1, th0, st, wide, v1 = refs[3 * nv_blocks :]
    pairs, rows = a1.shape[0], a1.shape[1]
    top, bottom = edges(rows, side)
    vec0, vec1, vv0 = vec0r[...], vec1r[...], vvec0r[...]
    small = sum(b[...] for b in smalls)
    q1, q2 = small[120:121], small[121:122]
    v0 = (
        vv0[2:3]
        * vv0[1:2]
        * (small[0:40] - small[80:120] * (q1 / count_val) - small[40:80] * (q2 / count_val))
    )
    static = sum(b[...] for b in stat)
    u1 = row_sum(v0 * static[40:80])
    u2 = row_sum(v0 * static[0:40])
    k0 = vec0[2:3] * vec0[1:2]
    e0 = q1 - k0 * u1 / count
    e1 = q2 - k0 * u2 / count
    for dy in range(3):
        taps = []
        for dx in range(3):
            r = 64 * (3 * dy + dx)
            taps.append(sum(g[r : r + 64] for g in g1s))
        v1[:, 128 * dy : 128 * dy + 128] = pair_form(*taps).astype(BF16)
    zero_ends(wide, 0)
    lhs = stem_rows(img[...], top, bottom).astype(BF16)
    tang = {}

    def prep(xp):
        if xp % 2 == 0:
            band = jnp.concatenate(
                [stem_band(v0, side, xp), stem_band(v0, side, xp + 1)], axis=1
            ).astype(BF16)
            z = mxu(lhs, band)
            tang[xp], tang[xp + 1] = z[:, 0:128], z[:, 128:256]
        xh0, y0 = bn(a0[xp], vec0)
        th = jnp.where(y0 > 0, k0 * tang.pop(xp) + e1 * xh0 + e0, 0.0).astype(BF16)
        th0[xp] = th
        put(wide, xp, [th])

    prep(0)
    p1 = jnp.zeros((1, 128), F32)
    p2 = jnp.zeros((1, 128), F32)
    for xp in range(pairs):
        if xp + 1 < pairs:
            prep(xp + 1)
        t = conv_block([(wide[0, xp], w1[0]), (wide0[0, xp], v1[...])], top, bottom)
        t1[xp] = t
        xh1 = (a1[xp] - vec1[0:1]) * vec1[1:2]
        p1 = p1 + row_sum(t)
        p2 = p2 + row_sum(t * xh1)
    vs = [sum(b[k : k + 1] for b in sts) for k in range(2)]
    st[...] = stack_rows([dup(p1), dup(p2), vs[0], vs[1], sts[0][2:3], sts[0][3:4]])


def k_tan2(side, nb, nv_blocks, count, *refs):
    t1, th0, a1, a2, mz, vec1r, vec2r, w2, wide1, info, own = refs[:11]
    refs = refs[11:]
    blocks = refs[:nb]
    refs = refs[nb:]
    g2s, heads = refs[:nv_blocks], refs[nv_blocks : 2 * nv_blocks]
    st, wide, v2 = refs[2 * nv_blocks :]
    pairs, rows = a1.shape[0], a1.shape[1]
    images = rows // side
    top, bottom = edges(rows, side)
    vec1, vec2 = vec1r[...], vec2r[...]
    u1 = sum(b[0:1] for b in blocks)
    u2 = sum(b[1:2] for b in blocks)
    k1 = vec1[2:3] * vec1[1:2]
    e0 = own[2:3] - k1 * u1 / count
    e1 = own[3:4] - k1 * u2 / count
    for dy in range(3):
        taps = []
        for dx in range(3):
            r = 64 * (3 * dy + dx)
            taps.append(sum(g[r : r + 64] for g in g2s))
        v2[:, 128 * dy : 128 * dy + 128] = pair_form(*taps).astype(BF16)
    zero_ends(wide, 0)

    def prep(xp):
        xh1, y1 = bn(a1[xp], vec1)
        th = jnp.where(y1 > 0, k1 * t1[xp] + e1 * xh1 + e0, 0.0).astype(BF16)
        put(wide, xp, [th])

    prep(0)
    p1 = jnp.zeros((1, 128), F32)
    p2 = jnp.zeros((1, 128), F32)
    asum = jnp.zeros((images, 128), F32)
    k2 = vec2[2:3] * vec2[1:2]
    for xp in range(pairs):
        if xp + 1 < pairs:
            prep(xp + 1)
        t = conv_block([(wide[0, xp], w2[0]), (wide1[0, xp], v2[...])], top, bottom)
        xh2 = (a2[xp] - vec2[0:1]) * vec2[1:2]
        p1 = p1 + row_sum(t)
        p2 = p2 + row_sum(t * xh2)
        m = mz[xp].astype(F32)
        asum = asum + jnp.sum(
            (m * (k2 * t + th0[xp].astype(F32))).reshape(images, side, 128), axis=1
        )
    asum = dup(asum)
    area = side * pairs * 2
    g, ms, xs, pooled, pm = (info[k] for k in range(5))
    inner = g * (asum + own[5:6] * xs + own[4:5] * ms)
    base = jnp.sum(jnp.where(low_half(inner.shape), inner, 0.0), axis=1, keepdims=True) / area
    vhead = sum(h[0:72] for h in heads)
    vh = jnp.concatenate([vhead[0:64], jnp.zeros((64, 128), F32)], axis=0)
    lin = lax.dot(pooled, vh, precision=HIGH) + vhead[64:65]
    base = base + jnp.sum(pm * lin, axis=1, keepdims=True)
    st[0:images] = jnp.broadcast_to(base, (images, 128))
    p1, p2 = dup(p1), dup(p2)
    st[images : images + 8] = stack_rows([jnp.where(low_half(p1.shape), p1, p2)])


def k_train_back2(side, nb, count, group_count, n, *refs):
    flag, a2, mz, a1, vec2r, vec1r, wt, info = refs[:8]
    refs = refs[8:]
    stat, dyn = refs[:nb], refs[nb : 2 * nb]
    dy1, st, back2, wgp, wide = refs[2 * nb :]
    pairs, rows = a2.shape[0], a2.shape[1]
    images = rows // side
    area = side * pairs * 2
    vec2 = vec2r[...]
    k2 = vec2[2:3] * vec2[1:2]
    each = stat[0].shape[0]
    tsum = 0.0
    for b in range(nb):
        for j in range(each):
            tsum = tsum + dyn[b][j, images : images + 1]
    tt = tsum * k2 / (count * area)
    raws, pers = [], []
    total = jnp.zeros((1, 1), F32)
    mag = jnp.zeros((1, 1), F32)
    for b in range(nb):
        for j in range(each):
            uw = stat[b][j, 0:images]
            pc = stat[b][j, images : 2 * images]
            per, clip = pc[:, 0:1], pc[:, 1:2]
            tan = dyn[b][j, 0:images, 0:1] - jnp.sum(uw * tt, axis=1, keepdims=True)
            score = -ALPHA * per * tan
            raw = clip * jnp.maximum(-score, 0.0)
            total = total + row_sum(raw)
            mag = mag + row_sum(clip * jnp.abs(score))
            raws.append(raw)
            pers.append(per)
    on = flag[0] == 1
    denom = jnp.maximum(total, 0.25 * mag) + 1e-06
    ssum = jnp.zeros((1, 128), F32)
    k = 0
    own = None
    for b in range(nb):
        for j in range(each):
            w = jnp.where(on, raws[k] / denom, 1.0 / group_count) * pers[k]
            own = w if own is None else own
            ssum = ssum + row_sum(w * stat[b][j, 0:images])
            k += 1
    ssum = ssum / area
    lt = low_half(ssum.shape)
    s1, s2 = dup(jnp.where(lt, ssum, 0.0)), dup(jnp.where(lt, 0.0, ssum))
    g, pooled, pm, ce = info[0], info[3], info[4], info[5]
    gp = own * g / area
    wgp[0:images] = gp
    head = lax.dot_general(pooled, own * pm, (((0,), (0,)), ((), ())), precision=HIGH)
    wgp[images : images + 64] = head[0:64]
    wgp[images + 64 : images + 72] = stack_rows([row_sum(own * pm), row_sum(own * ce), s1, s2])

    def extra(xp, back, parts):
        for i, p in enumerate(parts):
            back2[i, xp] = p

    q1, q2 = back_conv2(
        n, side, gp, vec2, s1, s2, count, a2, mz, a1, vec1r[...], wt, wide, dy1, None, extra
    )
    st[...] = stack_rows([q1, q2])


def k_train_back1(side, nb, count, n, *refs):
    dy1, a1, a0, mz, vec1r, vec0r, wt, img, wgp = refs[:9]
    blocks = refs[9 : 9 + nb]
    small, back1, wide, dy0 = refs[9 + nb :]
    pairs, rows = a1.shape[0], a1.shape[1]
    images = rows // side
    top, bottom = edges(rows, side)
    s1 = sum(b[0:1] for b in blocks)
    s2 = sum(b[1:2] for b in blocks)

    def extra(xp, back, parts):
        for i, p in enumerate(parts):
            back1[i, xp] = p

    q1, q2 = back_conv1(
        n, side, wgp[0:images], vec1r[...], vec0r[...], s1, s2, count, dy1, a1, a0, mz, wt, wide, dy0, extra
    )
    lhs = split(stem_rows(img[...], top, bottom), n)
    small[0:40] = stem_grad(side, pairs, lhs, lambda xp: dy0[xp], n)
    small[40:48] = stack_rows([q1, q2, s1, s2])


def k_dw(side, n, wide, back, g, acc):
    pairs, rows = back.shape[1], back.shape[2]
    top, bottom = edges(rows, side)
    acc[...] = jnp.zeros(acc.shape, F32)
    for xp in range(pairs):
        rhs = [shifted(back[i, xp].astype(F32), top, bottom).astype(BF16) for i in range(n)]
        t = None
        for i, j in TERMS[n]:
            d = mxu_t(wide[i, xp], rhs[j])
            t = d if t is None else t + d
        acc[...] += t
    fold_pair(acc[...], g)


VM = pl.BlockSpec(memory_space=pltpu.VMEM)
SM = pl.BlockSpec(memory_space=pltpu.SMEM)


def call(kernel, outs, args, scratch=(), smem=(), flops=0):
    specs = [SM if i in smem else VM for i in range(len(args))]
    return pl.pallas_call(
        kernel,
        out_shape=[jax.ShapeDtypeStruct(s, d) for s, d in outs],
        in_specs=specs,
        out_specs=[VM] * len(outs),
        scratch_shapes=[pltpu.VMEM(s, d) for s, d in scratch],
        compiler_params=pltpu.CompilerParams(vmem_limit_bytes=VMEM_BYTES),
        cost_estimate=pl.CostEstimate(flops=flops, bytes_accessed=1 << 20, transcendentals=0),
    )(*args)


def swap(x, k, n):
    return lax.ppermute(x, "dp", [(i, i ^ k) for i in range(n)])


def add(a, b, step):
    return a + b


def chan(count, a, b, step):
    d = a[0:1] - b[0:1]
    cross = d * d / (2.0 * count * step)
    return a + b + jnp.pad(cross, ((1, a.shape[0] - 2), (0, 0)))


def near(x, team, merge):
    n = lax.axis_size("dp")
    k = 1
    while k < team // 2:
        x = merge(x, swap(x, k, n), k)
        k *= 2
    return [x, swap(x, k, n)] if team > 1 else [x]


def far(x, merge):
    n = lax.axis_size("dp")
    k = 1
    while k < n // 4:
        x = merge(x, swap(x, k, n), k)
        k *= 2
    return [x] + [swap(x, j * k, n) for j in range(1, n // k)]


def far_list(x):
    n = lax.axis_size("dp")
    x = x[None]
    k = 1
    while k < n // 4:
        x = jnp.concatenate([x, swap(x, k, n)], axis=0)
        k *= 2
    return [x] + [swap(x, j * k, n) for j in range(1, n // k)]


def twice(w):
    return jnp.concatenate([w, w], axis=-1)


def body(
    train_images,
    train_labels,
    flip_flags,
    class_ids,
    clip_mask,
    norm_flag,
    val_images,
    val_labels,
    stem,
    convs,
    norms,
    head,
    m_stem,
    v_stem,
    m_convs,
    v_convs,
    m_norms,
    v_norms,
    m_head,
    v_head,
    mom_stem,
    mom_convs,
    mom_norms,
    mom_head,
):
    dp = lax.axis_size("dp")
    classes = head.shape[1]
    side, pairs = train_images.shape[1], train_images.shape[2] // 2
    images, val_each = train_images.shape[0], val_images.shape[0]
    group_train, group_val = dp * images, dp * val_each
    team = max(2, group_val // 16)
    rows, vrows = images * side, side * group_val // team
    vimages = group_val // team
    count, count_val = group_train * side * pairs * 2, group_val * side * pairs * 2
    nt, nval = 3, 1

    noisy = jnp.where(flip_flags == 1, class_ids, train_labels)

    def pack(img, lab):
        x = jnp.transpose(img, (0, 3, 1, 2))
        return call(
            k_pack, [((img.shape[0] * side, 128), F32)], [x, lab.astype(F32)[:, None]]
        )[0]

    vimg = pack(val_images, val_labels)
    vimg = jnp.concatenate(
        [vimg] + [swap(vimg, j * team, dp) for j in range(1, dp // team)], axis=0
    )
    img = pack(train_images, noisy)
    s36 = jnp.transpose(stem, (1, 0, 2, 3))
    s36 = jnp.pad(s36, ((0, 0), (0, 0), (0, 1), (0, 0))).reshape(36, 64)
    s40 = twice(jnp.pad(s36, ((0, 4), (0, 0))))
    nv = twice(jnp.pad(norms.reshape(6, 64), ((0, 2), (0, 0))))
    wd = twice(convs.reshape(2, 9, 64, 64))
    wt = twice(jnp.transpose(convs[:, ::-1, ::-1], (0, 1, 2, 4, 3)).reshape(2, 9, 64, 64))
    hp = jnp.pad(head[:-1], ((0, 64), (0, 128 - classes)))
    hpt = jnp.pad(twice(head[:-1].T), ((0, 128 - classes), (0, 0)))
    hb = jnp.pad(head[-1:], ((0, 7), (0, 128 - classes)))
    clip = jnp.broadcast_to(clip_mask.astype(F32)[:, None], (images, 128))

    act = (pairs, rows, 128)
    vact = (pairs, vrows, 128)
    st = ((8, 128), F32)

    def wide(n, r):
        return ((n, pairs, r, 256), BF16)

    a0, s0 = call(
        functools.partial(k_stem, nt, side, classes), [(act, F32), st], [img, s40]
    )
    b0 = far(s0, functools.partial(chan, rows * pairs * 2))
    w1, w2, t1w, t2w = call(
        k_weights,
        [((3, 256, 384), BF16), ((3, 256, 384), BF16), ((2, 256, 384), BF16), ((2, 256, 384), BF16)],
        [wd, wt],
    )
    va0, vs0 = call(
        functools.partial(k_stem, nval, side, classes), [(vact, F32), st], [vimg, s40]
    )
    vchan = functools.partial(chan, vrows * pairs * 2)
    vb0 = near(vs0, team, vchan)

    def conv(n, layer, r, total, a, blocks, w):
        return call(
            functools.partial(k_conv, n, side, len(blocks), layer, total),
            [((pairs, r, 128), F32), st, st, wide(n, r)],
            [a, nv] + blocks + [w],
        )

    a1, s1, vec0, wide0 = conv(nt, 0, rows, count, a0, b0, w1)
    b1 = far(s1, functools.partial(chan, rows * pairs * 2))
    va1, vs1, vvec0, vwide0 = conv(nval, 0, vrows, count_val, va0, vb0, w1)
    vb1 = near(vs1, team, vchan)
    va2, vs2, vvec1, vwide1 = conv(nval, 1, vrows, count_val, va1, vb1, w2)
    vb2 = near(vs2, team, vchan)
    a2, s2, vec1, wide1 = conv(nt, 1, rows, count, a1, b1, w2)
    b2 = far(s2, functools.partial(chan, rows * pairs * 2))

    vmz, vvec2, vgp, vextra = call(
        functools.partial(k_head, True, side, len(vb2), count_val, classes, group_val),
        [(vact, BF16), st, ((vimages, 128), F32), ((80, 128), F32)],
        [va2, va0, vvec0, nv, vimg, hp, hpt, hb] + vb2 + [clip],
    )
    vextras = near(vextra, team, add)
    static = far(
        call(functools.partial(k_static, side), [((80, 128), F32)], [img, a0, vec0])[0], add
    )
    mz, vec2, info, gather = call(
        functools.partial(k_head, False, side, len(b2), count, classes, group_train),
        [(act, BF16), st, ((6, images, 128), F32), ((2 * images, 128), F32)],
        [a2, a0, vec0, nv, img, hp, hpt, hb] + b2 + [clip],
    )
    stat = far_list(gather)

    vdy1, vst1, g2 = call(
        functools.partial(k_val_back2, side, len(vextras), count_val),
        [(vact, F32), st, ((576, 128), F32)],
        [va2, vmz, va1, vvec2, vvec1, vgp, t2w, vwide1] + vextras,
        [wide(1, vrows), ((256, 384), F32)],
    )
    vst1s = near(vst1, team, add)
    g2s = near(g2, team, add)
    g1, small = call(
        functools.partial(k_val_back1, side, len(vst1s), count_val),
        [((576, 128), F32), ((128, 128), F32)],
        [vdy1, va1, va0, vmz, vvec1, vvec0, vgp, t1w, vwide0, vimg] + vst1s,
        [wide(1, vrows), ((256, 384), F32), (vact, F32)],
    )
    smalls = near(small, team, add)
    g1s = near(g1, team, add)

    tan1, th0, ts1 = call(
        functools.partial(k_tan1, side, len(static), len(g1s), count, count_val),
        [(act, F32), (act, BF16), st],
        [img, a0, a1, vec0, vec1, w1, wide0, vvec0] + static + smalls + g1s + vst1s,
        [wide(1, rows), ((256, 384), BF16)],
    )
    tb1 = far(ts1, add)
    (ts2,) = call(
        functools.partial(k_tan2, side, len(tb1), len(g2s), count),
        [((images + 8, 128), F32)],
        [tan1, th0, a1, a2, mz, vec1, vec2, w2, wide1, info, ts1] + tb1 + g2s + vextras,
        [wide(1, rows), ((256, 384), BF16)],
    )
    dyn = far_list(ts2)

    nb_ = 2
    dy1, bs1, back2, wgp = call(
        functools.partial(k_train_back2, side, len(dyn), count, group_train, nb_),
        [(act, F32), st, ((nb_,) + act, BF16), ((images + 72, 128), F32)],
        [norm_flag, a2, mz, a1, vec2, vec1, t2w, info] + stat + dyn,
        [wide(nb_, rows)],
        smem=(0,),
    )
    bb1 = far(bs1, add)
    (d2,) = call(
        functools.partial(k_dw, side, nb_), [((576, 128), F32)], [wide1, back2], [((256, 384), F32)]
    )
    tsmall, back1 = call(
        functools.partial(k_train_back1, side, len(bb1), count, nb_),
        [((48, 128), F32), ((nb_,) + act, BF16)],
        [dy1, a1, a0, mz, vec1, vec0, t1w, img, wgp] + bb1,
        [wide(nb_, rows), (act, F32)],
    )
    (d1,) = call(
        functools.partial(k_dw, side, nb_), [((576, 128), F32)], [wide0, back1], [((256, 384), F32)]
    )

    grad_convs = jnp.stack([d1[:, :64], d2[:, :64]])
    tail = wgp[images:]
    summed_convs, ssmall, shead = lax.psum(
        (grad_convs, tsmall[:, :64], tail[0:66, :classes]), "dp"
    )
    stat_sum = sum(static)
    q1, q2 = ssmall[40:41], ssmall[41:42]
    gain0 = vec0[2:3, :64] * vec0[1:2, :64]
    gs = gain0 * (
        ssmall[0:36] - stat_sum[40:76, :64] * (q1 / count) - stat_sum[0:36, :64] * (q2 / count)
    )
    gs = jnp.transpose(gs.reshape(3, 3, 4, 64)[:, :, :3], (1, 0, 2, 3))
    gn = jnp.stack(
        [
            jnp.concatenate([q2, q1]),
            jnp.stack([tsmall[43, :64], tsmall[42, :64]]),
            jnp.stack([tail[67, :64], tail[66, :64]]),
        ]
    )
    grads = (gs, summed_convs.reshape(convs.shape), gn, shead[0:65])
    loss = shead[65, 0]
    params = (stem, convs, norms, head)
    firsts_in = (m_stem[0], m_convs[0], m_norms[0], m_head[0])
    seconds_in = (v_stem[0], v_convs[0], v_norms[0], v_head[0])
    firsts, seconds, deltas = ([], [], [])
    for p, gradient, m, v in zip(params, grads, firsts_in, seconds_in):
        first = 0.9 * m + 0.1 * gradient
        second = 0.999 * v + 0.001 * gradient * gradient
        step = (
            first / (1.0 - 0.9**STEP) / (jnp.sqrt(second / (1.0 - 0.999**STEP)) + 1e-08) + 0.01 * p
        )
        firsts.append(first[None])
        seconds.append(second[None])
        deltas.append(0.05 * step)
    groups = lax.axis_size("group")
    summed = lax.psum(tuple(deltas), "group")
    news, outers = ([], [])
    for p, total, m in zip(params, summed, (mom_stem, mom_convs, mom_norms, mom_head)):
        average = total / groups
        outer = 0.9 * m + average
        news.append(p - 0.7 * (average + 0.9 * outer))
        outers.append(outer)
    lows = [a.astype(jnp.bfloat16) for a in news]
    return (*news, *lows, *firsts, *seconds, *outers, loss[None])


def solution(mesh):
    split4 = P(("group", "dp"), None, None, None)
    split1 = P(("group", "dp"))
    group = P("group")
    whole = P()
    return jax.shard_map(
        body,
        mesh=mesh,
        in_specs=(split4, split1, split1, split1, split1, group, split4, split1)
        + (whole,) * 4
        + (group,) * 8
        + (whole,) * 4,
        out_specs=(whole,) * 8 + (group,) * 8 + (whole,) * 4 + (group,),
        check_vma=False,
    )
```

```python
import functools

import jax
import jax.numpy as jnp
from jax import lax
from jax.experimental import pallas as pl
from jax.experimental.pallas import tpu as pltpu
from jax.sharding import PartitionSpec as P

STEP = 10
BN_EPS = 1e-05
ALPHA = 0.1
F32 = jnp.float32
BF16 = jnp.bfloat16
HIGH = lax.Precision.HIGHEST
VMEM_BYTES = 56 * 1024 * 1024


TERMS = {
    1: ((0, 0),),
    2: ((1, 0), (0, 1), (0, 0)),
    3: ((2, 0), (1, 1), (0, 2), (1, 0), (0, 1), (0, 0)),
}


def mxu(a, b):
    return lax.dot_general(a, b, (((1,), (0,)), ((), ())), preferred_element_type=F32)


def mxu_t(a, b):
    return lax.dot_general(a, b, (((0,), (0,)), ((), ())), preferred_element_type=F32)


def split(x, n):
    parts = []
    for k in range(n):
        p = x.astype(BF16)
        parts.append(p)
        if k + 1 < n:
            x = x - p.astype(F32)
    return parts


def dup(v):
    return v + pltpu.roll(v, v.shape[-1] // 2, v.ndim - 1)


def low_half(shape):
    return lax.broadcasted_iota(jnp.int32, shape, len(shape) - 1) < shape[-1] // 2


def edges(rows, side):
    y = lax.rem(lax.broadcasted_iota(jnp.int32, (rows, 128), 0), side)
    return y == 0, y == side - 1


def down(x, top):
    return jnp.where(top, 0.0, pltpu.roll(x, 1, 0))


def up(x, bottom):
    return jnp.where(bottom, 0.0, pltpu.roll(x, x.shape[0] - 1, 0))


def row_sum(x):
    return jnp.sum(x, axis=0, keepdims=True)


def zero_ends(wide, k):
    last, rows = wide.shape[1] - 1, wide.shape[2]
    wide[k, last, :, 128:192] = jnp.zeros((rows, 64), BF16)
    wide[k, 0, :, 192:256] = jnp.zeros((rows, 64), BF16)


def put(wide, xp, parts):
    for k, part in enumerate(parts):
        wide[k, xp, :, 0:128] = part
        if xp > 0:
            wide[k, xp - 1, :, 128:192] = part[:, 0:64]
        if xp + 1 < wide.shape[1]:
            wide[k, xp + 1, :, 192:256] = part[:, 64:128]


def conv_block(pairs, top, bottom):
    z = None
    for a, b in pairs:
        t = mxu(a, b)
        z = t if z is None else z + t
    return down(z[:, 0:128], top) + z[:, 128:256] + up(z[:, 256:384], bottom)


def pair_form(t0, t1, t2):
    lt = low_half(t0.shape)
    return jnp.concatenate(
        [
            jnp.where(lt, t1, t0),
            jnp.where(lt, t2, t1),
            jnp.where(lt, 0.0, t2),
            jnp.where(lt, t0, 0.0),
        ],
        axis=0,
    )


def fold_pair(acc, out, base=0):
    for dy in range(3):
        b = acc[:, 128 * dy : 128 * dy + 128]
        even, odd, nxt, prv = b[0:64], b[64:128], b[128:192], b[192:256]
        lt = low_half(even.shape)
        taps = (jnp.where(lt, prv, even), jnp.where(lt, even, odd), jnp.where(lt, odd, nxt))
        for dx in range(3):
            r = base + 64 * (3 * dy + dx)
            out[r : r + 64] = dup(taps[dx])


def tap_distance(side, xp):
    xin = lax.broadcasted_iota(jnp.int32, (side, 128), 0)
    parity = jnp.where(low_half((side, 128)), 0, 1)
    return xin - 2 * xp - parity + 1


def stem_band(stem, side, xp):
    d = tap_distance(side, xp)
    blocks = []
    for dy in range(3):
        for c in range(4):
            if c == 3:
                blocks.append(jnp.zeros((side, 128), F32))
                continue
            s = [stem[12 * dx + 4 * dy + c : 12 * dx + 4 * dy + c + 1] for dx in range(3)]
            blocks.append(
                jnp.where(d == 0, s[0], jnp.where(d == 1, s[1], jnp.where(d == 2, s[2], 0.0)))
            )
    return jnp.concatenate(blocks, axis=0)


def stem_rows(img, top, bottom):
    lane = lax.broadcasted_iota(jnp.int32, img.shape, 1)
    img = jnp.where(lane < 96, img, 0.0)
    return jnp.concatenate([down(img, top), img, up(img, bottom)], axis=1)


def fold_stem(accs, side):
    rows = []
    for dx in range(3):
        for k in range(12):
            rows.append(dup(row_sum(accs[dx][side * k : side * k + side])))
    return jnp.concatenate(rows + [jnp.zeros((4, 128), F32)], axis=0)


def stem_fold_step(accs, f, side, xp):
    d = tap_distance(side, xp)
    d = jnp.concatenate([d] * 12, axis=0)
    return [a + jnp.where(d == dx, f, 0.0) for dx, a in enumerate(accs)]


def image_mark(img, images, at):
    row = img.reshape(images, img.shape[0] // images, 128)[:, 0, :]
    lane = lax.broadcasted_iota(jnp.int32, (images, 128), 1)
    return jnp.sum(jnp.where(lane == at, row, 0.0), axis=1, keepdims=True)


def label_onehot(img, images, classes):
    lab = image_mark(img, images, 96)
    lane = lax.broadcasted_iota(jnp.int32, (images, 128), 1)
    return jnp.where((lane.astype(F32) == lab) & (lane < classes), 1.0, 0.0)


def tree(xs):
    xs = list(xs)
    while len(xs) > 1:
        xs = [xs[k] + xs[k + 1] if k + 1 < len(xs) else xs[k] for k in range(0, len(xs), 2)]
    return xs[0]


def combine(blocks, count):
    each = count / len(blocks)
    mean = tree(b[0:1] for b in blocks) / count
    m2 = tree(b[1:2] + each * jnp.square(b[0:1] / each - mean) for b in blocks)
    return mean, lax.rsqrt(m2 / count + BN_EPS)


def stack_rows(rows, n=8):
    rows = list(rows)
    return jnp.concatenate(rows + [jnp.zeros((n - len(rows), 128), F32)], axis=0)


def centred_sums(a, s, count):
    mean = s / count
    m2 = jnp.zeros((1, 128), F32)
    for xp in range(a.shape[0]):
        d = a[xp] - mean
        m2 = m2 + row_sum(d * d)
    return dup(m2)


def k_weights(convs, norms, head_t, w1, w2, t1, t2, nv, hp, hpt, hb, sq):
    for k, (out, back) in enumerate(((w1, t1), (w2, t2))):
        for dy in range(3):
            sl = slice(128 * dy, 128 * dy + 128)
            taps = [both(convs[k, 3 * dy + dx]) for dx in range(3)]
            turned = [both(jnp.transpose(convs[k, 8 - 3 * dy - dx])) for dx in range(3)]
            for src, dst, n in ((taps, out, 3), (turned, back, 2)):
                for i, p in enumerate(split(pair_form(*src), n)):
                    dst[i, :, sl] = p
    nv[...] = stack_rows([both(norms[k // 2, k % 2 : k % 2 + 1]) for k in range(6)])
    classes, depth = head_t.shape
    sq[...] = jnp.zeros(sq.shape, F32)
    sq[0:classes, 0:depth] = head_t[...]
    sqv = sq[...]
    turned = jnp.transpose(sqv)
    row = lax.broadcasted_iota(jnp.int32, turned.shape, 0)
    hp[...] = jnp.where(row < depth - 1, turned, 0.0)
    hb[...] = stack_rows([turned[depth - 1 : depth]])
    hpt[...] = dup(jnp.where(low_half(sqv.shape), sqv, 0.0))


def both(w):
    return jnp.concatenate([w, w], axis=1)


def pack_image(img, n, marks):
    side = img.shape[2]
    lane = lax.broadcasted_iota(jnp.int32, (side, 32), 1)
    tail = jnp.zeros((side, 32), F32)
    for k, m in enumerate(marks):
        tail = jnp.where(lane == k, m.astype(F32), tail)
    return jnp.concatenate([img[n, 0], img[n, 1], img[n, 2], tail], axis=1)


def k_pack(lab, img, out):
    side = img.shape[2]
    for n in range(img.shape[0]):
        out[side * n : side * n + side] = pack_image(img, n, [lab[n]])


def k_first(n, side, classes, labels, flips, ids, clip, raw, stem, a0, st, img, s40):
    for i in range(raw.shape[0]):
        lab = jnp.where(flips[i] == 1, ids[i], labels[i])
        img[side * i : side * i + side] = pack_image(raw, i, [lab, clip[i]])
    s40[...] = jnp.zeros(s40.shape, F32)
    for dy in range(3):
        for dx in range(3):
            r = 12 * dx + 4 * dy
            s40[r : r + 3] = both(stem[dy, dx])
    k_stem(n, side, classes, img, s40, a0, st)


def k_stem(n, side, classes, img, stem, a0, st):
    rows = img.shape[0]
    pairs = a0.shape[0]
    top, bottom = edges(rows, side)
    lhs = split(stem_rows(img[...], top, bottom), n)
    s = jnp.zeros((1, 128), F32)
    st_stem = stem[...]
    for xp in range(0, pairs, 2):
        band = jnp.concatenate(
            [stem_band(st_stem, side, xp), stem_band(st_stem, side, xp + 1)], axis=1
        )
        rhs = split(band, n)
        z = None
        for i, j in TERMS[n]:
            t = mxu(lhs[i], rhs[j])
            z = t if z is None else z + t
        a0[xp] = z[:, 0:128]
        a0[xp + 1] = z[:, 128:256]
        s = s + row_sum(z[:, 0:128]) + row_sum(z[:, 128:256])
    s = dup(s)
    m2 = centred_sums(a0, s, rows * pairs * 2)
    counts = row_sum(label_onehot(img[...], rows // side, classes))
    st[...] = stack_rows([s, m2, counts])


SHARDS, CONV_ROWS, SMALL_ROWS = 8, 72, 16
SHARD_ROWS = CONV_ROWS + SMALL_ROWS
NORM_AT = SHARDS * SHARD_ROWS
PACKED = (NORM_AT + 8, 128)


def pack_params(stem_of, convs, norm_of, head_of, out, sq, small):
    out[NORM_AT : NORM_AT + 8] = jnp.zeros((8, 128), F32)
    for k in range(3):
        out[NORM_AT + 2 * k : NORM_AT + 2 * k + 2, 0:64] = norm_of(k)
    sq[...] = jnp.zeros(sq.shape, F32)
    head_t = head_of()
    sq[64 : 64 + head_t.shape[0], 0 : head_t.shape[1]] = head_t
    small[...] = jnp.transpose(sq[...])
    for dx in range(3):
        for dy in range(3):
            r = 12 * dx + 4 * dy
            small[r : r + 3, 0:64] = stem_of(dy, dx)
    for s in range(SHARDS):
        at = SHARD_ROWS * s
        for t in range(9):
            out[at + 8 * t : at + 8 * t + 8] = jnp.concatenate(
                [convs[0, t, 8 * s : 8 * s + 8], convs[1, t, 8 * s : 8 * s + 8]], axis=1
            )
        out[at + CONV_ROWS : at + SHARD_ROWS] = small[SMALL_ROWS * s : SMALL_ROWS * s + SMALL_ROWS]


def k_params(*refs):
    ins, outs, sq, small = refs[:16], refs[16:20], refs[20], refs[21]
    for k in range(4):
        stem, convs, norms, head = ins[4 * k : 4 * k + 4]
        own = k in (1, 2)
        pack_params(
            (lambda dy, dx, r=stem: r[dy, dx, :, 0, :]) if own else (lambda dy, dx, r=stem: r[dy, dx]),
            convs,
            lambda i, r=norms: r[i],
            (lambda r=head: r[:, 0, :]) if own else (lambda r=head: r[...]),
            outs[k],
            sq,
            small,
        )


def k_pieces(side, n, me, wide, back, d2, tsmall, wgp, st1, even, odd, acc, d1, small):
    weight_gradient(side, n, wide, back, d1, acc)
    images = wgp.shape[0] - 72
    lt = low_half((128, 128))
    small[...] = jnp.zeros((128, 128), F32)
    small[0:65] = wgp[images : images + 65]
    right = pltpu.roll(small[...], 64, 1)
    small[...] = jnp.zeros((128, 128), F32)
    small[0:40] = tsmall[0:40]
    small[...] = jnp.where(lt, small[...], right)
    rest = stack_rows(
        [tsmall[40:41], tsmall[41:42], st1[0:1], st1[1:2]]
        + [wgp[images + k : images + k + 1] for k in (66, 67, 65)]
    )
    lt8 = low_half((8, 128))
    for j in range(SHARDS):
        s = jnp.bitwise_xor(me[0], j)
        dst = (even, odd)[j % 2]
        k = j // 2
        for t in range(9):
            at = pl.ds(pl.multiple_of(64 * t + 8 * s, 8), 8)
            dst[k, 8 * t : 8 * t + 8] = jnp.where(lt8, d1[at], d2[at])
        dst[k, CONV_ROWS:SHARD_ROWS] = small[pl.ds(pl.multiple_of(SMALL_ROWS * s, 8), SMALL_ROWS)]
        dst[k, SHARD_ROWS : SHARD_ROWS + 8] = rest


def k_halves(even, got, *outs):
    for k, out in enumerate(outs):
        out[...] = even[k] + got[k]


def adam(q, p, m, v):
    first = 0.9 * m + 0.1 * q
    second = 0.999 * v + 0.001 * q * q
    step = first / (1.0 - 0.9**STEP) / (jnp.sqrt(second / (1.0 - 0.999**STEP)) + 1e-08) + 0.01 * p
    return first, second, 0.05 * step


def k_adam(count, nb, me, *refs):
    parts, refs = refs[:4], refs[4:]
    stat, refs = refs[:nb], refs[nb:]
    pp, pm, pv, vec0, grad, delta, rest, px, ps = refs
    total = tree([r[...] for r in parts])
    r8 = total[SHARD_ROWS : SHARD_ROWS + 8]
    rest[...] = r8
    st = tree([r[...] for r in stat])
    px[...] = jnp.zeros(px.shape, F32)
    ps[...] = jnp.zeros(ps.shape, F32)
    px[0:40] = st[0:40]
    ps[0:40] = st[40:80]
    at = pl.ds(pl.multiple_of(SMALL_ROWS * me[0], 8), SMALL_ROWS)
    gain = vec0[2:3] * vec0[1:2]
    sm = total[CONV_ROWS:SHARD_ROWS]
    fixed = gain * (sm - ps[at] * (r8[0:1] / count) - px[at] * (r8[1:2] / count))
    sm = jnp.where(low_half(sm.shape), fixed, sm)
    q = jnp.concatenate([total[0:CONV_ROWS], sm], axis=0)
    qn = stack_rows([r8[k : k + 1] for k in (1, 0, 3, 2, 5, 4)])
    grad[0:SHARD_ROWS] = q
    grad[SHARD_ROWS : SHARD_ROWS + 8] = qn
    at = pl.ds(pl.multiple_of(SHARD_ROWS * me[0], 8), SHARD_ROWS)
    delta[0:SHARD_ROWS] = adam(q, pp[at], pm[at], pv[at])[2]
    at = slice(NORM_AT, NORM_AT + 8)
    delta[SHARD_ROWS : SHARD_ROWS + 8] = adam(qn, pp[at], pm[at], pv[at])[2]


def k_total(ng, grad, *refs):
    deltas, (pay, norm) = refs[:ng], refs[ng:]
    total = tree([d[...] for d in deltas])
    pay[0:SHARD_ROWS] = grad[0:SHARD_ROWS]
    pay[SHARD_ROWS : 2 * SHARD_ROWS] = total[0:SHARD_ROWS]
    norm[0:8] = grad[SHARD_ROWS : SHARD_ROWS + 8]
    norm[8:16] = total[SHARD_ROWS : SHARD_ROWS + 8]


def k_update(groups, classes, me, *refs):
    pays, (norm, rest, pp, pm, pv, mom), refs = refs[:8], refs[8:14], refs[14:]
    news, lows, firsts, seconds, outers, loss = (
        refs[0:4],
        refs[4:8],
        refs[8:12],
        refs[12:16],
        refs[16:20],
        refs[20],
    )
    grad, delta = refs[21:]
    for j, pay in enumerate(pays):
        s = jnp.bitwise_xor(me[0], j)
        at = pl.ds(pl.multiple_of(SHARD_ROWS * s, 8), SHARD_ROWS)
        grad[at] = pay[0:SHARD_ROWS]
        delta[at] = pay[SHARD_ROWS : 2 * SHARD_ROWS]
    grad[NORM_AT : NORM_AT + 8] = norm[0:8]
    delta[NORM_AT : NORM_AT + 8] = norm[8:16]
    p = pp[...]
    first, second, _ = adam(grad[...], p, pm[...], pv[...])
    average = delta[...] / groups
    outer = 0.9 * mom[...] + average
    new = p - 0.7 * (average + 0.9 * outer)
    unpack(new, news, False)
    unpack(new, lows, False)
    unpack(outer, outers, False)
    unpack(first, firsts, True)
    unpack(second, seconds, True)
    loss[...] = jnp.broadcast_to(rest[6:7], (8, 128))


def unpack(x, outs, own):
    stem, convs, norms, head = outs
    dt = convs.dtype
    smalls = []
    for s in range(SHARDS):
        at = SHARD_ROWS * s
        for t in range(9):
            blk = x[at + 8 * t : at + 8 * t + 8].astype(dt)
            convs[0, t, 8 * s : 8 * s + 8] = blk[:, 0:64]
            convs[1, t, 8 * s : 8 * s + 8] = blk[:, 64:128]
        smalls.append(x[at + CONV_ROWS : at + SHARD_ROWS])
    small = jnp.concatenate(smalls, axis=0)
    turned = jnp.transpose(small)
    classes, depth = head.shape[0], head.shape[-1]
    head_t = turned[64 : 64 + classes, 0:depth].astype(dt)
    if own:
        for k in range(classes):
            head[k] = head_t[k : k + 1]
    else:
        head[...] = head_t
    for dy in range(3):
        for dx in range(3):
            r = 12 * dx + 4 * dy
            if own:
                for c in range(3):
                    stem[dy, dx, c] = small[r + c : r + c + 1, 0:64].astype(dt)
            else:
                stem[dy, dx] = small[r : r + 3, 0:64].astype(dt)
    for k in range(3):
        norms[k] = x[NORM_AT + 2 * k : NORM_AT + 2 * k + 2, 0:64].astype(dt)


def k_conv(n, side, nb, layer, count, *refs):
    a_in, nv = refs[0], refs[1]
    blocks, w = refs[2 : 2 + nb], refs[2 + nb]
    a_out, st, vec, wide = refs[3 + nb :]
    pairs, rows = a_in.shape[0], a_in.shape[1]
    top, bottom = edges(rows, side)
    bl = [b[...] for b in blocks]
    mean, r = combine(bl, count)
    gain, bias = nv[2 * layer : 2 * layer + 1], nv[2 * layer + 1 : 2 * layer + 2]
    counts = tree(b[2:3] for b in bl)
    vec[...] = stack_rows([mean, r, gain, bias, counts])
    for k in range(n):
        zero_ends(wide, k)

    def prep(xp):
        h = jnp.maximum(gain * ((a_in[xp] - mean) * r) + bias, 0.0)
        put(wide, xp, split(h, n))

    prep(0)
    s = jnp.zeros((1, 128), F32)
    for xp in range(pairs):
        if xp + 1 < pairs:
            prep(xp + 1)
        out = conv_block([(wide[i, xp], w[j]) for i, j in TERMS[n]], top, bottom)
        a_out[xp] = out
        s = s + row_sum(out)
    s = dup(s)
    m2 = centred_sums(a_out, s, rows * pairs * 2)
    st[...] = stack_rows([s, m2])


def bn(a, vec):
    xh = (a - vec[0:1]) * vec[1:2]
    return xh, vec[2:3] * xh + vec[3:4]


def k_head(val, side, nb, count, classes, group_count, *refs):
    a2, a0, vec0r, nv, img, hp, hpt, hb = refs[:8]
    blocks = refs[8 : 8 + nb]
    mz, vec2r, info, extra = refs[8 + nb :]
    pairs, rows = a2.shape[0], a2.shape[1]
    images = rows // side
    mean, r = combine([b[...] for b in blocks], count)
    vec2 = stack_rows([mean, r, nv[4:5], nv[5:6]])
    vec2r[...] = vec2
    vec0 = vec0r[...]
    zs = jnp.zeros((images, 128), F32)
    ms = jnp.zeros((images, 128), F32)
    xs = jnp.zeros((images, 128), F32)
    for xp in range(pairs):
        xh2, y2 = bn(a2[xp], vec2)
        z = y2 + jnp.maximum(bn(a0[xp], vec0)[1], 0.0)
        on = z > 0
        m = jnp.where(on, 1.0, 0.0)
        mz[xp] = m.astype(BF16)
        zs = zs + jnp.sum(jnp.where(on, z, 0.0).reshape(images, side, 128), axis=1)
        ms = ms + jnp.sum(m.reshape(images, side, 128), axis=1)
        xs = xs + jnp.sum(jnp.where(on, xh2, 0.0).reshape(images, side, 128), axis=1)
    area = side * pairs * 2
    lt = low_half((images, 128))
    pooled, ms, xs = dup(zs) / area, dup(ms), dup(xs)
    logits = lax.dot(pooled, hp[...], precision=HIGH) + hb[0:1]
    lane = lax.broadcasted_iota(jnp.int32, (images, 128), 1)
    ok = lane < classes
    top = jnp.max(jnp.where(ok, logits, -3e38), axis=1, keepdims=True)
    e = jnp.where(ok, jnp.exp(jnp.where(ok, logits - top, 0.0)), 0.0)
    tot = jnp.sum(e, axis=1, keepdims=True)
    onehot = label_onehot(img[...], images, classes)
    pm = e / tot - onehot
    ce = jnp.log(tot) + top - jnp.sum(onehot * logits, axis=1, keepdims=True)
    g = lax.dot(pm, hpt[...], precision=HIGH)
    if val:
        n_val = group_count
        gp = g / (n_val * area)
        info[...] = gp
        head = lax.dot_general(
            pooled, pm / n_val, (((0,), (0,)), ((), ())), precision=HIGH
        )
        extra[0:64] = head[0:64]
        extra[64:72] = stack_rows([row_sum(pm) / n_val])
        extra[72:80] = stack_rows([row_sum(gp * ms), row_sum(gp * xs)])
    else:
        cw = group_count / (classes * (vec0[4:5] + 1.0))
        per = jnp.sum(onehot * cw, axis=1, keepdims=True)
        uw = jnp.where(lt, g * ms, g * xs)
        pc = jnp.where(lane == 0, per, jnp.where(lane == 1, image_mark(img[...], images, 97), 0.0))
        extra[0:images] = uw
        extra[images : 2 * images] = pc
        for k, v in enumerate((g, ms, xs, pooled, pm, jnp.broadcast_to(ce, (images, 128)))):
            info[k] = v


def k_static(side, img, a0, vec0r, out):
    pairs, rows = a0.shape[0], a0.shape[1]
    top, bottom = edges(rows, side)
    vec0 = vec0r[...]
    lhs = split(stem_rows(img[...], top, bottom), 2)
    px, ps = stem_static(side, pairs, lhs, lambda xp: (a0[xp] - vec0[0:1]) * vec0[1:2], 2)
    out[0:40] = px
    out[40:80] = ps


def stem_grad(side, pairs, lhs, rhs_of, n):
    accs = [jnp.zeros((lhs[0].shape[1], 128), F32)] * 3
    for xp in range(0, pairs, 2):
        rhs = split(jnp.concatenate([rhs_of(xp), rhs_of(xp + 1)], axis=1), n)
        f = None
        for i, j in TERMS[n]:
            t = mxu_t(lhs[i], rhs[j])
            f = t if f is None else f + t
        accs = stem_fold_step(accs, f[:, 0:128], side, xp)
        accs = stem_fold_step(accs, f[:, 128:256], side, xp + 1)
    return fold_stem(accs, side)


def stem_static(side, pairs, lhs, rhs_of, n):
    px = stem_grad(side, pairs, lhs, rhs_of, n)
    sums = 0.0
    for part in lhs:
        sums = sums + jnp.sum(part.astype(F32), axis=0, keepdims=True)
    col = jnp.transpose(jnp.broadcast_to(sums, (8, sums.shape[1])))[:, 0:1]
    xin = lax.rem(lax.broadcasted_iota(jnp.int32, col.shape, 0), side)
    rows = []
    for dx in range(3):
        keep = xin <= side - 2 if dx == 0 else (xin >= 1 if dx == 2 else xin >= 0)
        c = jnp.where(keep, col, 0.0)
        for k in range(12):
            rows.append(jnp.broadcast_to(row_sum(c[side * k : side * k + side]), (1, 128)))
    ps = jnp.concatenate(rows + [jnp.zeros((4, 128), F32)], axis=0)
    return px, ps


def back_conv2(n, side, gp, vec2, s1, s2, count, a2, mz, a1, vec1, wt, wide, dy1, keep, extra):
    pairs, rows = a2.shape[0], a2.shape[1]
    images = rows // side
    top, bottom = edges(rows, side)
    for k in range(n):
        zero_ends(wide, k)
    k2 = vec2[2:3] * vec2[1:2]
    c0, c1 = k2 * s1 / count, k2 * s2 / count
    gk = gp * k2
    gk = jnp.broadcast_to(gk[:, None, :], (images, side, 128)).reshape(rows, 128)

    def prep(xp):
        xh2 = (a2[xp] - vec2[0:1]) * vec2[1:2]
        back = mz[xp].astype(F32) * gk - c0 - xh2 * c1
        parts = split(back, n)
        put(wide, xp, parts)
        extra(xp, back, parts)

    prep(0)
    q1 = jnp.zeros((1, 128), F32)
    q2 = jnp.zeros((1, 128), F32)
    for xp in range(pairs):
        if xp + 1 < pairs:
            prep(xp + 1)
        dh = conv_block([(wide[i, xp], wt[j]) for i, j in TERMS[n]], top, bottom)
        xh1, y1 = bn(a1[xp], vec1)
        dy = jnp.where(y1 > 0, dh, 0.0)
        dy1[xp] = dy
        q1 = q1 + row_sum(dy)
        q2 = q2 + row_sum(dy * xh1)
    return dup(q1), dup(q2)


def shifted(back, top, bottom):
    return jnp.concatenate([up(back, bottom), back, down(back, top)], axis=1)


def k_val_back2(side, nb, count, *refs):
    a2, mz, a1, vec2r, vec1r, gp, wt, wide1 = refs[:8]
    blocks = refs[8 : 8 + nb]
    dy1, st, g2 = refs[8 + nb : 11 + nb]
    wide, acc = refs[11 + nb :]
    rows = a2.shape[1]
    top, bottom = edges(rows, side)
    s1 = tree(b[72:73] for b in blocks)
    s2 = tree(b[73:74] for b in blocks)
    acc[...] = jnp.zeros(acc.shape, F32)

    def extra(xp, back, parts):
        acc[...] += mxu_t(wide1[0, xp], shifted(back, top, bottom).astype(BF16))

    q1, q2 = back_conv2(
        1, side, gp[...], vec2r[...], s1, s2, count, a2, mz, a1, vec1r[...], wt, wide, dy1, None, extra
    )
    fold_pair(acc[...], g2)
    st[...] = stack_rows([q1, q2, s1, s2])


def back_conv1(n, side, gp, vec1, vec0, s1, s2, count, dy1, a1, a0, mz, wt, wide, dy0, extra):
    pairs, rows = a1.shape[0], a1.shape[1]
    images = rows // side
    top, bottom = edges(rows, side)
    for k in range(n):
        zero_ends(wide, k)
    k1 = vec1[2:3] * vec1[1:2]
    c0, c1 = k1 * s1 / count, k1 * s2 / count
    gpr = jnp.broadcast_to(gp[:, None, :], (images, side, 128)).reshape(rows, 128)

    def prep(xp):
        xh1 = (a1[xp] - vec1[0:1]) * vec1[1:2]
        back = dy1[xp] * k1 - c0 - xh1 * c1
        parts = split(back, n)
        put(wide, xp, parts)
        extra(xp, back, parts)

    prep(0)
    q1 = jnp.zeros((1, 128), F32)
    q2 = jnp.zeros((1, 128), F32)
    for xp in range(pairs):
        if xp + 1 < pairs:
            prep(xp + 1)
        dh = conv_block([(wide[i, xp], wt[j]) for i, j in TERMS[n]], top, bottom)
        xh0, y0 = bn(a0[xp], vec0)
        dy = jnp.where(y0 > 0, dh + mz[xp].astype(F32) * gpr, 0.0)
        dy0[xp] = dy
        q1 = q1 + row_sum(dy)
        q2 = q2 + row_sum(dy * xh0)
    return dup(q1), dup(q2)


def k_val_back1(side, nb, count, *refs):
    dy1, a1, a0, mz, vec1r, vec0r, gp, wt, wide0, img = refs[:10]
    blocks = refs[10 : 10 + nb]
    g1, small = refs[10 + nb : 12 + nb]
    wide, acc, dy0 = refs[12 + nb :]
    pairs, rows = a1.shape[0], a1.shape[1]
    top, bottom = edges(rows, side)
    s1 = tree(b[0:1] for b in blocks)
    s2 = tree(b[1:2] for b in blocks)
    acc[...] = jnp.zeros(acc.shape, F32)
    vec0 = vec0r[...]

    def extra(xp, back, parts):
        acc[...] += mxu_t(wide0[0, xp], shifted(back, top, bottom).astype(BF16))

    q1, q2 = back_conv1(
        1, side, gp[...], vec1r[...], vec0, s1, s2, count, dy1, a1, a0, mz, wt, wide, dy0, extra
    )
    fold_pair(acc[...], g1)
    lhs = split(stem_rows(img[...], top, bottom), 1)
    small[0:40] = stem_grad(side, pairs, lhs, lambda xp: dy0[xp], 1)
    px, ps = stem_static(side, pairs, lhs, lambda xp: (a0[xp] - vec0[0:1]) * vec0[1:2], 1)
    small[40:80] = px
    small[80:120] = ps
    small[120:128] = stack_rows([q1, q2])


def k_tan1(side, nb, nv_blocks, count, count_val, *refs):
    img, a0, a1, vec0r, vec1r, w1, wide0, vvec0r = refs[:8]
    refs = refs[8:]
    stat = refs[:nb]
    refs = refs[nb:]
    smalls, g1s, sts = refs[:nv_blocks], refs[nv_blocks : 2 * nv_blocks], refs[2 * nv_blocks : 3 * nv_blocks]
    t1, th0, st, wide, v1 = refs[3 * nv_blocks :]
    pairs, rows = a1.shape[0], a1.shape[1]
    top, bottom = edges(rows, side)
    vec0, vec1, vv0 = vec0r[...], vec1r[...], vvec0r[...]
    small = sum(b[...] for b in smalls)
    q1, q2 = small[120:121], small[121:122]
    v0 = (
        vv0[2:3]
        * vv0[1:2]
        * (small[0:40] - small[80:120] * (q1 / count_val) - small[40:80] * (q2 / count_val))
    )
    static = tree(b[...] for b in stat)
    u1 = row_sum(v0 * static[40:80])
    u2 = row_sum(v0 * static[0:40])
    k0 = vec0[2:3] * vec0[1:2]
    e0 = q1 - k0 * u1 / count
    e1 = q2 - k0 * u2 / count
    for dy in range(3):
        taps = []
        for dx in range(3):
            r = 64 * (3 * dy + dx)
            taps.append(sum(g[r : r + 64] for g in g1s))
        v1[:, 128 * dy : 128 * dy + 128] = pair_form(*taps).astype(BF16)
    zero_ends(wide, 0)
    lhs = stem_rows(img[...], top, bottom).astype(BF16)
    tang = {}

    def prep(xp):
        if xp % 2 == 0:
            band = jnp.concatenate(
                [stem_band(v0, side, xp), stem_band(v0, side, xp + 1)], axis=1
            ).astype(BF16)
            z = mxu(lhs, band)
            tang[xp], tang[xp + 1] = z[:, 0:128], z[:, 128:256]
        xh0, y0 = bn(a0[xp], vec0)
        th = jnp.where(y0 > 0, k0 * tang.pop(xp) + e1 * xh0 + e0, 0.0).astype(BF16)
        th0[xp] = th
        put(wide, xp, [th])

    prep(0)
    p1 = jnp.zeros((1, 128), F32)
    p2 = jnp.zeros((1, 128), F32)
    for xp in range(pairs):
        if xp + 1 < pairs:
            prep(xp + 1)
        t = conv_block([(wide[0, xp], w1[0]), (wide0[0, xp], v1[...])], top, bottom)
        t1[xp] = t
        xh1 = (a1[xp] - vec1[0:1]) * vec1[1:2]
        p1 = p1 + row_sum(t)
        p2 = p2 + row_sum(t * xh1)
    vs = [sum(b[k : k + 1] for b in sts) for k in range(2)]
    st[...] = stack_rows([dup(p1), dup(p2), vs[0], vs[1], sts[0][2:3], sts[0][3:4]])


def k_tan2(side, nb, nv_blocks, count, *refs):
    t1, th0, a1, a2, mz, vec1r, vec2r, w2, wide1, info, own = refs[:11]
    refs = refs[11:]
    blocks = refs[:nb]
    refs = refs[nb:]
    g2s, heads = refs[:nv_blocks], refs[nv_blocks : 2 * nv_blocks]
    st, wide, v2 = refs[2 * nv_blocks :]
    pairs, rows = a1.shape[0], a1.shape[1]
    images = rows // side
    top, bottom = edges(rows, side)
    vec1, vec2 = vec1r[...], vec2r[...]
    u1 = tree(b[0:1] for b in blocks)
    u2 = tree(b[1:2] for b in blocks)
    k1 = vec1[2:3] * vec1[1:2]
    e0 = own[2:3] - k1 * u1 / count
    e1 = own[3:4] - k1 * u2 / count
    for dy in range(3):
        taps = []
        for dx in range(3):
            r = 64 * (3 * dy + dx)
            taps.append(sum(g[r : r + 64] for g in g2s))
        v2[:, 128 * dy : 128 * dy + 128] = pair_form(*taps).astype(BF16)
    zero_ends(wide, 0)

    def prep(xp):
        xh1, y1 = bn(a1[xp], vec1)
        th = jnp.where(y1 > 0, k1 * t1[xp] + e1 * xh1 + e0, 0.0).astype(BF16)
        put(wide, xp, [th])

    prep(0)
    p1 = jnp.zeros((1, 128), F32)
    p2 = jnp.zeros((1, 128), F32)
    asum = jnp.zeros((images, 128), F32)
    k2 = vec2[2:3] * vec2[1:2]
    for xp in range(pairs):
        if xp + 1 < pairs:
            prep(xp + 1)
        t = conv_block([(wide[0, xp], w2[0]), (wide1[0, xp], v2[...])], top, bottom)
        xh2 = (a2[xp] - vec2[0:1]) * vec2[1:2]
        p1 = p1 + row_sum(t)
        p2 = p2 + row_sum(t * xh2)
        m = mz[xp].astype(F32)
        asum = asum + jnp.sum(
            (m * (k2 * t + th0[xp].astype(F32))).reshape(images, side, 128), axis=1
        )
    asum = dup(asum)
    area = side * pairs * 2
    g, ms, xs, pooled, pm = (info[k] for k in range(5))
    inner = g * (asum + own[5:6] * xs + own[4:5] * ms)
    base = jnp.sum(jnp.where(low_half(inner.shape), inner, 0.0), axis=1, keepdims=True) / area
    vhead = sum(h[0:72] for h in heads)
    vh = jnp.concatenate([vhead[0:64], jnp.zeros((64, 128), F32)], axis=0)
    lin = lax.dot(pooled, vh, precision=HIGH) + vhead[64:65]
    base = base + jnp.sum(pm * lin, axis=1, keepdims=True)
    st[0:images] = jnp.broadcast_to(base, (images, 128))
    p1, p2 = dup(p1), dup(p2)
    st[images : images + 8] = stack_rows([jnp.where(low_half(p1.shape), p1, p2)])


def k_train_back2(side, nb, count, group_count, n, *refs):
    flag, a2, mz, a1, vec2r, vec1r, wt, info = refs[:8]
    refs = refs[8:]
    stat, dyn = refs[:nb], refs[nb : 2 * nb]
    dy1, st, back2, wgp, wide = refs[2 * nb :]
    pairs, rows = a2.shape[0], a2.shape[1]
    images = rows // side
    area = side * pairs * 2
    vec2 = vec2r[...]
    k2 = vec2[2:3] * vec2[1:2]
    each = stat[0].shape[0]
    tsum = 0.0
    for b in range(nb):
        for j in range(each):
            tsum = tsum + dyn[b][j, images : images + 1]
    tt = tsum * k2 / (count * area)
    raws, pers = [], []
    total = jnp.zeros((1, 1), F32)
    mag = jnp.zeros((1, 1), F32)
    for b in range(nb):
        for j in range(each):
            uw = stat[b][j, 0:images]
            pc = stat[b][j, images : 2 * images]
            per, clip = pc[:, 0:1], pc[:, 1:2]
            tan = dyn[b][j, 0:images, 0:1] - jnp.sum(uw * tt, axis=1, keepdims=True)
            score = -ALPHA * per * tan
            raw = clip * jnp.maximum(-score, 0.0)
            total = total + row_sum(raw)
            mag = mag + row_sum(clip * jnp.abs(score))
            raws.append(raw)
            pers.append(per)
    on = flag[0] == 1
    denom = jnp.maximum(total, 0.25 * mag) + 1e-06
    ssum = jnp.zeros((1, 128), F32)
    k = 0
    own = None
    for b in range(nb):
        for j in range(each):
            w = jnp.where(on, raws[k] / denom, 1.0 / group_count) * pers[k]
            own = w if own is None else own
            ssum = ssum + row_sum(w * stat[b][j, 0:images])
            k += 1
    ssum = ssum / area
    lt = low_half(ssum.shape)
    s1, s2 = dup(jnp.where(lt, ssum, 0.0)), dup(jnp.where(lt, 0.0, ssum))
    g, pooled, pm, ce = info[0], info[3], info[4], info[5]
    gp = own * g / area
    wgp[0:images] = gp
    head = lax.dot_general(pooled, own * pm, (((0,), (0,)), ((), ())), precision=HIGH)
    wgp[images : images + 64] = head[0:64]
    mine = row_sum(own * stat[0][0, 0:images]) / area
    o1, o2 = dup(jnp.where(lt, mine, 0.0)), dup(jnp.where(lt, 0.0, mine))
    wgp[images + 64 : images + 72] = stack_rows([row_sum(own * pm), row_sum(own * ce), o1, o2])

    def extra(xp, back, parts):
        for i, p in enumerate(parts):
            back2[i, xp] = p

    q1, q2 = back_conv2(
        n, side, gp, vec2, s1, s2, count, a2, mz, a1, vec1r[...], wt, wide, dy1, None, extra
    )
    st[...] = stack_rows([q1, q2])


def k_train_back1(side, nb, count, n, *refs):
    dy1, a1, a0, mz, vec1r, vec0r, wt, img, wgp = refs[:9]
    blocks = refs[9 : 9 + nb]
    small, back1, wide, dy0 = refs[9 + nb :]
    pairs, rows = a1.shape[0], a1.shape[1]
    images = rows // side
    top, bottom = edges(rows, side)
    s1 = tree(b[0:1] for b in blocks)
    s2 = tree(b[1:2] for b in blocks)

    def extra(xp, back, parts):
        for i, p in enumerate(parts):
            back1[i, xp] = p

    q1, q2 = back_conv1(
        n, side, wgp[0:images], vec1r[...], vec0r[...], s1, s2, count, dy1, a1, a0, mz, wt, wide, dy0, extra
    )
    lhs = split(stem_rows(img[...], top, bottom), n)
    small[0:40] = stem_grad(side, pairs, lhs, lambda xp: dy0[xp], n)
    small[40:48] = stack_rows([q1, q2, s1, s2])


def weight_gradient(side, n, wide, back, g, acc):
    pairs, rows = back.shape[1], back.shape[2]
    top, bottom = edges(rows, side)
    acc[...] = jnp.zeros(acc.shape, F32)
    for xp in range(pairs):
        rhs = [shifted(back[i, xp].astype(F32), top, bottom).astype(BF16) for i in range(n)]
        t = None
        for i, j in TERMS[n]:
            d = mxu_t(wide[i, xp], rhs[j])
            t = d if t is None else t + d
        acc[...] += t
    fold_pair(acc[...], g)


VM = pl.BlockSpec(memory_space=pltpu.VMEM)
SM = pl.BlockSpec(memory_space=pltpu.SMEM)


def call(kernel, outs, args, scratch=(), smem=(), flops=0):
    specs = [SM if i in smem else VM for i in range(len(args))]
    return pl.pallas_call(
        kernel,
        out_shape=[jax.ShapeDtypeStruct(s, d) for s, d in outs],
        in_specs=specs,
        out_specs=[VM] * len(outs),
        scratch_shapes=[pltpu.VMEM(s, d) for s, d in scratch],
        compiler_params=pltpu.CompilerParams(vmem_limit_bytes=VMEM_BYTES),
        cost_estimate=pl.CostEstimate(flops=flops, bytes_accessed=1 << 20, transcendentals=0),
    )(*args)


def swap(x, k, n):
    return lax.ppermute(x, "dp", [(i, i ^ k) for i in range(n)])


def add(a, b, step):
    return a + b


def chan(count, a, b, step):
    d = a[0:1] - b[0:1]
    cross = d * d / (2.0 * count * step)
    return a + b + jnp.pad(cross, ((1, a.shape[0] - 2), (0, 0)))


def near(x, team, merge):
    n = lax.axis_size("dp")
    k = 1
    while k < team // 2:
        x = merge(x, swap(x, k, n), k)
        k *= 2
    return [x, swap(x, k, n)] if team > 1 else [x]


def far(x, merge):
    n = lax.axis_size("dp")
    k = 1
    while k < n // 4:
        x = merge(x, swap(x, k, n), k)
        k *= 2
    return [x] + [swap(x, j * k, n) for j in range(1, n // k)]


def far_list(x):
    n = lax.axis_size("dp")
    x = x[None]
    k = 1
    while k < n // 4:
        x = jnp.concatenate([x, swap(x, k, n)], axis=0)
        k *= 2
    return [x] + [swap(x, j * k, n) for j in range(1, n // k)]


def body(
    train_images,
    train_labels,
    flip_flags,
    class_ids,
    clip_mask,
    norm_flag,
    val_images,
    val_labels,
    stem,
    convs,
    norms,
    head,
    m_stem,
    v_stem,
    m_convs,
    v_convs,
    m_norms,
    v_norms,
    m_head,
    v_head,
    mom_stem,
    mom_convs,
    mom_norms,
    mom_head,
):
    dp = lax.axis_size("dp")
    classes = head.shape[1]
    side, pairs = train_images.shape[1], train_images.shape[2] // 2
    images, val_each = train_images.shape[0], val_images.shape[0]
    group_train, group_val = dp * images, dp * val_each
    team = max(2, group_val // 16)
    rows, vrows = images * side, side * group_val // team
    vimages = group_val // team
    count, count_val = group_train * side * pairs * 2, group_val * side * pairs * 2
    nt, nval = 3, 1

    act = (pairs, rows, 128)
    st = ((8, 128), F32)
    square = ((128, 128), F32)

    def planes(img):
        return jnp.transpose(img, (0, 3, 1, 2))

    (vimg,) = call(
        k_pack, [((val_each * side, 128), F32)], [val_labels, planes(val_images)], smem=(0,)
    )
    vimg = jnp.concatenate(
        [vimg] + [swap(vimg, j * team, dp) for j in range(1, dp // team)], axis=0
    )
    a0, s0, img, s40 = call(
        functools.partial(k_first, nt, side, classes),
        [(act, F32), st, ((rows, 128), F32), ((40, 128), F32)],
        [train_labels, flip_flags, class_ids, clip_mask, planes(train_images), stem],
        smem=(0, 1, 2, 3),
    )
    forms = [((n, 256, 384), BF16) for n in (3, 3, 2, 2)]
    w1, w2, t1w, t2w, nv, hp, hpt, hb = call(
        k_weights,
        forms + [st, square, square, st],
        [convs.reshape(2, 9, 64, 64), norms, head.T],
        [square],
    )
    moment_views = [
        (
            jnp.transpose(x[0], (1, 2, 3, 0, 4)),
            x[1].reshape(2, 9, 64, 64),
            x[2][0],
            jnp.transpose(x[3], (2, 0, 1)),
        )
        for x in ((m_stem, m_convs, m_norms, m_head), (v_stem, v_convs, v_norms, v_head))
    ]
    packed = call(
        k_params,
        [(PACKED, F32)] * 4,
        [stem, convs.reshape(2, 9, 64, 64), norms, head.T]
        + [x for views in moment_views for x in views]
        + [mom_stem, mom_convs.reshape(2, 9, 64, 64), mom_norms, mom_head.T],
        [square, square],
    )

    act = (pairs, rows, 128)
    vact = (pairs, vrows, 128)

    def wide(n, r):
        return ((n, pairs, r, 256), BF16)

    b0 = far(s0, functools.partial(chan, rows * pairs * 2))
    va0, vs0 = call(
        functools.partial(k_stem, nval, side, classes), [(vact, F32), st], [vimg, s40]
    )
    vchan = functools.partial(chan, vrows * pairs * 2)
    vb0 = near(vs0, team, vchan)

    def conv(n, layer, r, total, a, blocks, w):
        return call(
            functools.partial(k_conv, n, side, len(blocks), layer, total),
            [((pairs, r, 128), F32), st, st, wide(n, r)],
            [a, nv] + blocks + [w],
        )

    a1, s1, vec0, wide0 = conv(nt, 0, rows, count, a0, b0, w1)
    b1 = far(s1, functools.partial(chan, rows * pairs * 2))
    va1, vs1, vvec0, vwide0 = conv(nval, 0, vrows, count_val, va0, vb0, w1)
    vb1 = near(vs1, team, vchan)
    va2, vs2, vvec1, vwide1 = conv(nval, 1, vrows, count_val, va1, vb1, w2)
    vb2 = near(vs2, team, vchan)
    a2, s2, vec1, wide1 = conv(nt, 1, rows, count, a1, b1, w2)
    b2 = far(s2, functools.partial(chan, rows * pairs * 2))

    vmz, vvec2, vgp, vextra = call(
        functools.partial(k_head, True, side, len(vb2), count_val, classes, group_val),
        [(vact, BF16), st, ((vimages, 128), F32), ((80, 128), F32)],
        [va2, va0, vvec0, nv, vimg, hp, hpt, hb] + vb2,
    )
    vextras = near(vextra, team, add)
    static = far(
        call(functools.partial(k_static, side), [((80, 128), F32)], [img, a0, vec0])[0], add
    )
    mz, vec2, info, gather = call(
        functools.partial(k_head, False, side, len(b2), count, classes, group_train),
        [(act, BF16), st, ((6, images, 128), F32), ((2 * images, 128), F32)],
        [a2, a0, vec0, nv, img, hp, hpt, hb] + b2,
    )
    stat = far_list(gather)

    vdy1, vst1, g2 = call(
        functools.partial(k_val_back2, side, len(vextras), count_val),
        [(vact, F32), st, ((576, 128), F32)],
        [va2, vmz, va1, vvec2, vvec1, vgp, t2w, vwide1] + vextras,
        [wide(1, vrows), ((256, 384), F32)],
    )
    vst1s = near(vst1, team, add)
    g2s = near(g2, team, add)
    g1, small = call(
        functools.partial(k_val_back1, side, len(vst1s), count_val),
        [((576, 128), F32), ((128, 128), F32)],
        [vdy1, va1, va0, vmz, vvec1, vvec0, vgp, t1w, vwide0, vimg] + vst1s,
        [wide(1, vrows), ((256, 384), F32), (vact, F32)],
    )
    smalls = near(small, team, add)
    g1s = near(g1, team, add)

    tan1, th0, ts1 = call(
        functools.partial(k_tan1, side, len(static), len(g1s), count, count_val),
        [(act, F32), (act, BF16), st],
        [img, a0, a1, vec0, vec1, w1, wide0, vvec0] + static + smalls + g1s + vst1s,
        [wide(1, rows), ((256, 384), BF16)],
    )
    tb1 = far(ts1, add)
    (ts2,) = call(
        functools.partial(k_tan2, side, len(tb1), len(g2s), count),
        [((images + 8, 128), F32)],
        [tan1, th0, a1, a2, mz, vec1, vec2, w2, wide1, info, ts1] + tb1 + g2s + vextras,
        [wide(1, rows), ((256, 384), BF16)],
    )
    dyn = far_list(ts2)

    nb_ = 2
    dy1, bs1, back2, wgp = call(
        functools.partial(k_train_back2, side, len(dyn), count, group_train, nb_),
        [(act, F32), st, ((nb_,) + act, BF16), ((images + 72, 128), F32)],
        [norm_flag, a2, mz, a1, vec2, vec1, t2w, info] + stat + dyn,
        [wide(nb_, rows)],
        smem=(0,),
    )
    bb1 = far(bs1, add)
    (d2,) = call(
        functools.partial(weight_gradient, side, nb_), [((576, 128), F32)], [wide1, back2], [((256, 384), F32)]
    )
    tsmall, back1 = call(
        functools.partial(k_train_back1, side, len(bb1), count, nb_),
        [((48, 128), F32), ((nb_,) + act, BF16)],
        [dy1, a1, a0, mz, vec1, vec0, t1w, img, wgp] + bb1,
        [wide(nb_, rows), (act, F32)],
    )

    me = lax.rem(lax.axis_index("dp"), SHARDS).astype(jnp.int32).reshape(1)
    piece = (SHARD_ROWS + 8, 128)
    even, odd = call(
        functools.partial(k_pieces, side, nb_),
        [((4,) + piece, F32)] * 2,
        [me, wide0, back1, d2, tsmall, wgp, bs1],
        [((256, 384), F32), ((576, 128), F32), square],
        smem=(0,),
    )
    k = SHARDS
    while k < dp:
        even, odd = even + swap(even, k, dp), odd + swap(odd, k, dp)
        k *= 2
    halves = call(k_halves, [(piece, F32)] * 4, [even, swap(odd, 1, dp)])
    parts = [halves[0]] + [swap(halves[k], 2 * k, dp) for k in range(1, 4)]
    grad, delta, rest = call(
        functools.partial(k_adam, count, len(static)),
        [(piece, F32), (piece, F32), st],
        [me] + parts + static + list(packed[:3]) + [vec0],
        [square, square],
        smem=(0,),
    )
    groups = lax.axis_size("group")
    deltas = [delta] + [
        lax.ppermute(delta, "group", [(i, i ^ k) for i in range(groups)])
        for k in range(1, groups)
    ]
    pay, norm = call(
        functools.partial(k_total, groups),
        [((2 * SHARD_ROWS, 128), F32), ((16, 128), F32)],
        [grad] + deltas,
    )
    pays = []
    for k in range(4):
        x = swap(pay, 2 * k, dp) if k else pay
        pays += [x, swap(x, 1, dp)]
    p4 = [(3, 3, 3, 64), (2, 9, 64, 64), (3, 2, 64), (classes, head.shape[0])]
    g4 = [(3, 3, 3, 1, 64), (2, 9, 64, 64), (3, 2, 64), (classes, 1, head.shape[0])]
    outs = call(
        functools.partial(k_update, groups, classes),
        [(x, F32) for x in p4]
        + [(x, BF16) for x in p4]
        + [(x, F32) for x in g4 + g4 + p4]
        + [st],
        [me] + pays + [norm, rest] + list(packed),
        [(PACKED, F32)] * 2,
        smem=(0,),
    )

    def plain(stem, convs, norms, head):
        return [stem, convs.reshape(2, 3, 3, 64, 64), norms, head.T]

    def own(stem, convs, norms, head):
        return [
            jnp.transpose(stem, (3, 0, 1, 2, 4)),
            convs.reshape(1, 2, 3, 3, 64, 64),
            norms[None],
            jnp.transpose(head, (1, 2, 0)),
        ]

    return (
        *plain(*outs[0:4]),
        *plain(*outs[4:8]),
        *own(*outs[8:12]),
        *own(*outs[12:16]),
        *plain(*outs[16:20]),
        outs[20][0, 0:1],
    )


def solution(mesh):
    split4 = P(("group", "dp"), None, None, None)
    split1 = P(("group", "dp"))
    group = P("group")
    whole = P()
    return jax.shard_map(
        body,
        mesh=mesh,
        in_specs=(split4, split1, split1, split1, split1, group, split4, split1)
        + (whole,) * 4
        + (group,) * 8
        + (whole,) * 4,
        out_specs=(whole,) * 8 + (group,) * 8 + (whole,) * 4 + (group,),
        check_vma=False,
    )
```

```python
import functools
import math

import jax
import jax.numpy as jnp
from jax import lax
from jax.experimental import pallas as pl
from jax.experimental.pallas import tpu as pltpu
from jax.sharding import PartitionSpec as P

STEP = 10
BN_EPS = 1e-05
ALPHA = 0.1
F32 = jnp.float32
BF16 = jnp.bfloat16
HIGH = lax.Precision.HIGHEST
VMEM_BYTES = 14 * 1024 * 1024
KEEP = 200000


TERMS = {
    1: ((0, 0),),
    2: ((1, 0), (0, 1), (0, 0)),
    3: ((2, 0), (1, 1), (0, 2), (1, 0), (0, 1), (0, 0)),
}


def mxu(a, b):
    return lax.dot_general(a, b, (((1,), (0,)), ((), ())), preferred_element_type=F32)


def mxu_t(a, b):
    return lax.dot_general(a, b, (((0,), (0,)), ((), ())), preferred_element_type=F32)


def split(x, n):
    parts = []
    for k in range(n):
        p = x.astype(BF16)
        parts.append(p)
        if k + 1 < n:
            x = x - p.astype(F32)
    return parts


def dup(v):
    return v + pltpu.roll(v, v.shape[-1] // 2, v.ndim - 1)


def low_half(shape):
    return lax.broadcasted_iota(jnp.int32, shape, len(shape) - 1) < shape[-1] // 2


def edges(rows, side):
    y = lax.rem(lax.broadcasted_iota(jnp.int32, (rows, 128), 0), side)
    return y == 0, y == side - 1


def down(x, top):
    return jnp.where(top, 0.0, pltpu.roll(x, 1, 0))


def up(x, bottom):
    return jnp.where(bottom, 0.0, pltpu.roll(x, x.shape[0] - 1, 0))


def row_sum(x):
    return jnp.sum(x, axis=0, keepdims=True)


def zero_ends(wide):
    last, rows = wide.shape[0] - 1, wide.shape[1]
    wide[last, :, 128:192] = jnp.zeros((rows, 64), BF16)
    wide[0, :, 192:256] = jnp.zeros((rows, 64), BF16)


def put(wides, xp, parts):
    for wide, part in zip(wides, parts):
        wide[xp, :, 0:128] = part
        if xp > 0:
            wide[xp - 1, :, 128:192] = part[:, 0:64]
        if xp + 1 < wide.shape[0]:
            wide[xp + 1, :, 192:256] = part[:, 64:128]


def row_taps(z, top, bottom):
    return down(z[:, 0:128], top) + z[:, 128:256] + up(z[:, 256:384], bottom)


def conv_block(lhs, w, top, bottom):
    n = len(lhs)
    z = [mxu(x, w[:, 0 : 384 * (n - k)]) for k, x in enumerate(lhs)]
    total = None
    for rank in range(n - 1, -1, -1):
        for k in range(rank + 1):
            j = rank - k
            part = z[k][:, 384 * j : 384 * j + 384]
            total = part if total is None else total + part
    return row_taps(total, top, bottom)


def pair_form(t0, t1, t2):
    lt = low_half(t0.shape)
    return jnp.concatenate(
        [
            jnp.where(lt, t1, t0),
            jnp.where(lt, t2, t1),
            jnp.where(lt, 0.0, t2),
            jnp.where(lt, t0, 0.0),
        ],
        axis=0,
    )


def fold_pair(acc, out, base=0):
    for dy in range(3):
        b = acc[:, 128 * dy : 128 * dy + 128]
        even, odd, nxt, prv = b[0:64], b[64:128], b[128:192], b[192:256]
        lt = low_half(even.shape)
        taps = (jnp.where(lt, prv, even), jnp.where(lt, even, odd), jnp.where(lt, odd, nxt))
        for dx in range(3):
            r = base + 64 * (3 * dy + dx)
            out[r : r + 64] = dup(taps[dx])


def near_rows(side, xp):
    first, last = max(0, 2 * xp - 1) // 8, min(side - 1, 2 * xp + 2) // 8
    shape = (8, 128)
    parity = jnp.where(low_half(shape), 0, 1)
    rows = lax.broadcasted_iota(jnp.int32, shape, 0)
    return {b: rows + (8 * b + 1 - 2 * xp) - parity for b in range(first, last + 1)}


def stem_band(stem, side, xp):
    near = near_rows(side, xp)
    zero = jnp.zeros((8, 128), F32)
    blocks = []
    for dy in range(3):
        for c in range(4):
            s = [stem[12 * dx + 4 * dy + c : 12 * dx + 4 * dy + c + 1] for dx in range(3)]
            for b in range(side // 8):
                if c == 3 or b not in near:
                    blocks.append(zero)
                    continue
                d = near[b]
                blocks.append(
                    jnp.where(d == 0, s[0], jnp.where(d == 1, s[1], jnp.where(d == 2, s[2], 0.0)))
                )
    return jnp.concatenate(blocks, axis=0)


def stem_rows(img, top, bottom):
    lane = lax.broadcasted_iota(jnp.int32, img.shape, 1)
    img = jnp.where(lane < 96, img, 0.0)
    return jnp.concatenate([down(img, top), img, up(img, bottom)], axis=1)


def image_mark(img, images, at):
    row = img.reshape(images, img.shape[0] // images, 128)[:, 0, :]
    lane = lax.broadcasted_iota(jnp.int32, (images, 128), 1)
    return jnp.sum(jnp.where(lane == at, row, 0.0), axis=1, keepdims=True)


def label_onehot(img, images, classes):
    lab = image_mark(img, images, 96)
    lane = lax.broadcasted_iota(jnp.int32, (images, 128), 1)
    return jnp.where((lane.astype(F32) == lab) & (lane < classes), 1.0, 0.0)


def tree(xs):
    xs = list(xs)
    while len(xs) > 1:
        xs = [xs[k] + xs[k + 1] if k + 1 < len(xs) else xs[k] for k in range(0, len(xs), 2)]
    return xs[0]


def combine(blocks, count):
    each = count / len(blocks)
    mean = tree(b[0:1] for b in blocks) / count
    m2 = tree(b[1:2] + each * jnp.square(b[0:1] / each - mean) for b in blocks)
    return mean, lax.rsqrt(m2 / count + BN_EPS)


def stack_rows(rows, n=8):
    rows = list(rows)
    return jnp.concatenate(rows + [jnp.zeros((n - len(rows), 128), F32)], axis=0)


def centred_sums(a, s, count):
    mean = s / count
    m2 = jnp.zeros((1, 128), F32)
    for xp in range(a.shape[0]):
        d = a[xp].astype(F32) - mean
        m2 = m2 + row_sum(d * d)
    return dup(m2)


def k_weights(convs, norms, head_t, w1, w2, t1, t2, nv, hp, hpt, hb, sq):
    for k, (out, back) in enumerate(((w1, t1), (w2, t2))):
        for dy in range(3):
            taps = [both(convs[k, 3 * dy + dx]) for dx in range(3)]
            turned = [both(jnp.transpose(convs[k, 8 - 3 * dy - dx])) for dx in range(3)]
            for src, dst, n in ((taps, out, 3), (turned, back, 2)):
                for i, p in enumerate(split(pair_form(*src), n)):
                    dst[:, 384 * i + 128 * dy : 384 * i + 128 * dy + 128] = p
    nv[...] = stack_rows([both(norms[k // 2, k % 2 : k % 2 + 1]) for k in range(6)])
    classes, depth = head_t.shape
    sq[...] = jnp.zeros(sq.shape, F32)
    sq[0:classes, 0:depth] = head_t[...]
    sqv = sq[...]
    turned = jnp.transpose(sqv)
    row = lax.broadcasted_iota(jnp.int32, turned.shape, 0)
    hp[...] = jnp.where(row < depth - 1, turned, 0.0)
    hb[...] = stack_rows([turned[depth - 1 : depth]])
    hpt[...] = dup(jnp.where(low_half(sqv.shape), sqv, 0.0))


def both(w):
    return jnp.concatenate([w, w], axis=1)


def pack_image(img, n, marks):
    side = img.shape[2]
    lane = lax.broadcasted_iota(jnp.int32, (side, 32), 1)
    tail = jnp.zeros((side, 32), F32)
    for k, m in enumerate(marks):
        tail = jnp.where(lane == k, m.astype(F32), tail)
    return jnp.concatenate([img[n, 0], img[n, 1], img[n, 2], tail], axis=1)


def k_pack(lab, img, out):
    side = img.shape[2]
    for n in range(img.shape[0]):
        out[side * n : side * n + side] = pack_image(img, n, [lab[n]])


def k_first(n, side, classes, labels, flips, ids, clip, raw, stem, after, a0, st, img, s40):
    for i in range(raw.shape[0]):
        lab = jnp.where(flips[i] == 1, ids[i], labels[i])
        img[side * i : side * i + side] = pack_image(raw, i, [lab, clip[i]])
    s40[...] = jnp.zeros(s40.shape, F32)
    for dy in range(3):
        for dx in range(3):
            r = 12 * dx + 4 * dy
            s40[r : r + 3] = both(stem[dy, dx])
    k_stem(n, side, classes, img, s40, a0, st)


def k_stem(n, side, classes, img, stem, a0, st):
    rows = img.shape[0]
    pairs = a0.shape[0]
    top, bottom = edges(rows, side)
    lhs = split(stem_rows(img[...], top, bottom), n)
    s = jnp.zeros((1, 128), F32)
    st_stem = stem[...]
    for xp in range(0, pairs, 2):
        band = jnp.concatenate(
            [stem_band(st_stem, side, xp), stem_band(st_stem, side, xp + 1)], axis=1
        )
        rhs = split(band, n)
        z = None
        for i, j in TERMS[n]:
            t = mxu(lhs[i], rhs[j])
            z = t if z is None else z + t
        a0[xp] = z[:, 0:128].astype(a0.dtype)
        a0[xp + 1] = z[:, 128:256].astype(a0.dtype)
        s = s + row_sum(z[:, 0:128]) + row_sum(z[:, 128:256])
    s = dup(s)
    m2 = centred_sums(a0, s, rows * pairs * 2)
    counts = row_sum(label_onehot(img[...], rows // side, classes))
    st[...] = stack_rows([s, m2, counts])


SHARDS, CONV_ROWS, SMALL_ROWS = 8, 72, 16
SHARD_ROWS = CONV_ROWS + SMALL_ROWS
NORM_AT = SHARDS * SHARD_ROWS
PACKED = (NORM_AT + 8, 128)


def pack_params(stem_of, convs, norm_of, head_of, out, sq, small):
    out[NORM_AT : NORM_AT + 8] = jnp.zeros((8, 128), F32)
    for k in range(3):
        out[NORM_AT + 2 * k : NORM_AT + 2 * k + 2, 0:64] = norm_of(k)
    sq[...] = jnp.zeros(sq.shape, F32)
    head_t = head_of()
    sq[64 : 64 + head_t.shape[0], 0 : head_t.shape[1]] = head_t
    small[...] = jnp.transpose(sq[...])
    for dx in range(3):
        for dy in range(3):
            r = 12 * dx + 4 * dy
            small[r : r + 3, 0:64] = stem_of(dy, dx)
    for s in range(SHARDS):
        at = SHARD_ROWS * s
        for t in range(9):
            out[at + 8 * t : at + 8 * t + 8] = jnp.concatenate(
                [convs[0, t, 8 * s : 8 * s + 8], convs[1, t, 8 * s : 8 * s + 8]], axis=1
            )
        out[at + CONV_ROWS : at + SHARD_ROWS] = small[SMALL_ROWS * s : SMALL_ROWS * s + SMALL_ROWS]


def k_params(*refs):
    ins, outs, sq, small = refs[:16], refs[16:20], refs[20], refs[21]
    for k in range(4):
        stem, convs, norms, head = ins[4 * k : 4 * k + 4]
        own = k in (1, 2)
        pack_params(
            (lambda dy, dx, r=stem: r[dy, dx, :, 0, :]) if own else (lambda dy, dx, r=stem: r[dy, dx]),
            convs,
            lambda i, r=norms: r[i],
            (lambda r=head: r[:, 0, :]) if own else (lambda r=head: r[...]),
            outs[k],
            sq,
            small,
        )


def k_pieces(side, n, count, me, *refs):
    a0, vec0, a1, vec1, dy1, d2, tsmall, wgp, st1, even, odd, acc, d1, small = refs[:14]
    back_at = back_of_norm1(vec1[...], tsmall[42:43], tsmall[43:44], count, dy1, a1)
    weight_gradient(side, n, a0, vec0[...], back_at, refs[14:], acc, d1)
    images = wgp.shape[0] - 80
    lt = low_half((128, 128))
    small[...] = jnp.zeros((128, 128), F32)
    small[0:65] = wgp[images : images + 65]
    right = pltpu.roll(small[...], 64, 1)
    small[...] = jnp.zeros((128, 128), F32)
    small[0:40] = tsmall[0:40]
    small[...] = jnp.where(lt, small[...], right)
    rest = stack_rows(
        [tsmall[40:41], tsmall[41:42], st1[0:1], st1[1:2]]
        + [wgp[images + k : images + k + 1] for k in (66, 67, 65)]
    )
    lt8 = low_half((8, 128))
    for j in range(SHARDS):
        s = jnp.bitwise_xor(me[0], j)
        dst = (even, odd)[j % 2]
        k = j // 2
        for t in range(9):
            at = pl.ds(pl.multiple_of(64 * t + 8 * s, 8), 8)
            dst[k, 8 * t : 8 * t + 8] = jnp.where(lt8, d1[at], d2[at])
        dst[k, CONV_ROWS:SHARD_ROWS] = small[pl.ds(pl.multiple_of(SMALL_ROWS * s, 8), SMALL_ROWS)]
        dst[k, SHARD_ROWS : SHARD_ROWS + 8] = rest


def k_halves(even, got, *outs):
    for k, out in enumerate(outs):
        out[...] = even[k] + got[k]


def adam(q, p, m, v):
    first = 0.9 * m + 0.1 * q
    second = 0.999 * v + 0.001 * q * q
    step = first / (1.0 - 0.9**STEP) / (jnp.sqrt(second / (1.0 - 0.999**STEP)) + 1e-08) + 0.01 * p
    return first, second, 0.05 * step


def k_adam(count, nb, me, *refs):
    parts, refs = refs[:4], refs[4:]
    stat, refs = refs[:nb], refs[nb:]
    pp, pm, pv, vec0, grad, delta, rest, px, ps = refs
    total = tree([r[...] for r in parts])
    r8 = total[SHARD_ROWS : SHARD_ROWS + 8]
    rest[...] = r8
    st = tree([r[...] for r in stat])
    px[...] = jnp.zeros(px.shape, F32)
    ps[...] = jnp.zeros(ps.shape, F32)
    px[0:40] = st[8:48]
    ps[0:40] = st[48:88]
    at = pl.ds(pl.multiple_of(SMALL_ROWS * me[0], 8), SMALL_ROWS)
    gain = vec0[2:3] * vec0[1:2]
    sm = total[CONV_ROWS:SHARD_ROWS]
    fixed = gain * (sm - ps[at] * (r8[0:1] / count) - px[at] * (r8[1:2] / count))
    sm = jnp.where(low_half(sm.shape), fixed, sm)
    q = jnp.concatenate([total[0:CONV_ROWS], sm], axis=0)
    qn = stack_rows([r8[k : k + 1] for k in (1, 0, 3, 2, 5, 4)])
    grad[0:SHARD_ROWS] = q
    grad[SHARD_ROWS : SHARD_ROWS + 8] = qn
    at = pl.ds(pl.multiple_of(SHARD_ROWS * me[0], 8), SHARD_ROWS)
    delta[0:SHARD_ROWS] = adam(q, pp[at], pm[at], pv[at])[2]
    at = slice(NORM_AT, NORM_AT + 8)
    delta[SHARD_ROWS : SHARD_ROWS + 8] = adam(qn, pp[at], pm[at], pv[at])[2]


def k_total(ng, grad, *refs):
    deltas, (pay, norm) = refs[:ng], refs[ng:]
    total = tree([d[...] for d in deltas])
    pay[0:SHARD_ROWS] = grad[0:SHARD_ROWS]
    pay[SHARD_ROWS : 2 * SHARD_ROWS] = total[0:SHARD_ROWS]
    norm[0:8] = grad[SHARD_ROWS : SHARD_ROWS + 8]
    norm[8:16] = total[SHARD_ROWS : SHARD_ROWS + 8]


def k_update(groups, classes, me, *refs):
    pays, (norm, rest, pp, pm, pv, mom), refs = refs[:8], refs[8:14], refs[14:]
    news, lows, firsts, seconds, outers, loss = (
        refs[0:4],
        refs[4:8],
        refs[8:12],
        refs[12:16],
        refs[16:20],
        refs[20],
    )
    grad, delta = refs[21:]
    for j, pay in enumerate(pays):
        s = jnp.bitwise_xor(me[0], j)
        at = pl.ds(pl.multiple_of(SHARD_ROWS * s, 8), SHARD_ROWS)
        grad[at] = pay[0:SHARD_ROWS]
        delta[at] = pay[SHARD_ROWS : 2 * SHARD_ROWS]
    grad[NORM_AT : NORM_AT + 8] = norm[0:8]
    delta[NORM_AT : NORM_AT + 8] = norm[8:16]
    p = pp[...]
    first, second, _ = adam(grad[...], p, pm[...], pv[...])
    average = delta[...] / groups
    outer = 0.9 * mom[...] + average
    new = p - 0.7 * (average + 0.9 * outer)
    unpack(new, news, False)
    unpack(new, lows, False)
    unpack(outer, outers, False)
    unpack(first, firsts, True)
    unpack(second, seconds, True)
    loss[...] = rest[6, 0:1]


def unpack(x, outs, own):
    stem, convs, norms, head = outs
    dt = convs.dtype
    smalls = []
    for s in range(SHARDS):
        at = SHARD_ROWS * s
        for t in range(9):
            blk = x[at + 8 * t : at + 8 * t + 8].astype(dt)
            convs[0, t, 8 * s : 8 * s + 8] = blk[:, 0:64]
            convs[1, t, 8 * s : 8 * s + 8] = blk[:, 64:128]
        smalls.append(x[at + CONV_ROWS : at + SHARD_ROWS])
    small = jnp.concatenate(smalls, axis=0)
    turned = jnp.transpose(small)
    classes, depth = head.shape[0], head.shape[-1]
    head_t = turned[64 : 64 + classes, 0:depth].astype(dt)
    if own:
        for k in range(classes):
            head[k] = head_t[k : k + 1]
    else:
        head[...] = head_t
    for dy in range(3):
        for dx in range(3):
            r = 12 * dx + 4 * dy
            if own:
                for c in range(3):
                    stem[dy, dx, c] = small[r + c : r + c + 1, 0:64].astype(dt)
            else:
                stem[dy, dx] = small[r : r + 3, 0:64].astype(dt)
    for k in range(3):
        norms[k] = x[NORM_AT + 2 * k : NORM_AT + 2 * k + 2, 0:64].astype(dt)


def k_conv(n, side, nb, layer, count, carried, *refs):
    a_in, nv = refs[0], refs[1]
    blocks, w = refs[2 : 2 + nb], refs[2 + nb]
    refs = refs[3 + nb :]
    riders, refs = refs[:carried], refs[carried:]
    a_out, st, vec = refs[:3]
    wides = refs[3:]
    for rider in riders:
        st[8:] = rider[...]
    pairs, rows = a_in.shape[0], a_in.shape[1]
    top, bottom = edges(rows, side)
    bl = [b[...] for b in blocks]
    mean, r = combine(bl, count)
    gain, bias = nv[2 * layer : 2 * layer + 1], nv[2 * layer + 1 : 2 * layer + 2]
    counts = tree(b[2:3] for b in bl)
    vec[...] = stack_rows([mean, r, gain, bias, counts])
    for wide in wides:
        zero_ends(wide)

    def prep(xp):
        h = jnp.maximum(gain * ((a_in[xp].astype(F32) - mean) * r) + bias, 0.0)
        put(wides, xp, split(h, n))

    prep(0)
    s = jnp.zeros((1, 128), F32)
    for xp in range(pairs):
        if xp + 1 < pairs:
            prep(xp + 1)
        out = conv_block([wide[xp] for wide in wides], w, top, bottom)
        a_out[xp] = out.astype(a_out.dtype)
        s = s + row_sum(out)
    s = dup(s)
    m2 = centred_sums(a_out, s, rows * pairs * 2)
    st[0:8] = stack_rows([s, m2])


def bn(a, vec):
    xh = (a.astype(F32) - vec[0:1]) * vec[1:2]
    return xh, vec[2:3] * xh + vec[3:4]


def k_head(val, side, nb, count, classes, group_count, *refs):
    a2, a0, vec0r, nv, img, hp, hpt, hb = refs[:8]
    blocks = refs[8 : 8 + nb]
    mz, vec2r, info, extra = refs[8 + nb :]
    pairs, rows = a2.shape[0], a2.shape[1]
    images = rows // side
    mean, r = combine([b[...] for b in blocks], count)
    vec2 = stack_rows([mean, r, nv[4:5], nv[5:6]])
    vec2r[...] = vec2
    vec0 = vec0r[...]
    zs = jnp.zeros((images, 128), F32)
    ms = jnp.zeros((images, 128), F32)
    xs = jnp.zeros((images, 128), F32)
    for xp in range(pairs):
        xh2, y2 = bn(a2[xp], vec2)
        z = y2 + jnp.maximum(bn(a0[xp], vec0)[1], 0.0)
        on = z > 0
        m = jnp.where(on, 1.0, 0.0)
        mz[xp] = m.astype(BF16)
        zs = zs + jnp.sum(jnp.where(on, z, 0.0).reshape(images, side, 128), axis=1)
        ms = ms + jnp.sum(m.reshape(images, side, 128), axis=1)
        xs = xs + jnp.sum(jnp.where(on, xh2, 0.0).reshape(images, side, 128), axis=1)
    area = side * pairs * 2
    lt = low_half((images, 128))
    pooled, ms, xs = dup(zs) / area, dup(ms), dup(xs)
    logits = lax.dot(pooled, hp[...], precision=HIGH) + hb[0:1]
    lane = lax.broadcasted_iota(jnp.int32, (images, 128), 1)
    ok = lane < classes
    top = jnp.max(jnp.where(ok, logits, -3e38), axis=1, keepdims=True)
    e = jnp.where(ok, jnp.exp(jnp.where(ok, logits - top, 0.0)), 0.0)
    tot = jnp.sum(e, axis=1, keepdims=True)
    onehot = label_onehot(img[...], images, classes)
    pm = e / tot - onehot
    ce = jnp.log(tot) + top - jnp.sum(onehot * logits, axis=1, keepdims=True)
    g = lax.dot(pm, hpt[...], precision=HIGH)
    if val:
        n_val = group_count
        gp = g / (n_val * area)
        info[...] = gp
        head = lax.dot_general(
            pooled, pm / n_val, (((0,), (0,)), ((), ())), precision=HIGH
        )
        extra[0:64] = head[0:64]
        extra[64:72] = stack_rows([row_sum(pm) / n_val])
        extra[72:80] = stack_rows([row_sum(gp * ms), row_sum(gp * xs)])
    else:
        cw = group_count / (classes * (vec0[4:5] + 1.0))
        per = jnp.sum(onehot * cw, axis=1, keepdims=True)
        uw = jnp.where(lt, g * ms, g * xs)
        pc = jnp.where(lane == 0, per, jnp.where(lane == 1, image_mark(img[...], images, 97), 0.0))
        extra[0:images] = uw
        extra[images : 2 * images] = pc
        for k, v in enumerate((g, ms, xs, pooled, pm, jnp.broadcast_to(ce, (images, 128)))):
            info[k] = v


def k_static(side, img, a0, vec0r, out):
    pairs, rows = a0.shape[0], a0.shape[1]
    top, bottom = edges(rows, side)
    vec0 = vec0r[...]
    whole = stem_rows(img[...], top, bottom)
    lhs = turned_rows(split(whole, 2))
    out[0:40] = stem_grad(
        side, pairs, lhs, lambda xp: split((a0[xp] - vec0[0:1]) * vec0[1:2], 2)
    )[0]
    out[40:80] = patch_sums(side, whole)


def turned_rows(parts):
    out = []
    for p in parts:
        t = jnp.transpose(p)
        out.append(jnp.concatenate([t[0:96], t[128:224], t[256:352]], axis=0))
    return out


def stem_grad(side, pairs, lhs, *rhs_of):
    n = len(lhs)
    count = len(rhs_of)
    accs = [{} for _ in rhs_of]
    width = 128 * count
    for xp in range(pairs):
        parts = [f(xp) for f in rhs_of]
        rhs = [jnp.concatenate([p[i] for p in parts], axis=1) for i in range(n)]
        f = None
        for i, j in TERMS[n]:
            t = mxu(lhs[i], rhs[j])
            f = t if f is None else f + t
        near = near_rows(side, xp)
        for q in range(count):
            for k in range(9):
                for b, d in near.items():
                    blk = f[side * k + 8 * b : side * k + 8 * b + 8, 128 * q : 128 * q + 128]
                    for dx in range(3):
                        v = jnp.where(d == dx, blk, 0.0)
                        key = (dx, k)
                        accs[q][key] = accs[q][key] + v if key in accs[q] else v
    outs = []
    zero = jnp.zeros((1, 128), F32)
    for acc in accs:
        rows = []
        for dx in range(3):
            for dy in range(3):
                rows += [dup(row_sum(acc[dx, 3 * dy + c])) for c in range(3)] + [zero]
        outs.append(jnp.concatenate(rows + [zero] * 4, axis=0))
    return outs


def patch_sums(side, whole):
    sums = row_sum(whole)
    col = jnp.transpose(jnp.broadcast_to(sums, (8, sums.shape[1])))[:, 0:1]
    xin = lax.rem(lax.broadcasted_iota(jnp.int32, col.shape, 0), side)
    rows = []
    for dx in range(3):
        keep = xin <= side - 2 if dx == 0 else (xin >= 1 if dx == 2 else xin >= 0)
        c = jnp.where(keep, col, 0.0)
        for k in range(12):
            rows.append(jnp.broadcast_to(row_sum(c[side * k : side * k + side]), (1, 128)))
    return jnp.concatenate(rows + [jnp.zeros((4, 128), F32)], axis=0)


def back_of_norm2(gp, vec2, s1, s2, count, side, a2, mz):
    images, rows = gp.shape[0], a2.shape[1]
    k2 = vec2[2:3] * vec2[1:2]
    c0, c1 = k2 * s1 / count, k2 * s2 / count
    gk = jnp.broadcast_to((gp * k2)[:, None, :], (images, side, 128)).reshape(rows, 128)

    def at(xp):
        xh2 = (a2[xp].astype(F32) - vec2[0:1]) * vec2[1:2]
        return mz[xp].astype(F32) * gk - c0 - xh2 * c1

    return at


def back_of_norm1(vec1, s1, s2, count, dy1, a1):
    k1 = vec1[2:3] * vec1[1:2]
    c0, c1 = k1 * s1 / count, k1 * s2 / count

    def at(xp):
        xh1 = (a1[xp].astype(F32) - vec1[0:1]) * vec1[1:2]
        return dy1[xp].astype(F32) * k1 - c0 - xh1 * c1

    return at


def back_conv2(n, side, gp, vec2, s1, s2, count, a2, mz, a1, vec1, wt, wides, dy1, extra):
    pairs, rows = a2.shape[0], a2.shape[1]
    images = rows // side
    top, bottom = edges(rows, side)
    for wide in wides:
        zero_ends(wide)
    back_at = back_of_norm2(gp, vec2, s1, s2, count, side, a2, mz)

    def prep(xp):
        back = back_at(xp)
        parts = split(back, n)
        put(wides, xp, parts)
        if extra is not None:
            extra(xp, back, parts)

    prep(0)
    q1 = jnp.zeros((1, 128), F32)
    q2 = jnp.zeros((1, 128), F32)
    for xp in range(pairs):
        if xp + 1 < pairs:
            prep(xp + 1)
        dh = conv_block([wide[xp] for wide in wides], wt, top, bottom)
        xh1, y1 = bn(a1[xp], vec1)
        dy = jnp.where(y1 > 0, dh, 0.0)
        dy1[xp] = dy.astype(dy1.dtype)
        q1 = q1 + row_sum(dy)
        q2 = q2 + row_sum(dy * xh1)
    return dup(q1), dup(q2)


def shifted(back, top, bottom):
    return jnp.concatenate([up(back, bottom), back, down(back, top)], axis=1)


def k_val_back2(side, nb, count, *refs):
    a2, mz, a1, vec2r, vec1r, gp, wt, wide1 = refs[:8]
    blocks = refs[8 : 8 + nb]
    dy1, st, g2 = refs[8 + nb : 11 + nb]
    wide, acc = refs[11 + nb :]
    wides = (wide,)
    rows = a2.shape[1]
    top, bottom = edges(rows, side)
    s1 = tree(b[72:73] for b in blocks)
    s2 = tree(b[73:74] for b in blocks)
    acc[...] = jnp.zeros(acc.shape, F32)

    def extra(xp, back, parts):
        acc[...] += mxu_t(shifted(back, top, bottom).astype(BF16), wide1[xp])

    q1, q2 = back_conv2(
        1, side, gp[...], vec2r[...], s1, s2, count, a2, mz, a1, vec1r[...], wt, wides, dy1, extra
    )
    fold_pair(jnp.transpose(acc[...]), g2)
    st[...] = stack_rows([q1, q2, s1, s2])


def back_conv1(n, side, gp, vec1, vec0, s1, s2, count, dy1, a1, a0, mz, wt, wides, dy0, extra):
    pairs, rows = a1.shape[0], a1.shape[1]
    images = rows // side
    top, bottom = edges(rows, side)
    for wide in wides:
        zero_ends(wide)
    back_at = back_of_norm1(vec1, s1, s2, count, dy1, a1)
    gpr = jnp.broadcast_to(gp[:, None, :], (images, side, 128)).reshape(rows, 128)

    def prep(xp):
        back = back_at(xp)
        parts = split(back, n)
        put(wides, xp, parts)
        if extra is not None:
            extra(xp, back, parts)

    prep(0)
    q1 = jnp.zeros((1, 128), F32)
    q2 = jnp.zeros((1, 128), F32)
    for xp in range(pairs):
        if xp + 1 < pairs:
            prep(xp + 1)
        dh = conv_block([wide[xp] for wide in wides], wt, top, bottom)
        xh0, y0 = bn(a0[xp], vec0)
        dy = jnp.where(y0 > 0, dh + mz[xp].astype(F32) * gpr, 0.0)
        dy0[xp] = dy.astype(dy0.dtype)
        q1 = q1 + row_sum(dy)
        q2 = q2 + row_sum(dy * xh0)
    return dup(q1), dup(q2)


def k_val_back1(side, nb, count, *refs):
    dy1, a1, a0, mz, vec1r, vec0r, gp, wt, wide0, img = refs[:10]
    blocks = refs[10 : 10 + nb]
    g1, small = refs[10 + nb : 12 + nb]
    wide, acc, dy0 = refs[12 + nb :]
    wides = (wide,)
    pairs, rows = a1.shape[0], a1.shape[1]
    top, bottom = edges(rows, side)
    s1 = tree(b[0:1] for b in blocks)
    s2 = tree(b[1:2] for b in blocks)
    acc[...] = jnp.zeros(acc.shape, F32)
    vec0 = vec0r[...]

    def extra(xp, back, parts):
        acc[...] += mxu_t(shifted(back, top, bottom).astype(BF16), wide0[xp])

    q1, q2 = back_conv1(
        1, side, gp[...], vec1r[...], vec0, s1, s2, count, dy1, a1, a0, mz, wt, wides, dy0, extra
    )
    fold_pair(jnp.transpose(acc[...]), g1)
    whole = stem_rows(img[...], top, bottom)
    small[0:40], small[40:80] = stem_grad(
        side,
        pairs,
        turned_rows([whole.astype(BF16)]),
        lambda xp: [dy0[xp]],
        lambda xp: [((a0[xp].astype(F32) - vec0[0:1]) * vec0[1:2]).astype(BF16)],
    )
    small[80:120] = patch_sums(side, whole)
    small[120:128] = stack_rows([q1, q2])


def k_tan1(side, nb, nv_blocks, count, count_val, *refs):
    img, a0, a1, vec0r, vec1r, w1, vvec0r, gather = refs[:8]
    refs = refs[8:]
    stat = refs[:nb]
    refs = refs[nb:]
    smalls, g1s, sts = refs[:nv_blocks], refs[nv_blocks : 2 * nv_blocks], refs[2 * nv_blocks : 3 * nv_blocks]
    t1, th0, st, wide, wide0, v1 = refs[3 * nv_blocks :]
    pairs, rows = a1.shape[0], a1.shape[1]
    top, bottom = edges(rows, side)
    vec0, vec1, vv0 = vec0r[...], vec1r[...], vvec0r[...]
    small = sum(b[...] for b in smalls)
    q1, q2 = small[120:121], small[121:122]
    v0 = (
        vv0[2:3]
        * vv0[1:2]
        * (small[0:40] - small[80:120] * (q1 / count_val) - small[40:80] * (q2 / count_val))
    )
    static = tree(b[...] for b in stat)
    u1 = row_sum(v0 * static[48:88])
    u2 = row_sum(v0 * static[8:48])
    k0 = vec0[2:3] * vec0[1:2]
    e0 = q1 - k0 * u1 / count
    e1 = q2 - k0 * u2 / count
    for dy in range(3):
        taps = []
        for dx in range(3):
            r = 64 * (3 * dy + dx)
            taps.append(sum(g[r : r + 64] for g in g1s))
        v1[:, 128 * dy : 128 * dy + 128] = pair_form(*taps).astype(BF16)
    zero_ends(wide)
    zero_ends(wide0)
    lhs = stem_rows(img[...], top, bottom).astype(BF16)
    tang = {}

    def prep(xp):
        if xp % 2 == 0:
            band = jnp.concatenate(
                [stem_band(v0, side, xp), stem_band(v0, side, xp + 1)], axis=1
            ).astype(BF16)
            z = mxu(lhs, band)
            tang[xp], tang[xp + 1] = z[:, 0:128], z[:, 128:256]
        xh0, y0 = bn(a0[xp], vec0)
        th = jnp.where(y0 > 0, k0 * tang.pop(xp) + e1 * xh0 + e0, 0.0).astype(BF16)
        th0[xp] = th
        put((wide, wide0), xp, [th, jnp.maximum(y0, 0.0).astype(BF16)])

    prep(0)
    p1 = jnp.zeros((1, 128), F32)
    p2 = jnp.zeros((1, 128), F32)
    for xp in range(pairs):
        if xp + 1 < pairs:
            prep(xp + 1)
        t = row_taps(mxu(wide[xp], w1[:, 0:384]) + mxu(wide0[xp], v1[...]), top, bottom)
        t1[xp] = t
        xh1 = (a1[xp] - vec1[0:1]) * vec1[1:2]
        p1 = p1 + row_sum(t)
        p2 = p2 + row_sum(t * xh1)
    vs = [sum(b[k : k + 1] for b in sts) for k in range(2)]
    st[0:8] = stack_rows([dup(p1), dup(p2), vs[0], vs[1], sts[0][2:3], sts[0][3:4]])
    st[8:] = gather[...]


def k_tan2(side, nb, nv_blocks, count, *refs):
    t1, th0, a1, a2, mz, vec1r, vec2r, w2, info, own = refs[:10]
    refs = refs[10:]
    blocks = refs[:nb]
    refs = refs[nb:]
    g2s, heads = refs[:nv_blocks], refs[nv_blocks : 2 * nv_blocks]
    st, wide, wide1, v2 = refs[2 * nv_blocks :]
    pairs, rows = a1.shape[0], a1.shape[1]
    images = rows // side
    top, bottom = edges(rows, side)
    vec1, vec2 = vec1r[...], vec2r[...]
    each = blocks[0].shape[0]
    u1 = tree(b[j, 0:1] for b in blocks for j in range(each))
    u2 = tree(b[j, 1:2] for b in blocks for j in range(each))
    k1 = vec1[2:3] * vec1[1:2]
    e0 = own[2:3] - k1 * u1 / count
    e1 = own[3:4] - k1 * u2 / count
    for dy in range(3):
        taps = []
        for dx in range(3):
            r = 64 * (3 * dy + dx)
            taps.append(sum(g[r : r + 64] for g in g2s))
        v2[:, 128 * dy : 128 * dy + 128] = pair_form(*taps).astype(BF16)
    zero_ends(wide)
    zero_ends(wide1)

    def prep(xp):
        xh1, y1 = bn(a1[xp], vec1)
        th = jnp.where(y1 > 0, k1 * t1[xp] + e1 * xh1 + e0, 0.0).astype(BF16)
        put((wide, wide1), xp, [th, jnp.maximum(y1, 0.0).astype(BF16)])

    prep(0)
    p1 = jnp.zeros((1, 128), F32)
    p2 = jnp.zeros((1, 128), F32)
    asum = jnp.zeros((images, 128), F32)
    k2 = vec2[2:3] * vec2[1:2]
    for xp in range(pairs):
        if xp + 1 < pairs:
            prep(xp + 1)
        t = row_taps(mxu(wide[xp], w2[:, 0:384]) + mxu(wide1[xp], v2[...]), top, bottom)
        xh2 = (a2[xp] - vec2[0:1]) * vec2[1:2]
        p1 = p1 + row_sum(t)
        p2 = p2 + row_sum(t * xh2)
        m = mz[xp].astype(F32)
        asum = asum + jnp.sum(
            (m * (k2 * t + th0[xp].astype(F32))).reshape(images, side, 128), axis=1
        )
    asum = dup(asum)
    area = side * pairs * 2
    g, ms, xs, pooled, pm = (info[k] for k in range(5))
    inner = g * (asum + own[5:6] * xs + own[4:5] * ms)
    base = jnp.sum(jnp.where(low_half(inner.shape), inner, 0.0), axis=1, keepdims=True) / area
    vhead = sum(h[0:72] for h in heads)
    vh = jnp.concatenate([vhead[0:64], jnp.zeros((64, 128), F32)], axis=0)
    lin = lax.dot(pooled, vh, precision=HIGH) + vhead[64:65]
    base = base + jnp.sum(pm * lin, axis=1, keepdims=True)
    st[0:images] = jnp.broadcast_to(base, (images, 128))
    p1, p2 = dup(p1), dup(p2)
    st[images : images + 8] = stack_rows([jnp.where(low_half(p1.shape), p1, p2)])


def k_train_back2(side, nb, count, group_count, n, *refs):
    flag, a2, mz, a1, vec2r, vec1r, wt, info = refs[:8]
    refs = refs[8:]
    stat, dyn = refs[:nb], refs[nb : 2 * nb]
    dy1, st, wgp = refs[2 * nb : 2 * nb + 3]
    wides = refs[2 * nb + 3 :]
    pairs, rows = a2.shape[0], a2.shape[1]
    images = rows // side
    area = side * pairs * 2
    vec2 = vec2r[...]
    k2 = vec2[2:3] * vec2[1:2]
    each = stat[0].shape[0]
    tsum = 0.0
    for b in range(nb):
        for j in range(each):
            tsum = tsum + dyn[b][j, images : images + 1]
    tt = tsum * k2 / (count * area)
    raws, pers = [], []
    total = jnp.zeros((1, 1), F32)
    mag = jnp.zeros((1, 1), F32)
    for b in range(nb):
        for j in range(each):
            uw = stat[b][j, 8 : 8 + images]
            pc = stat[b][j, 8 + images : 8 + 2 * images]
            per, clip = pc[:, 0:1], pc[:, 1:2]
            tan = dyn[b][j, 0:images, 0:1] - jnp.sum(uw * tt, axis=1, keepdims=True)
            score = -ALPHA * per * tan
            raw = clip * jnp.maximum(-score, 0.0)
            total = total + row_sum(raw)
            mag = mag + row_sum(clip * jnp.abs(score))
            raws.append(raw)
            pers.append(per)
    on = flag[0] == 1
    denom = jnp.maximum(total, 0.25 * mag) + 1e-06
    ssum = jnp.zeros((1, 128), F32)
    k = 0
    own = None
    for b in range(nb):
        for j in range(each):
            w = jnp.where(on, raws[k] / denom, 1.0 / group_count) * pers[k]
            own = w if own is None else own
            ssum = ssum + row_sum(w * stat[b][j, 8 : 8 + images])
            k += 1
    ssum = ssum / area
    lt = low_half(ssum.shape)
    s1, s2 = dup(jnp.where(lt, ssum, 0.0)), dup(jnp.where(lt, 0.0, ssum))
    g, pooled, pm, ce = info[0], info[3], info[4], info[5]
    gp = own * g / area
    wgp[0:images] = gp
    head = lax.dot_general(pooled, own * pm, (((0,), (0,)), ((), ())), precision=HIGH)
    wgp[images : images + 64] = head[0:64]
    mine = row_sum(own * stat[0][0, 8 : 8 + images]) / area
    o1, o2 = dup(jnp.where(lt, mine, 0.0)), dup(jnp.where(lt, 0.0, mine))
    wgp[images + 64 : images + 72] = stack_rows([row_sum(own * pm), row_sum(own * ce), o1, o2])

    wgp[images + 72 : images + 80] = stack_rows([s1, s2])
    q1, q2 = back_conv2(
        n, side, gp, vec2, s1, s2, count, a2, mz, a1, vec1r[...], wt, wides, dy1, None
    )
    st[...] = stack_rows([q1, q2])


def k_train_back1(side, nb, count, n, *refs):
    dy1, a1, a0, mz, vec1r, vec0r, wt, img, wgp = refs[:9]
    blocks = refs[9 : 9 + nb]
    small, dy0 = refs[9 + nb : 11 + nb]
    wides = refs[11 + nb :]
    pairs, rows = a1.shape[0], a1.shape[1]
    images = rows // side
    top, bottom = edges(rows, side)
    s1 = tree(b[0:1] for b in blocks)
    s2 = tree(b[1:2] for b in blocks)

    q1, q2 = back_conv1(
        n, side, wgp[0:images], vec1r[...], vec0r[...], s1, s2, count, dy1, a1, a0, mz, wt, wides, dy0, None
    )
    lhs = turned_rows(split(stem_rows(img[...], top, bottom), n))
    small[0:40] = stem_grad(side, pairs, lhs, lambda xp: split(dy0[xp], n))[0]
    small[40:48] = stack_rows([q1, q2, s1, s2])


def weight_gradient(side, n, a, vec, back_at, wides, acc, g):
    pairs, rows = a.shape[0], a.shape[1]
    top, bottom = edges(rows, side)
    acc[...] = jnp.zeros(acc.shape, F32)
    for wide in wides:
        zero_ends(wide)

    def prep(xp):
        put(wides, xp, split(jnp.maximum(bn(a[xp], vec)[1], 0.0), n))

    prep(0)
    for xp in range(pairs):
        if xp + 1 < pairs:
            prep(xp + 1)
        lhs = split(shifted(back_at(xp), top, bottom), n)
        t = None
        for i, j in TERMS[n]:
            d = mxu_t(lhs[i], wides[j][xp])
            t = d if t is None else t + d
        acc[...] += t
    fold_pair(jnp.transpose(acc[...]), g)


def k_dw2(side, n, count, a1, vec1, a2, vec2, mz, wgp, g, acc, *wides):
    images = a1.shape[1] // side
    at = images + 72
    back_at = back_of_norm2(
        wgp[0:images], vec2[...], wgp[at : at + 1], wgp[at + 1 : at + 2], count, side, a2, mz
    )
    weight_gradient(side, n, a1, vec1[...], back_at, wides, acc, g)


VM = pl.BlockSpec(memory_space=pltpu.VMEM)
SM = pl.BlockSpec(memory_space=pltpu.SMEM)


def call(kernel, outs, args, scratch=(), smem=(), raw=(), us=1.0):
    def placed(i, x):
        if i in raw:
            return pltpu.with_memory_space_constraint(x, pltpu.HBM)
        return pltpu.with_memory_space_constraint(x, pltpu.VMEM) if x.size >= KEEP else x

    return pl.pallas_call(
        kernel,
        out_shape=[
            pltpu.VMEM(s, d) if math.prod(s) >= KEEP else jax.ShapeDtypeStruct(s, d)
            for s, d in outs
        ],
        in_specs=[SM if i in smem else VM for i in range(len(args))],
        out_specs=[VM] * len(outs),
        scratch_shapes=[pltpu.VMEM(s, d) for s, d in scratch],
        compiler_params=pltpu.CompilerParams(vmem_limit_bytes=VMEM_BYTES),
        cost_estimate=pl.CostEstimate(
            flops=int(us * 1.1e9), bytes_accessed=1 << 16, transcendentals=0
        ),
    )(*[placed(i, x) for i, x in enumerate(args)])


def swap(x, k, n):
    return lax.ppermute(x, "dp", [(i, i ^ k) for i in range(n)])


def add(a, b, step):
    return a + b


def chan(count, a, b, step):
    d = a[0:1] - b[0:1]
    cross = d * d / (2.0 * count * step)
    return a + b + jnp.pad(cross, ((1, a.shape[0] - 2), (0, 0)))


def near(x, team, merge):
    n = lax.axis_size("dp")
    k = 1
    while k < team // 2:
        x = merge(x, swap(x, k, n), k)
        k *= 2
    return [x, swap(x, k, n)] if team > 1 else [x]


def far(x, merge):
    n = lax.axis_size("dp")
    k = 1
    while k < n // 4:
        x = merge(x, swap(x, k, n), k)
        k *= 2
    return [x] + [swap(x, j * k, n) for j in range(1, n // k)]


def far_list(x):
    n = lax.axis_size("dp")
    x = x[None]
    k = 1
    while k < n // 4:
        x = jnp.concatenate([x, swap(x, k, n)], axis=0)
        k *= 2
    return [x] + [swap(x, j * k, n) for j in range(1, n // k)]


def body(
    train_images,
    train_labels,
    flip_flags,
    class_ids,
    clip_mask,
    norm_flag,
    val_images,
    val_labels,
    stem,
    convs,
    norms,
    head,
    m_stem,
    v_stem,
    m_convs,
    v_convs,
    m_norms,
    v_norms,
    m_head,
    v_head,
    mom_stem,
    mom_convs,
    mom_norms,
    mom_head,
):
    dp = lax.axis_size("dp")
    classes = head.shape[1]
    side, pairs = train_images.shape[1], train_images.shape[2] // 2
    images, val_each = train_images.shape[0], val_images.shape[0]
    group_train, group_val = dp * images, dp * val_each
    team = max(2, group_val // 16)
    rows, vrows = images * side, side * group_val // team
    vimages = group_val // team
    count, count_val = group_train * side * pairs * 2, group_val * side * pairs * 2
    nt, nval = 3, 1

    act = (pairs, rows, 128)
    st = ((8, 128), F32)
    square = ((128, 128), F32)

    def planes(img):
        return jnp.transpose(img, (0, 3, 1, 2))

    (vpack,) = call(
        k_pack, [((val_each * side, 128), F32)], [val_labels, planes(val_images)], smem=(0,), raw=(0, 1)
    )
    vimg = jnp.concatenate(
        [vpack] + [swap(vpack, j * team, dp) for j in range(1, dp // team)], axis=0
    )
    a0, s0, img, s40 = call(
        functools.partial(k_first, nt, side, classes),
        [(act, F32), st, ((rows, 128), F32), ((40, 128), F32)],
        [train_labels, flip_flags, class_ids, clip_mask, planes(train_images), stem, vpack],
        smem=(0, 1, 2, 3),
        raw=range(6),
        us=4.5,
    )
    forms = [((256, 384 * n), BF16) for n in (3, 3, 2, 2)]
    w1, w2, t1w, t2w, nv, hp, hpt, hb = call(
        k_weights,
        forms + [st, square, square, st],
        [convs.reshape(2, 9, 64, 64), norms, head.T],
        [square],
        raw=range(3),
        us=2.0,
    )
    moment_views = [
        (
            jnp.transpose(x[0], (1, 2, 3, 0, 4)),
            x[1].reshape(2, 9, 64, 64),
            x[2][0],
            jnp.transpose(x[3], (2, 0, 1)),
        )
        for x in ((m_stem, m_convs, m_norms, m_head), (v_stem, v_convs, v_norms, v_head))
    ]
    packed = call(
        k_params,
        [(PACKED, F32)] * 4,
        [stem, convs.reshape(2, 9, 64, 64), norms, head.T]
        + [x for views in moment_views for x in views]
        + [mom_stem, mom_convs.reshape(2, 9, 64, 64), mom_norms, mom_head.T],
        [square, square],
        raw=range(16),
        us=2.0,
    )

    act = (pairs, rows, 128)
    vact = (pairs, vrows, 128)

    def wide(r):
        return ((pairs, r, 256), BF16)

    b0 = far(s0, functools.partial(chan, rows * pairs * 2))
    va0, vs0 = call(
        functools.partial(k_stem, nval, side, classes), [(vact, BF16), st], [vimg, s40], us=2.4
    )
    vchan = functools.partial(chan, vrows * pairs * 2)
    vb0 = near(vs0, team, vchan)

    def conv(n, layer, r, total, a, blocks, w, rider=()):
        pay = ((8 + sum(x.shape[0] for x in rider), 128), F32)
        return call(
            functools.partial(k_conv, n, side, len(blocks), layer, total, len(rider)),
            [((pairs, r, 128), F32 if n > 1 else BF16), pay, st] + [wide(r)] * (n == 1),
            [a, nv] + blocks + [w] + list(rider),
            [wide(r)] * n * (n > 1),
            us=7.8 if n > 1 else 3.3,
        )

    a1, s1, vec0 = conv(nt, 0, rows, count, a0, b0, w1)
    b1 = far(s1, functools.partial(chan, rows * pairs * 2))
    va1, vs1, vvec0, vwide0 = conv(nval, 0, vrows, count_val, va0, vb0, w1)
    vb1 = near(vs1, team, vchan)
    va2, vs2, vvec1, vwide1 = conv(nval, 1, vrows, count_val, va1, vb1, w2)
    vb2 = near(vs2, team, vchan)
    static = call(
        functools.partial(k_static, side), [((80, 128), F32)], [img, a0, vec0], us=2.0
    )
    a2, s2, vec1 = conv(nt, 1, rows, count, a1, b1, w2, static)
    b2 = far(s2, functools.partial(chan, rows * pairs * 2))

    vmz, vvec2, vgp, vextra = call(
        functools.partial(k_head, True, side, len(vb2), count_val, classes, group_val),
        [(vact, BF16), st, ((vimages, 128), F32), ((80, 128), F32)],
        [va2, va0, vvec0, nv, vimg, hp, hpt, hb] + vb2,
    )
    vextras = near(vextra, team, add)
    mz, vec2, info, gather = call(
        functools.partial(k_head, False, side, len(b2), count, classes, group_train),
        [(act, BF16), st, ((6, images, 128), F32), ((2 * images, 128), F32)],
        [a2, a0, vec0, nv, img, hp, hpt, hb] + b2,
    )

    vdy1, vst1, g2 = call(
        functools.partial(k_val_back2, side, len(vextras), count_val),
        [(vact, BF16), st, ((576, 128), F32)],
        [va2, vmz, va1, vvec2, vvec1, vgp, t2w, vwide1] + vextras,
        [wide(vrows), ((384, 256), F32)],
    )
    vst1s = near(vst1, team, add)
    g2s = near(g2, team, add)
    g1, small = call(
        functools.partial(k_val_back1, side, len(vst1s), count_val),
        [((576, 128), F32), ((128, 128), F32)],
        [vdy1, va1, va0, vmz, vvec1, vvec0, vgp, t1w, vwide0, vimg] + vst1s,
        [wide(vrows), ((384, 256), F32), (vact, BF16)],
    )
    smalls = near(small, team, add)
    g1s = near(g1, team, add)

    tan1, th0, ts1 = call(
        functools.partial(k_tan1, side, len(b2), len(g1s), count, count_val),
        [(act, F32), (act, BF16), ((8 + 2 * images, 128), F32)],
        [img, a0, a1, vec0, vec1, w1, vvec0, gather] + b2 + smalls + g1s + vst1s,
        [wide(rows), wide(rows), ((256, 384), BF16)],
    )
    stat = far_list(ts1)
    (ts2,) = call(
        functools.partial(k_tan2, side, len(stat), len(g2s), count),
        [((images + 8, 128), F32)],
        [tan1, th0, a1, a2, mz, vec1, vec2, w2, info, ts1] + stat + g2s + vextras,
        [wide(rows), wide(rows), ((256, 384), BF16)],
    )
    dyn = far_list(ts2)

    nb_ = 2
    dy1, bs1, wgp = call(
        functools.partial(k_train_back2, side, len(dyn), count, group_train, nb_),
        [(act, F32), st, ((images + 80, 128), F32)],
        [norm_flag, a2, mz, a1, vec2, vec1, t2w, info] + stat + dyn,
        [wide(rows)] * nb_,
        smem=(0,),
    )
    bb1 = far(bs1, add)
    (d2,) = call(
        functools.partial(k_dw2, side, nb_, count),
        [((576, 128), F32)],
        [a1, vec1, a2, vec2, mz, wgp],
        [((384, 256), F32)] + [wide(rows)] * nb_,
        us=3.6,
    )
    (tsmall,) = call(
        functools.partial(k_train_back1, side, len(bb1), count, nb_),
        [((48, 128), F32)],
        [dy1, a1, a0, mz, vec1, vec0, t1w, img, wgp] + bb1,
        [(act, F32)] + [wide(rows)] * nb_,
        us=5.5,
    )

    me = lax.rem(lax.axis_index("dp"), SHARDS).astype(jnp.int32).reshape(1)
    piece = (SHARD_ROWS + 8, 128)
    even, odd = call(
        functools.partial(k_pieces, side, nb_, count),
        [((4,) + piece, F32)] * 2,
        [me, a0, vec0, a1, vec1, dy1, d2, tsmall, wgp, bs1],
        [((384, 256), F32), ((576, 128), F32), square] + [wide(rows)] * nb_,
        us=4.0,
        smem=(0,),
    )
    k = SHARDS
    while k < dp:
        even, odd = even + swap(even, k, dp), odd + swap(odd, k, dp)
        k *= 2
    halves = call(k_halves, [(piece, F32)] * 4, [even, swap(odd, 1, dp)])
    parts = [halves[0]] + [swap(halves[k], 2 * k, dp) for k in range(1, 4)]
    grad, delta, rest = call(
        functools.partial(k_adam, count, len(b2)),
        [(piece, F32), (piece, F32), st],
        [me] + parts + b2 + list(packed[:3]) + [vec0],
        [square, square],
        smem=(0,),
    )
    groups = lax.axis_size("group")
    deltas = [delta] + [
        lax.ppermute(delta, "group", [(i, i ^ k) for i in range(groups)])
        for k in range(1, groups)
    ]
    pay, norm = call(
        functools.partial(k_total, groups),
        [((2 * SHARD_ROWS, 128), F32), ((16, 128), F32)],
        [grad] + deltas,
    )
    pays = []
    for k in range(4):
        x = swap(pay, 2 * k, dp) if k else pay
        pays += [x, swap(x, 1, dp)]
    p4 = [(3, 3, 3, 64), (2, 9, 64, 64), (3, 2, 64), (classes, head.shape[0])]
    g4 = [(3, 3, 3, 1, 64), (2, 9, 64, 64), (3, 2, 64), (classes, 1, head.shape[0])]
    outs = call(
        functools.partial(k_update, groups, classes),
        [(x, F32) for x in p4]
        + [(x, BF16) for x in p4]
        + [(x, F32) for x in g4 + g4 + p4]
        + [((1,), F32)],
        [me] + pays + [norm, rest] + list(packed),
        [(PACKED, F32)] * 2,
        smem=(0,),
    )

    def plain(stem, convs, norms, head):
        return [stem, convs.reshape(2, 3, 3, 64, 64), norms, head.T]

    def own(stem, convs, norms, head):
        return [
            jnp.transpose(stem, (3, 0, 1, 2, 4)),
            convs.reshape(1, 2, 3, 3, 64, 64),
            norms[None],
            jnp.transpose(head, (1, 2, 0)),
        ]

    return (
        *plain(*outs[0:4]),
        *plain(*outs[4:8]),
        *own(*outs[8:12]),
        *own(*outs[12:16]),
        *plain(*outs[16:20]),
        outs[20],
    )


def solution(mesh):
    split4 = P(("group", "dp"), None, None, None)
    split1 = P(("group", "dp"))
    group = P("group")
    whole = P()
    return jax.shard_map(
        body,
        mesh=mesh,
        in_specs=(split4, split1, split1, split1, split1, group, split4, split1)
        + (whole,) * 4
        + (group,) * 8
        + (whole,) * 4,
        out_specs=(whole,) * 8 + (group,) * 8 + (whole,) * 4 + (group,),
        check_vma=False,
    )
```

```python
import functools
import math

import jax
import jax.numpy as jnp
from jax import lax
from jax.experimental import pallas as pl
from jax.experimental.pallas import tpu as pltpu
from jax.sharding import PartitionSpec as P

STEP = 10
BN_EPS = 1e-05
ALPHA = 0.1
F32 = jnp.float32
BF16 = jnp.bfloat16
HIGH = lax.Precision.HIGHEST
VMEM_BYTES = 18 * 1024 * 1024
KEEP = 200000


TERMS = {
    1: ((0, 0),),
    2: ((1, 0), (0, 1), (0, 0)),
    3: ((2, 0), (1, 1), (0, 2), (1, 0), (0, 1), (0, 0)),
}


def mxu(a, b):
    return lax.dot_general(a, b, (((1,), (0,)), ((), ())), preferred_element_type=F32)


def mxu_t(a, b):
    return lax.dot_general(a, b, (((0,), (0,)), ((), ())), preferred_element_type=F32)


def split(x, n):
    parts = []
    for k in range(n):
        p = x.astype(BF16)
        parts.append(p)
        if k + 1 < n:
            x = x - p.astype(F32)
    return parts


def dup(v):
    return v + pltpu.roll(v, v.shape[-1] // 2, v.ndim - 1)


def low_half(shape):
    return lax.broadcasted_iota(jnp.int32, shape, len(shape) - 1) < shape[-1] // 2


def edges(rows, side):
    y = lax.rem(lax.broadcasted_iota(jnp.int32, (rows, 128), 0), side)
    return y == 0, y == side - 1


def down(x, top):
    return jnp.where(top, 0.0, pltpu.roll(x, 1, 0))


def up(x, bottom):
    return jnp.where(bottom, 0.0, pltpu.roll(x, x.shape[0] - 1, 0))


def row_sum(x):
    return jnp.sum(x, axis=0, keepdims=True)


def part(x):
    return jnp.sum(x.reshape(x.shape[0] // 8, 8, 128), axis=0)


def image_part(x, images):
    return jnp.sum(x.reshape(images, x.shape[0] // (8 * images), 8, 128), axis=1)


def zero_ends(wide):
    last, rows = wide.shape[0] - 1, wide.shape[1]
    wide[last, :, 128:192] = jnp.zeros((rows, 64), BF16)
    wide[0, :, 192:256] = jnp.zeros((rows, 64), BF16)


def put(wides, xp, parts):
    for wide, part in zip(wides, parts):
        wide[xp, :, 0:128] = part
        if xp > 0:
            wide[xp - 1, :, 128:192] = part[:, 0:64]
        if xp + 1 < wide.shape[0]:
            wide[xp + 1, :, 192:256] = part[:, 64:128]


def row_taps(z, top, bottom):
    return down(z[:, 0:128], top) + z[:, 128:256] + up(z[:, 256:384], bottom)


def conv_block(lhs, w, top, bottom):
    n = len(lhs)
    z = [mxu(x, w[:, 0 : 384 * (n - k)]) for k, x in enumerate(lhs)]
    total = None
    for rank in range(n - 1, -1, -1):
        for k in range(rank + 1):
            j = rank - k
            part = z[k][:, 384 * j : 384 * j + 384]
            total = part if total is None else total + part
    return row_taps(total, top, bottom)


def pair_form(t0, t1, t2):
    lt = low_half(t0.shape)
    return jnp.concatenate(
        [
            jnp.where(lt, t1, t0),
            jnp.where(lt, t2, t1),
            jnp.where(lt, 0.0, t2),
            jnp.where(lt, t0, 0.0),
        ],
        axis=0,
    )


def fold_pair(acc, out, base=0):
    for dy in range(3):
        b = acc[:, 128 * dy : 128 * dy + 128]
        even, odd, nxt, prv = b[0:64], b[64:128], b[128:192], b[192:256]
        lt = low_half(even.shape)
        taps = (jnp.where(lt, prv, even), jnp.where(lt, even, odd), jnp.where(lt, odd, nxt))
        for dx in range(3):
            r = base + 64 * (3 * dy + dx)
            out[r : r + 64] = dup(taps[dx])


def near_rows(side, xp):
    first, last = max(0, 2 * xp - 1) // 8, min(side - 1, 2 * xp + 2) // 8
    shape = (8, 128)
    parity = jnp.where(low_half(shape), 0, 1)
    rows = lax.broadcasted_iota(jnp.int32, shape, 0)
    return {b: rows + (8 * b + 1 - 2 * xp) - parity for b in range(first, last + 1)}


def stem_band(stem, side, xp):
    near = near_rows(side, xp)
    zero = jnp.zeros((8, 128), F32)
    blocks = []
    for dy in range(3):
        for c in range(3):
            s = [stem[12 * dx + 4 * dy + c : 12 * dx + 4 * dy + c + 1] for dx in range(3)]
            for b in range(side // 8):
                if b not in near:
                    blocks.append(zero)
                    continue
                d = near[b]
                blocks.append(
                    jnp.where(d == 0, s[0], jnp.where(d == 1, s[1], jnp.where(d == 2, s[2], 0.0)))
                )
    return jnp.concatenate(blocks, axis=0)


def stem_rows(img, top, bottom):
    return jnp.concatenate(
        [down(img, top)[:, 0:96], img[:, 0:96], up(img, bottom)[:, 0:96]], axis=1
    )


def image_mark(img, images, at):
    row = img.reshape(images, img.shape[0] // images, 128)[:, 0, :]
    lane = lax.broadcasted_iota(jnp.int32, (images, 128), 1)
    return jnp.sum(jnp.where(lane == at, row, 0.0), axis=1, keepdims=True)


def label_onehot(img, images, classes):
    lab = image_mark(img, images, 96)
    lane = lax.broadcasted_iota(jnp.int32, (images, 128), 1)
    return jnp.where((lane.astype(F32) == lab) & (lane < classes), 1.0, 0.0)


def tree(xs):
    xs = list(xs)
    while len(xs) > 1:
        xs = [xs[k] + xs[k + 1] if k + 1 < len(xs) else xs[k] for k in range(0, len(xs), 2)]
    return xs[0]


def combine(blocks, count):
    each = count / len(blocks)
    mean = tree(b[0:1] for b in blocks) / count
    m2 = tree(b[1:2] + each * jnp.square(b[0:1] / each - mean) for b in blocks)
    return mean, lax.rsqrt(m2 / count + BN_EPS)


def stack_rows(rows, n=8):
    rows = list(rows)
    return jnp.concatenate(rows + [jnp.zeros((n - len(rows), 128), F32)], axis=0)


def centred_sums(a, s, count):
    mean = s / count
    m2 = jnp.zeros((8, 128), F32)
    for xp in range(a.shape[0]):
        d = a[xp].astype(F32) - mean
        m2 = m2 + part(d * d)
    return dup(row_sum(m2))


def k_weights(convs, norms, head_t, w1, w2, t1, t2, nv, hp, hpt, hb, sq):
    for k, (out, back) in enumerate(((w1, t1), (w2, t2))):
        for dy in range(3):
            taps = [both(convs[k, 3 * dy + dx]) for dx in range(3)]
            turned = [both(jnp.transpose(convs[k, 8 - 3 * dy - dx])) for dx in range(3)]
            for src, dst, n in ((taps, out, 3), (turned, back, 2)):
                for i, p in enumerate(split(pair_form(*src), n)):
                    dst[:, 384 * i + 128 * dy : 384 * i + 128 * dy + 128] = p
    nv[...] = stack_rows([both(norms[k // 2, k % 2 : k % 2 + 1]) for k in range(6)])
    classes, depth = head_t.shape
    sq[...] = jnp.zeros(sq.shape, F32)
    sq[0:classes, 0:depth] = head_t[...]
    sqv = sq[...]
    turned = jnp.transpose(sqv)
    row = lax.broadcasted_iota(jnp.int32, turned.shape, 0)
    hp[...] = jnp.where(row < depth - 1, turned, 0.0)
    hb[...] = stack_rows([turned[depth - 1 : depth]])
    hpt[...] = dup(jnp.where(low_half(sqv.shape), sqv, 0.0))


def both(w):
    return jnp.concatenate([w, w], axis=1)


def pack_image(img, n, marks):
    side = img.shape[2]
    lane = lax.broadcasted_iota(jnp.int32, (side, 32), 1)
    tail = jnp.zeros((side, 32), F32)
    for k, m in enumerate(marks):
        tail = jnp.where(lane == k, m.astype(F32), tail)
    return jnp.concatenate([img[n, 0], img[n, 1], img[n, 2], tail], axis=1)


def k_first(n, side, classes, *refs):
    labels, flips, ids, clip, vlabels, raw, vraw, stem, a0, st, img, s40, vpack = refs
    for i in range(raw.shape[0]):
        lab = jnp.where(flips[i] == 1, ids[i], labels[i])
        img[side * i : side * i + side] = pack_image(raw, i, [lab, clip[i]])
    for i in range(vraw.shape[0]):
        vpack[side * i : side * i + side] = pack_image(vraw, i, [vlabels[i]])
    s40[...] = jnp.zeros(s40.shape, F32)
    for dy in range(3):
        for dx in range(3):
            r = 12 * dx + 4 * dy
            s40[r : r + 3] = both(stem[dy, dx])
    stem_conv(n, side, img, s40[...], a0, st)
    counts = row_sum(label_onehot(img[...], raw.shape[0], classes))
    st[2:3] = counts


def k_val_stem(side, each, s40, *refs):
    blocks, (a0, st, img) = refs[:-3], refs[-3:]
    for k, b in enumerate(blocks):
        img[each * k : each * k + each] = b[8 : 8 + each]
    stem_conv(1, side, img, s40[...], a0, st)


def stem_conv(n, side, img, stem, a0, st):
    rows = img.shape[0]
    pairs = a0.shape[0]
    top, bottom = edges(rows, side)
    parts = split(stem_rows(img[...], top, bottom), n)
    lhs = jnp.concatenate([parts[i] for i, _ in TERMS[n]], axis=1)
    s = jnp.zeros((8, 128), F32)
    for xp in range(0, pairs, 2):
        band = jnp.concatenate([stem_band(stem, side, xp), stem_band(stem, side, xp + 1)], axis=1)
        rhs = split(band, n)
        z = mxu(lhs, jnp.concatenate([rhs[j] for _, j in TERMS[n]], axis=0))
        a0[xp] = z[:, 0:128].astype(a0.dtype)
        a0[xp + 1] = z[:, 128:256].astype(a0.dtype)
        s = s + part(z[:, 0:128]) + part(z[:, 128:256])
    s = dup(row_sum(s))
    m2 = centred_sums(a0, s, rows * pairs * 2)
    st[...] = stack_rows([s, m2])


SHARDS, CONV_ROWS, SMALL_ROWS = 8, 72, 16
SHARD_ROWS = CONV_ROWS + SMALL_ROWS
NORM_AT = SHARDS * SHARD_ROWS
PACKED = (NORM_AT + 8, 128)


def pack_params(stem_of, convs, norm_of, head_of, out, sq, small):
    out[NORM_AT : NORM_AT + 8] = jnp.zeros((8, 128), F32)
    for k in range(3):
        out[NORM_AT + 2 * k : NORM_AT + 2 * k + 2, 0:64] = norm_of(k)
    sq[...] = jnp.zeros(sq.shape, F32)
    head_t = head_of()
    sq[64 : 64 + head_t.shape[0], 0 : head_t.shape[1]] = head_t
    small[...] = jnp.transpose(sq[...])
    for dx in range(3):
        for dy in range(3):
            r = 12 * dx + 4 * dy
            small[r : r + 3, 0:64] = stem_of(dy, dx)
    for s in range(SHARDS):
        at = SHARD_ROWS * s
        for t in range(9):
            out[at + 8 * t : at + 8 * t + 8] = jnp.concatenate(
                [convs[0, t, 8 * s : 8 * s + 8], convs[1, t, 8 * s : 8 * s + 8]], axis=1
            )
        out[at + CONV_ROWS : at + SHARD_ROWS] = small[SMALL_ROWS * s : SMALL_ROWS * s + SMALL_ROWS]


def k_params(*refs):
    ins, outs, sq, small = refs[:16], refs[16:20], refs[20], refs[21]
    for k in range(4):
        stem, convs, norms, head = ins[4 * k : 4 * k + 4]
        own = k in (1, 2)
        pack_params(
            (lambda dy, dx, r=stem: r[dy, dx, :, 0, :]) if own else (lambda dy, dx, r=stem: r[dy, dx]),
            convs,
            lambda i, r=norms: r[i],
            (lambda r=head: r[:, 0, :]) if own else (lambda r=head: r[...]),
            outs[k],
            sq,
            small,
        )


def k_halves(even, got, *outs):
    for k, out in enumerate(outs):
        out[...] = even[k] + got[k]


def adam(q, p, m, v):
    first = 0.9 * m + 0.1 * q
    second = 0.999 * v + 0.001 * q * q
    step = first / (1.0 - 0.9**STEP) / (jnp.sqrt(second / (1.0 - 0.999**STEP)) + 1e-08) + 0.01 * p
    return first, second, 0.05 * step


def k_adam(count, nb, me, *refs):
    parts, refs = refs[:4], refs[4:]
    stat, refs = refs[:nb], refs[nb:]
    pp, pm, pv, vec0, grad, delta, rest, px, ps = refs
    total = tree([r[...] for r in parts])
    r8 = total[SHARD_ROWS : SHARD_ROWS + 8]
    rest[...] = r8
    st = tree([r[...] for r in stat])
    px[...] = jnp.zeros(px.shape, F32)
    ps[...] = jnp.zeros(ps.shape, F32)
    px[0:40] = st[8:48]
    ps[0:40] = st[48:88]
    at = pl.ds(pl.multiple_of(SMALL_ROWS * me[0], 8), SMALL_ROWS)
    gain = vec0[2:3] * vec0[1:2]
    sm = total[CONV_ROWS:SHARD_ROWS]
    fixed = gain * (sm - ps[at] * (r8[0:1] / count) - px[at] * (r8[1:2] / count))
    sm = jnp.where(low_half(sm.shape), fixed, sm)
    q = jnp.concatenate([total[0:CONV_ROWS], sm], axis=0)
    qn = stack_rows([r8[k : k + 1] for k in (1, 0, 3, 2, 5, 4)])
    grad[0:SHARD_ROWS] = q
    grad[SHARD_ROWS : SHARD_ROWS + 8] = qn
    at = pl.ds(pl.multiple_of(SHARD_ROWS * me[0], 8), SHARD_ROWS)
    delta[0:SHARD_ROWS] = adam(q, pp[at], pm[at], pv[at])[2]
    at = slice(NORM_AT, NORM_AT + 8)
    delta[SHARD_ROWS : SHARD_ROWS + 8] = adam(qn, pp[at], pm[at], pv[at])[2]


def k_total(ng, grad, *refs):
    deltas, (pay, norm) = refs[:ng], refs[ng:]
    total = tree([d[...] for d in deltas])
    pay[0:SHARD_ROWS] = grad[0:SHARD_ROWS]
    pay[SHARD_ROWS : 2 * SHARD_ROWS] = total[0:SHARD_ROWS]
    norm[0:8] = grad[SHARD_ROWS : SHARD_ROWS + 8]
    norm[8:16] = total[SHARD_ROWS : SHARD_ROWS + 8]


def k_update(groups, classes, me, *refs):
    pays, (norm, rest, pp, pm, pv, mom), refs = refs[:8], refs[8:14], refs[14:]
    news, lows, firsts, seconds, outers, loss = (
        refs[0:4],
        refs[4:8],
        refs[8:12],
        refs[12:16],
        refs[16:20],
        refs[20],
    )
    grad, delta = refs[21:]
    for j, pay in enumerate(pays):
        s = jnp.bitwise_xor(me[0], j)
        at = pl.ds(pl.multiple_of(SHARD_ROWS * s, 8), SHARD_ROWS)
        grad[at] = pay[0:SHARD_ROWS]
        delta[at] = pay[SHARD_ROWS : 2 * SHARD_ROWS]
    grad[NORM_AT : NORM_AT + 8] = norm[0:8]
    delta[NORM_AT : NORM_AT + 8] = norm[8:16]
    p = pp[...]
    first, second, _ = adam(grad[...], p, pm[...], pv[...])
    average = delta[...] / groups
    outer = 0.9 * mom[...] + average
    new = p - 0.7 * (average + 0.9 * outer)
    unpack(new, news, False)
    unpack(new, lows, False)
    unpack(outer, outers, False)
    unpack(first, firsts, True)
    unpack(second, seconds, True)
    loss[...] = rest[6, 0:1]


def unpack(x, outs, own):
    stem, convs, norms, head = outs
    dt = convs.dtype
    smalls = []
    for s in range(SHARDS):
        at = SHARD_ROWS * s
        for t in range(9):
            blk = x[at + 8 * t : at + 8 * t + 8].astype(dt)
            convs[0, t, 8 * s : 8 * s + 8] = blk[:, 0:64]
            convs[1, t, 8 * s : 8 * s + 8] = blk[:, 64:128]
        smalls.append(x[at + CONV_ROWS : at + SHARD_ROWS])
    small = jnp.concatenate(smalls, axis=0)
    turned = jnp.transpose(small)
    classes, depth = head.shape[0], head.shape[-1]
    head_t = turned[64 : 64 + classes, 0:depth].astype(dt)
    if own:
        for k in range(classes):
            head[k] = head_t[k : k + 1]
    else:
        head[...] = head_t
    for dy in range(3):
        for dx in range(3):
            r = 12 * dx + 4 * dy
            if own:
                for c in range(3):
                    stem[dy, dx, c] = small[r + c : r + c + 1, 0:64].astype(dt)
            else:
                stem[dy, dx] = small[r : r + 3, 0:64].astype(dt)
    for k in range(3):
        norms[k] = x[NORM_AT + 2 * k : NORM_AT + 2 * k + 2, 0:64].astype(dt)


def k_conv(n, side, nb, layer, count, carried, *refs):
    a_in, nv = refs[0], refs[1]
    blocks, w = refs[2 : 2 + nb], refs[2 + nb]
    refs = refs[3 + nb :]
    riders, refs = refs[:carried], refs[carried:]
    a_out, st, vec = refs[:3]
    wides = refs[3:]
    for rider in riders:
        st[8:] = rider[...]
    pairs, rows = a_in.shape[0], a_in.shape[1]
    top, bottom = edges(rows, side)
    bl = [b[0:8] for b in blocks]
    mean, r = combine(bl, count)
    gain, bias = nv[2 * layer : 2 * layer + 1], nv[2 * layer + 1 : 2 * layer + 2]
    counts = tree(b[2:3] for b in bl)
    scale = gain * r
    vec[...] = stack_rows([mean, r, gain, bias, counts, scale])
    for wide in wides:
        zero_ends(wide)

    def prep(xp):
        h = jnp.maximum((a_in[xp].astype(F32) - mean) * scale + bias, 0.0)
        put(wides, xp, split(h, n))

    prep(0)
    s = jnp.zeros((8, 128), F32)
    for xp in range(pairs):
        if xp + 1 < pairs:
            prep(xp + 1)
        out = conv_block([wide[xp] for wide in wides], w, top, bottom)
        a_out[xp] = out.astype(a_out.dtype)
        s = s + part(out)
    s = dup(row_sum(s))
    m2 = centred_sums(a_out, s, rows * pairs * 2)
    st[0:8] = stack_rows([s, m2])


def bn(a, vec):
    d = a.astype(F32) - vec[0:1]
    return d * vec[1:2], d * vec[5:6] + vec[3:4]


def k_head(val, side, nb, count, classes, group_count, *refs):
    a2, a0, vec0r, nv, img, hp, hpt, hb = refs[:8]
    blocks = refs[8 : 8 + nb]
    mz, vec2r, info, extra = refs[8 + nb :]
    pairs, rows = a2.shape[0], a2.shape[1]
    images = rows // side
    mean, r = combine([b[0:8] for b in blocks], count)
    zero = jnp.zeros((1, 128), F32)
    vec2 = stack_rows([mean, r, nv[4:5], nv[5:6], zero, nv[4:5] * r])
    vec2r[...] = vec2
    vec0 = vec0r[...]
    zs = jnp.zeros((images, 8, 128), F32)
    ms = jnp.zeros((images, 8, 128), F32)
    xs = jnp.zeros((images, 8, 128), F32)
    for xp in range(pairs):
        xh2, y2 = bn(a2[xp], vec2)
        z = y2 + jnp.maximum(bn(a0[xp], vec0)[1], 0.0)
        on = z > 0
        m = jnp.where(on, 1.0, 0.0)
        mz[xp] = m.astype(BF16)
        zs = zs + image_part(jnp.maximum(z, 0.0), images)
        ms = ms + image_part(m, images)
        xs = xs + image_part(jnp.where(on, xh2, 0.0), images)
    zs, ms, xs = (jnp.sum(v, axis=1) for v in (zs, ms, xs))
    area = side * pairs * 2
    lt = low_half((images, 128))
    pooled, ms, xs = dup(zs) / area, dup(ms), dup(xs)
    logits = lax.dot(pooled, hp[...], precision=HIGH) + hb[0:1]
    lane = lax.broadcasted_iota(jnp.int32, (images, 128), 1)
    ok = lane < classes
    top = jnp.max(jnp.where(ok, logits, -3e38), axis=1, keepdims=True)
    e = jnp.where(ok, jnp.exp(jnp.where(ok, logits - top, 0.0)), 0.0)
    tot = jnp.sum(e, axis=1, keepdims=True)
    onehot = label_onehot(img[...], images, classes)
    pm = e / tot - onehot
    ce = jnp.log(tot) + top - jnp.sum(onehot * logits, axis=1, keepdims=True)
    g = lax.dot(pm, hpt[...], precision=HIGH)
    if val:
        n_val = group_count
        gp = g / (n_val * area)
        info[...] = gp
        head = lax.dot_general(
            pooled, pm / n_val, (((0,), (0,)), ((), ())), precision=HIGH
        )
        extra[0:64] = head[0:64]
        extra[64:72] = stack_rows([row_sum(pm) / n_val])
        extra[72:80] = stack_rows([row_sum(gp * ms), row_sum(gp * xs)])
    else:
        cw = group_count / (classes * (vec0[4:5] + 1.0))
        per = jnp.sum(onehot * cw, axis=1, keepdims=True)
        uw = jnp.where(lt, g * ms, g * xs)
        pc = jnp.where(lane == 0, per, jnp.where(lane == 1, image_mark(img[...], images, 97), 0.0))
        extra[0:images] = uw
        extra[images : 2 * images] = pc
        for k, v in enumerate((g, ms, xs, pooled, pm, jnp.broadcast_to(ce, (images, 128)))):
            info[k] = v


def k_static(side, img, a0, vec0r, out):
    pairs, rows = a0.shape[0], a0.shape[1]
    top, bottom = edges(rows, side)
    vec0 = vec0r[...]
    whole = stem_rows(img[...], top, bottom)
    lhs = turned_rows(split(whole, 2))
    out[0:40] = stem_grad(
        side, pairs, lhs, lambda xp: split((a0[xp] - vec0[0:1]) * vec0[1:2], 2)
    )[0]
    out[40:80] = patch_sums(side, whole)


def turned_rows(parts):
    return [jnp.transpose(p) for p in parts]


def stem_grad(side, pairs, lhs, *rhs_of):
    n = len(lhs)
    count = len(rhs_of)
    accs = [{} for _ in rhs_of]
    width = 128 * count
    for xp in range(pairs):
        parts = [f(xp) for f in rhs_of]
        rhs = [jnp.concatenate([p[i] for p in parts], axis=1) for i in range(n)]
        f = None
        for i, j in TERMS[n]:
            t = mxu(lhs[i], rhs[j])
            f = t if f is None else f + t
        near = near_rows(side, xp)
        for q in range(count):
            for k in range(9):
                for b, d in near.items():
                    blk = f[side * k + 8 * b : side * k + 8 * b + 8, 128 * q : 128 * q + 128]
                    for dx in range(3):
                        v = jnp.where(d == dx, blk, 0.0)
                        key = (dx, k)
                        accs[q][key] = accs[q][key] + v if key in accs[q] else v
    outs = []
    zero = jnp.zeros((1, 128), F32)
    for acc in accs:
        rows = []
        for dx in range(3):
            for dy in range(3):
                rows += [dup(row_sum(acc[dx, 3 * dy + c])) for c in range(3)] + [zero]
        outs.append(jnp.concatenate(rows + [zero] * 4, axis=0))
    return outs


def patch_sums(side, whole):
    sums = row_sum(whole)
    col = jnp.transpose(jnp.broadcast_to(sums, (8, sums.shape[1])))[:, 0:1]
    xin = lax.rem(lax.broadcasted_iota(jnp.int32, col.shape, 0), side)
    rows = []
    for dx in range(3):
        keep = xin <= side - 2 if dx == 0 else (xin >= 1 if dx == 2 else xin >= 0)
        c = jnp.where(keep, col, 0.0)
        for k in range(12):
            if k % 4 == 3:
                rows.append(jnp.zeros((1, 128), F32))
                continue
            r = side * (3 * (k // 4) + k % 4)
            rows.append(jnp.broadcast_to(row_sum(c[r : r + side]), (1, 128)))
    return jnp.concatenate(rows + [jnp.zeros((4, 128), F32)], axis=0)


def back_of_norm2(gp, vec2, s1, s2, count, side, a2, mz):
    images, rows = gp.shape[0], a2.shape[1]
    k2 = vec2[2:3] * vec2[1:2]
    c0, c1 = k2 * s1 / count, k2 * s2 / count
    gk = jnp.broadcast_to((gp * k2)[:, None, :], (images, side, 128)).reshape(rows, 128)

    c1 = c1 * vec2[1:2]
    c0 = c0 - vec2[0:1] * c1

    def at(xp):
        return mz[xp].astype(F32) * gk - (a2[xp].astype(F32) * c1 + c0)

    return at


def back_of_norm1(vec1, s1, s2, count, dy1, a1):
    k1 = vec1[2:3] * vec1[1:2]
    c0, c1 = k1 * s1 / count, k1 * s2 / count

    c1 = c1 * vec1[1:2]
    c0 = c0 - vec1[0:1] * c1

    def at(xp):
        return dy1[xp].astype(F32) * k1 - (a1[xp].astype(F32) * c1 + c0)

    return at


def back_conv2(n, side, gp, vec2, s1, s2, count, a2, mz, a1, vec1, wt, wides, dy1, extra):
    pairs, rows = a2.shape[0], a2.shape[1]
    images = rows // side
    top, bottom = edges(rows, side)
    for wide in wides:
        zero_ends(wide)
    back_at = back_of_norm2(gp, vec2, s1, s2, count, side, a2, mz)

    def prep(xp):
        back = back_at(xp)
        parts = split(back, n)
        put(wides, xp, parts)
        if extra is not None:
            extra(xp, back, parts)

    prep(0)
    q1 = jnp.zeros((8, 128), F32)
    q2 = jnp.zeros((8, 128), F32)
    for xp in range(pairs):
        if xp + 1 < pairs:
            prep(xp + 1)
        dh = conv_block([wide[xp] for wide in wides], wt, top, bottom)
        xh1, y1 = bn(a1[xp], vec1)
        dy = jnp.where(y1 > 0, dh, 0.0)
        dy1[xp] = dy.astype(dy1.dtype)
        q1 = q1 + part(dy)
        q2 = q2 + part(dy * xh1)
    return dup(row_sum(q1)), dup(row_sum(q2))


def shifted(back, top, bottom):
    return jnp.concatenate([up(back, bottom), back, down(back, top)], axis=1)


def k_val_back2(side, nb, count, *refs):
    a2, mz, a1, vec2r, vec1r, gp, wt, wide1 = refs[:8]
    blocks = refs[8 : 8 + nb]
    dy1, st, g2 = refs[8 + nb : 11 + nb]
    wide, acc = refs[11 + nb :]
    wides = (wide,)
    rows = a2.shape[1]
    top, bottom = edges(rows, side)
    s1 = tree(b[72:73] for b in blocks)
    s2 = tree(b[73:74] for b in blocks)
    acc[...] = jnp.zeros(acc.shape, F32)

    def extra(xp, back, parts):
        acc[...] += mxu_t(shifted(back, top, bottom).astype(BF16), wide1[xp])

    q1, q2 = back_conv2(
        1, side, gp[...], vec2r[...], s1, s2, count, a2, mz, a1, vec1r[...], wt, wides, dy1, extra
    )
    fold_pair(jnp.transpose(acc[...]), g2)
    st[...] = stack_rows([q1, q2, s1, s2])


def back_conv1(n, side, gp, vec1, vec0, s1, s2, count, dy1, a1, a0, mz, wt, wides, dy0, extra):
    pairs, rows = a1.shape[0], a1.shape[1]
    images = rows // side
    top, bottom = edges(rows, side)
    for wide in wides:
        zero_ends(wide)
    back_at = back_of_norm1(vec1, s1, s2, count, dy1, a1)
    gpr = jnp.broadcast_to(gp[:, None, :], (images, side, 128)).reshape(rows, 128)

    def prep(xp):
        back = back_at(xp)
        parts = split(back, n)
        put(wides, xp, parts)
        if extra is not None:
            extra(xp, back, parts)

    prep(0)
    q1 = jnp.zeros((8, 128), F32)
    q2 = jnp.zeros((8, 128), F32)
    for xp in range(pairs):
        if xp + 1 < pairs:
            prep(xp + 1)
        dh = conv_block([wide[xp] for wide in wides], wt, top, bottom)
        xh0, y0 = bn(a0[xp], vec0)
        dy = jnp.where(y0 > 0, dh + mz[xp].astype(F32) * gpr, 0.0)
        dy0[xp] = dy.astype(dy0.dtype)
        q1 = q1 + part(dy)
        q2 = q2 + part(dy * xh0)
    return dup(row_sum(q1)), dup(row_sum(q2))


def k_val_back1(side, nb, count, *refs):
    dy1, a1, a0, mz, vec1r, vec0r, gp, wt, wide0, img = refs[:10]
    blocks = refs[10 : 10 + nb]
    g1, small = refs[10 + nb : 12 + nb]
    wide, acc, dy0 = refs[12 + nb :]
    wides = (wide,)
    pairs, rows = a1.shape[0], a1.shape[1]
    top, bottom = edges(rows, side)
    s1 = tree(b[0:1] for b in blocks)
    s2 = tree(b[1:2] for b in blocks)
    acc[...] = jnp.zeros(acc.shape, F32)
    vec0 = vec0r[...]

    def extra(xp, back, parts):
        acc[...] += mxu_t(shifted(back, top, bottom).astype(BF16), wide0[xp])

    q1, q2 = back_conv1(
        1, side, gp[...], vec1r[...], vec0, s1, s2, count, dy1, a1, a0, mz, wt, wides, dy0, extra
    )
    fold_pair(jnp.transpose(acc[...]), g1)
    whole = stem_rows(img[...], top, bottom)
    small[0:40], small[40:80] = stem_grad(
        side,
        pairs,
        turned_rows([whole.astype(BF16)]),
        lambda xp: [dy0[xp]],
        lambda xp: [((a0[xp].astype(F32) - vec0[0:1]) * vec0[1:2]).astype(BF16)],
    )
    small[80:120] = patch_sums(side, whole)
    small[120:128] = stack_rows([q1, q2])


def k_tan1(side, nb, nv_blocks, count, count_val, *refs):
    img, a0, a1, vec0r, vec1r, w1, vvec0r = refs[:7]
    refs = refs[7:]
    stat = refs[:nb]
    refs = refs[nb:]
    smalls, g1s, sts = refs[:nv_blocks], refs[nv_blocks : 2 * nv_blocks], refs[2 * nv_blocks : 3 * nv_blocks]
    t1, th0, st, wide, wide0, v1 = refs[3 * nv_blocks :]
    pairs, rows = a1.shape[0], a1.shape[1]
    top, bottom = edges(rows, side)
    vec0, vec1, vv0 = vec0r[...], vec1r[...], vvec0r[...]
    small = sum(b[...] for b in smalls)
    q1, q2 = small[120:121], small[121:122]
    v0 = (
        vv0[2:3]
        * vv0[1:2]
        * (small[0:40] - small[80:120] * (q1 / count_val) - small[40:80] * (q2 / count_val))
    )
    static = tree(b[...] for b in stat)
    u1 = row_sum(v0 * static[48:88])
    u2 = row_sum(v0 * static[8:48])
    k0 = vec0[2:3] * vec0[1:2]
    e0 = q1 - k0 * u1 / count
    e1 = q2 - k0 * u2 / count
    for dy in range(3):
        taps = []
        for dx in range(3):
            r = 64 * (3 * dy + dx)
            taps.append(sum(g[r : r + 64] for g in g1s))
        v1[:, 128 * dy : 128 * dy + 128] = pair_form(*taps).astype(BF16)
    zero_ends(wide)
    zero_ends(wide0)
    lhs = stem_rows(img[...], top, bottom).astype(BF16)
    tang = {}

    def prep(xp):
        if xp % 2 == 0:
            band = jnp.concatenate(
                [stem_band(v0, side, xp), stem_band(v0, side, xp + 1)], axis=1
            ).astype(BF16)
            z = mxu(lhs, band)
            tang[xp], tang[xp + 1] = z[:, 0:128], z[:, 128:256]
        xh0, y0 = bn(a0[xp], vec0)
        th = jnp.where(y0 > 0, k0 * tang.pop(xp) + e1 * xh0 + e0, 0.0).astype(BF16)
        th0[xp] = th
        put((wide, wide0), xp, [th, jnp.maximum(y0, 0.0).astype(BF16)])

    prep(0)
    p1 = jnp.zeros((8, 128), F32)
    p2 = jnp.zeros((8, 128), F32)
    for xp in range(pairs):
        if xp + 1 < pairs:
            prep(xp + 1)
        t = row_taps(mxu(wide[xp], w1[:, 0:384]) + mxu(wide0[xp], v1[...]), top, bottom)
        t1[xp] = t
        xh1 = (a1[xp] - vec1[0:1]) * vec1[1:2]
        p1 = p1 + part(t)
        p2 = p2 + part(t * xh1)
    vs = [sum(b[k : k + 1] for b in sts) for k in range(2)]
    st[...] = stack_rows([dup(row_sum(p1)), dup(row_sum(p2)), vs[0], vs[1], sts[0][2:3], sts[0][3:4]])


def k_tan2(side, nb, nv_blocks, count, *refs):
    t1, th0, a1, a2, mz, vec1r, vec2r, w2, info, own, gather = refs[:11]
    refs = refs[11:]
    blocks = refs[:nb]
    refs = refs[nb:]
    g2s, heads = refs[:nv_blocks], refs[nv_blocks : 2 * nv_blocks]
    st, wide, wide1, v2 = refs[2 * nv_blocks :]
    pairs, rows = a1.shape[0], a1.shape[1]
    images = rows // side
    top, bottom = edges(rows, side)
    vec1, vec2 = vec1r[...], vec2r[...]
    u1 = tree(b[0:1] for b in blocks)
    u2 = tree(b[1:2] for b in blocks)
    k1 = vec1[2:3] * vec1[1:2]
    e0 = own[2:3] - k1 * u1 / count
    e1 = own[3:4] - k1 * u2 / count
    for dy in range(3):
        taps = []
        for dx in range(3):
            r = 64 * (3 * dy + dx)
            taps.append(sum(g[r : r + 64] for g in g2s))
        v2[:, 128 * dy : 128 * dy + 128] = pair_form(*taps).astype(BF16)
    zero_ends(wide)
    zero_ends(wide1)

    def prep(xp):
        xh1, y1 = bn(a1[xp], vec1)
        th = jnp.where(y1 > 0, k1 * t1[xp] + e1 * xh1 + e0, 0.0).astype(BF16)
        put((wide, wide1), xp, [th, jnp.maximum(y1, 0.0).astype(BF16)])

    prep(0)
    p1 = jnp.zeros((8, 128), F32)
    p2 = jnp.zeros((8, 128), F32)
    asum = jnp.zeros((images, 8, 128), F32)
    k2 = vec2[2:3] * vec2[1:2]
    for xp in range(pairs):
        if xp + 1 < pairs:
            prep(xp + 1)
        t = row_taps(mxu(wide[xp], w2[:, 0:384]) + mxu(wide1[xp], v2[...]), top, bottom)
        xh2 = (a2[xp] - vec2[0:1]) * vec2[1:2]
        p1 = p1 + part(t)
        p2 = p2 + part(t * xh2)
        m = mz[xp].astype(F32)
        asum = asum + image_part(m * (k2 * t + th0[xp].astype(F32)), images)
    asum = dup(jnp.sum(asum, axis=1))
    area = side * pairs * 2
    g, ms, xs, pooled, pm = (info[k] for k in range(5))
    inner = g * (asum + own[5:6] * xs + own[4:5] * ms)
    base = jnp.sum(jnp.where(low_half(inner.shape), inner, 0.0), axis=1, keepdims=True) / area
    vhead = sum(h[0:72] for h in heads)
    vh = jnp.concatenate([vhead[0:64], jnp.zeros((64, 128), F32)], axis=0)
    lin = lax.dot(pooled, vh, precision=HIGH) + vhead[64:65]
    base = base + jnp.sum(pm * lin, axis=1, keepdims=True)
    st[0:images] = jnp.broadcast_to(base, (images, 128))
    p1, p2 = dup(row_sum(p1)), dup(row_sum(p2))
    st[images : images + 8] = stack_rows([jnp.where(low_half(p1.shape), p1, p2)])
    st[images + 8 :] = gather[...]


def k_train_back2(side, nb, count, group_count, n, *refs):
    flag, a2, mz, a1, vec2r, vec1r, wt, info = refs[:8]
    refs = refs[8:]
    dyn = refs[:nb]
    dy1, st, wgp = refs[nb : nb + 3]
    wides = refs[nb + 3 :]
    pairs, rows = a2.shape[0], a2.shape[1]
    images = rows // side
    area = side * pairs * 2
    vec2 = vec2r[...]
    k2 = vec2[2:3] * vec2[1:2]
    each = dyn[0].shape[0]
    at = images + 8
    tsum = 0.0
    for b in range(nb):
        for j in range(each):
            tsum = tsum + dyn[b][j, images : images + 1]
    tt = tsum * k2 / (count * area)
    raws, pers = [], []
    total = jnp.zeros((1, 1), F32)
    mag = jnp.zeros((1, 1), F32)
    for b in range(nb):
        for j in range(each):
            uw = dyn[b][j, at : at + images]
            pc = dyn[b][j, at + images : at + 2 * images]
            per, clip = pc[:, 0:1], pc[:, 1:2]
            tan = dyn[b][j, 0:images, 0:1] - jnp.sum(uw * tt, axis=1, keepdims=True)
            score = -ALPHA * per * tan
            raw = clip * jnp.maximum(-score, 0.0)
            total = total + row_sum(raw)
            mag = mag + row_sum(clip * jnp.abs(score))
            raws.append(raw)
            pers.append(per)
    on = flag[0] == 1
    denom = jnp.maximum(total, 0.25 * mag) + 1e-06
    ssum = jnp.zeros((1, 128), F32)
    k = 0
    own = None
    for b in range(nb):
        for j in range(each):
            w = jnp.where(on, raws[k] / denom, 1.0 / group_count) * pers[k]
            own = w if own is None else own
            ssum = ssum + row_sum(w * dyn[b][j, at : at + images])
            k += 1
    ssum = ssum / area
    lt = low_half(ssum.shape)
    s1, s2 = dup(jnp.where(lt, ssum, 0.0)), dup(jnp.where(lt, 0.0, ssum))
    g, pooled, pm, ce = info[0], info[3], info[4], info[5]
    gp = own * g / area
    wgp[0:images] = gp
    head = lax.dot_general(pooled, own * pm, (((0,), (0,)), ((), ())), precision=HIGH)
    wgp[images : images + 64] = head[0:64]
    mine = row_sum(own * dyn[0][0, at : at + images]) / area
    o1, o2 = dup(jnp.where(lt, mine, 0.0)), dup(jnp.where(lt, 0.0, mine))
    wgp[images + 64 : images + 72] = stack_rows([row_sum(own * pm), row_sum(own * ce), o1, o2])

    wgp[images + 72 : images + 80] = stack_rows([s1, s2])
    q1, q2 = back_conv2(
        n, side, gp, vec2, s1, s2, count, a2, mz, a1, vec1r[...], wt, wides, dy1, None
    )
    st[...] = stack_rows([q1, q2])


def k_train_back1(side, nb, n, count, me, *refs):
    dy1, a1, a0, mz, vec1r, vec0r, wt, img, wgp, d2, st1 = refs[:11]
    blocks = refs[11 : 11 + nb]
    even, odd, acc, d1, small, dy0 = refs[11 + nb : 17 + nb]
    wides, inputs = refs[17 + nb : 17 + nb + n], refs[17 + nb + n :]
    pairs, rows = a1.shape[0], a1.shape[1]
    images = rows // side
    top, bottom = edges(rows, side)
    s1 = tree(b[0:1] for b in blocks)
    s2 = tree(b[1:2] for b in blocks)
    vec0 = vec0r[...]
    acc[...] = jnp.zeros(acc.shape, F32)
    for wide in inputs:
        zero_ends(wide)
    held = {}

    def gradient(xp):
        lhs = split(shifted(held.pop(xp), top, bottom), n)
        t = None
        for i, j in TERMS[n]:
            d = mxu_t(lhs[i], inputs[j][xp])
            t = d if t is None else t + d
        acc[...] += t

    def extra(xp, back, parts):
        put(inputs, xp, split(jnp.maximum(bn(a0[xp], vec0)[1], 0.0), n))
        held[xp] = back
        if xp > 0:
            gradient(xp - 1)

    q1, q2 = back_conv1(
        n, side, wgp[0:images], vec1r[...], vec0, s1, s2, count, dy1, a1, a0, mz, wt, wides, dy0, extra
    )
    gradient(pairs - 1)
    fold_pair(jnp.transpose(acc[...]), d1)
    lhs = turned_rows(split(stem_rows(img[...], top, bottom), n))
    stem = stem_grad(side, pairs, lhs, lambda xp: split(dy0[xp], n))[0]
    small[...] = jnp.zeros((128, 128), F32)
    small[0:65] = wgp[images : images + 65]
    right = pltpu.roll(small[...], 64, 1)
    small[...] = jnp.zeros((128, 128), F32)
    small[0:40] = stem
    small[...] = jnp.where(low_half((128, 128)), small[...], right)
    rest = stack_rows(
        [q1, q2, st1[0:1], st1[1:2]] + [wgp[images + k : images + k + 1] for k in (66, 67, 65)]
    )
    lt8 = low_half((8, 128))
    for j in range(SHARDS):
        s = jnp.bitwise_xor(me[0], j)
        dst = (even, odd)[j % 2]
        k = j // 2
        for t in range(9):
            at = pl.ds(pl.multiple_of(64 * t + 8 * s, 8), 8)
            dst[k, 8 * t : 8 * t + 8] = jnp.where(lt8, d1[at], d2[at])
        dst[k, CONV_ROWS:SHARD_ROWS] = small[pl.ds(pl.multiple_of(SMALL_ROWS * s, 8), SMALL_ROWS)]
        dst[k, SHARD_ROWS : SHARD_ROWS + 8] = rest


def weight_gradient(side, n, a, vec, back_at, wides, acc, g):
    pairs, rows = a.shape[0], a.shape[1]
    top, bottom = edges(rows, side)
    acc[...] = jnp.zeros(acc.shape, F32)
    for wide in wides:
        zero_ends(wide)

    def prep(xp):
        put(wides, xp, split(jnp.maximum(bn(a[xp], vec)[1], 0.0), n))

    prep(0)
    for xp in range(pairs):
        if xp + 1 < pairs:
            prep(xp + 1)
        lhs = split(shifted(back_at(xp), top, bottom), n)
        t = None
        for i, j in TERMS[n]:
            d = mxu_t(lhs[i], wides[j][xp])
            t = d if t is None else t + d
        acc[...] += t
    fold_pair(jnp.transpose(acc[...]), g)


def k_dw2(side, n, count, a1, vec1, a2, vec2, mz, wgp, g, acc, *wides):
    images = a1.shape[1] // side
    at = images + 72
    back_at = back_of_norm2(
        wgp[0:images], vec2[...], wgp[at : at + 1], wgp[at + 1 : at + 2], count, side, a2, mz
    )
    weight_gradient(side, n, a1, vec1[...], back_at, wides, acc, g)


VM = pl.BlockSpec(memory_space=pltpu.VMEM)
SM = pl.BlockSpec(memory_space=pltpu.SMEM)


def call(kernel, outs, args, scratch=(), smem=(), raw=(), us=1.0, after=()):
    count = len(args)

    def run(*refs):
        kernel(*refs[:count], *refs[count + len(after) :])

    def placed(i, x):
        if i in raw:
            return pltpu.with_memory_space_constraint(x, pltpu.HBM)
        return pltpu.with_memory_space_constraint(x, pltpu.VMEM) if x.size >= KEEP else x

    return pl.pallas_call(
        run,
        out_shape=[
            pltpu.VMEM(s, d) if math.prod(s) >= KEEP else jax.ShapeDtypeStruct(s, d)
            for s, d in outs
        ],
        in_specs=[SM if i in smem else VM for i in range(count)]
        + [pl.BlockSpec(memory_space=pl.ANY)] * len(after),
        out_specs=[VM] * len(outs),
        scratch_shapes=[pltpu.VMEM(s, d) for s, d in scratch],
        compiler_params=pltpu.CompilerParams(vmem_limit_bytes=VMEM_BYTES),
        cost_estimate=pl.CostEstimate(
            flops=int(us * 1.1e9), bytes_accessed=1 << 16, transcendentals=0
        ),
    )(*[placed(i, x) for i, x in enumerate(args)], *[placed(-1, x) for x in after])


def swap(x, k, n):
    return lax.ppermute(x, "dp", [(i, i ^ k) for i in range(n)])


def add(a, b, step):
    return a + b


def chan(count, a, b, step):
    d = a[0:1] - b[0:1]
    cross = d * d / (2.0 * count * step)
    return a + b + jnp.pad(cross, ((1, a.shape[0] - 2), (0, 0)))


def near(x, team, merge):
    n = lax.axis_size("dp")
    k = 1
    while k < team // 2:
        x = merge(x, swap(x, k, n), k)
        k *= 2
    return [x, swap(x, k, n)] if team > 1 else [x]


def far(x, merge, rider=None):
    n = lax.axis_size("dp")
    k = 1
    while k < n // 4:
        x = merge(x, swap(x, k, n), k)
        k *= 2
    if rider is not None:
        x = jnp.concatenate([x, rider], axis=0)
    return [x] + [swap(x, j * k, n) for j in range(1, n // k)]


def far_list(x):
    n = lax.axis_size("dp")
    x = x[None]
    k = 1
    while k < n // 4:
        x = jnp.concatenate([x, swap(x, k, n)], axis=0)
        k *= 2
    return [x] + [swap(x, j * k, n) for j in range(1, n // k)]


def body(
    train_images,
    train_labels,
    flip_flags,
    class_ids,
    clip_mask,
    norm_flag,
    val_images,
    val_labels,
    stem,
    convs,
    norms,
    head,
    m_stem,
    v_stem,
    m_convs,
    v_convs,
    m_norms,
    v_norms,
    m_head,
    v_head,
    mom_stem,
    mom_convs,
    mom_norms,
    mom_head,
):
    dp = lax.axis_size("dp")
    classes = head.shape[1]
    side, pairs = train_images.shape[1], train_images.shape[2] // 2
    images, val_each = train_images.shape[0], val_images.shape[0]
    group_train, group_val = dp * images, dp * val_each
    team = max(2, group_val // 16)
    rows, vrows = images * side, side * group_val // team
    vimages = group_val // team
    count, count_val = group_train * side * pairs * 2, group_val * side * pairs * 2
    nt, nval = 3, 1

    act = (pairs, rows, 128)
    st = ((8, 128), F32)
    square = ((128, 128), F32)

    def planes(img):
        return jnp.transpose(img, (0, 3, 1, 2))

    me = lax.rem(lax.axis_index("dp"), SHARDS).astype(jnp.int32).reshape(1)
    a0, s0, img, s40, vpack = call(
        functools.partial(k_first, nt, side, classes),
        [(act, F32), st, ((rows, 128), F32), ((40, 128), F32), ((val_each * side, 128), F32)],
        [train_labels, flip_flags, class_ids, clip_mask, val_labels]
        + [planes(train_images), planes(val_images), stem],
        smem=range(5),
        raw=range(8),
        us=4.5,
        after=[me],
    )
    b0 = far(s0, functools.partial(chan, rows * pairs * 2), vpack)
    forms = [((256, 384 * n), BF16) for n in (3, 3, 2, 2)]
    w1, w2, t1w, t2w, nv, hp, hpt, hb = call(
        k_weights,
        forms + [st, square, square, st],
        [convs.reshape(2, 9, 64, 64), norms, head.T],
        [square],
        raw=range(3),
        us=2.0,
    )
    moment_views = [
        (
            jnp.transpose(x[0], (1, 2, 3, 0, 4)),
            x[1].reshape(2, 9, 64, 64),
            x[2][0],
            jnp.transpose(x[3], (2, 0, 1)),
        )
        for x in ((m_stem, m_convs, m_norms, m_head), (v_stem, v_convs, v_norms, v_head))
    ]
    packed = call(
        k_params,
        [(PACKED, F32)] * 4,
        [stem, convs.reshape(2, 9, 64, 64), norms, head.T]
        + [x for views in moment_views for x in views]
        + [mom_stem, mom_convs.reshape(2, 9, 64, 64), mom_norms, mom_head.T],
        [square, square],
        raw=range(16),
        us=2.0,
    )

    act = (pairs, rows, 128)
    vact = (pairs, vrows, 128)

    def wide(r):
        return ((pairs, r, 256), BF16)

    va0, vs0, vimg = call(
        functools.partial(k_val_stem, side, val_each * side),
        [(vact, BF16), st, ((vrows, 128), F32)],
        [s40] + b0,
        us=2.4,
    )
    vchan = functools.partial(chan, vrows * pairs * 2)
    vb0 = near(vs0, team, vchan)

    def conv(n, layer, r, total, a, blocks, w, rider=(), after=()):
        pay = ((8 + sum(x.shape[0] for x in rider), 128), F32)
        return call(
            functools.partial(k_conv, n, side, len(blocks), layer, total, len(rider)),
            [((pairs, r, 128), F32 if n > 1 else BF16), pay, st] + [wide(r)] * (n == 1),
            [a, nv] + blocks + [w] + list(rider),
            [wide(r)] * n * (n > 1),
            us=6.7 if n > 1 else 3.3,
            after=after,
        )

    a1, s1, vec0 = conv(nt, 0, rows, count, a0, b0, w1)
    b1 = far(s1, functools.partial(chan, rows * pairs * 2))
    va1, vs1, vvec0, vwide0 = conv(nval, 0, vrows, count_val, va0, vb0, w1, after=[s1])
    vb1 = near(vs1, team, vchan)
    va2, vs2, vvec1, vwide1 = conv(nval, 1, vrows, count_val, va1, vb1, w2, after=b1[:1])
    vb2 = near(vs2, team, vchan)
    static = call(
        functools.partial(k_static, side), [((80, 128), F32)], [img, a0, vec0], us=2.0, after=b1[:1]
    )
    a2, s2, vec1 = conv(nt, 1, rows, count, a1, b1, w2, static)
    b2 = far(s2, functools.partial(chan, rows * pairs * 2))

    vmz, vvec2, vgp, vextra = call(
        functools.partial(k_head, True, side, len(vb2), count_val, classes, group_val),
        [(vact, BF16), st, ((vimages, 128), F32), ((80, 128), F32)],
        [va2, va0, vvec0, nv, vimg, hp, hpt, hb] + vb2,
        us=4.0,
        after=[s2],
    )
    vextras = near(vextra, team, add)
    vdy1, vst1, g2 = call(
        functools.partial(k_val_back2, side, len(vextras), count_val),
        [(vact, BF16), st, ((576, 128), F32)],
        [va2, vmz, va1, vvec2, vvec1, vgp, t2w, vwide1] + vextras,
        [wide(vrows), ((384, 256), F32)],
        us=6.0,
        after=b2[:1],
    )
    vst1s = near(vst1, team, add)
    g2s = near(g2, team, add)
    g1, small = call(
        functools.partial(k_val_back1, side, len(vst1s), count_val),
        [((576, 128), F32), ((128, 128), F32)],
        [vdy1, va1, va0, vmz, vvec1, vvec0, vgp, t1w, vwide0, vimg] + vst1s,
        [wide(vrows), ((384, 256), F32), (vact, BF16)],
        us=7.0,
        after=b2[1:],
    )
    smalls = near(small, team, add)
    g1s = near(g1, team, add)

    tan1, th0, ts1 = call(
        functools.partial(k_tan1, side, len(b2), len(g1s), count, count_val),
        [(act, F32), (act, BF16), st],
        [img, a0, a1, vec0, vec1, w1, vvec0] + b2 + smalls + g1s + vst1s,
        [wide(rows), wide(rows), ((256, 384), BF16)],
        us=4.0,
    )
    tb1 = far(ts1, add)
    mz, vec2, info, gather = call(
        functools.partial(k_head, False, side, len(b2), count, classes, group_train),
        [(act, BF16), st, ((6, images, 128), F32), ((2 * images, 128), F32)],
        [a2, a0, vec0, nv, img, hp, hpt, hb] + b2,
        us=2.2,
        after=[ts1],
    )
    (ts2,) = call(
        functools.partial(k_tan2, side, len(tb1), len(g2s), count),
        [((3 * images + 8, 128), F32)],
        [tan1, th0, a1, a2, mz, vec1, vec2, w2, info, ts1, gather] + tb1 + g2s + vextras,
        [wide(rows), wide(rows), ((256, 384), BF16)],
        us=4.0,
    )
    dyn = far_list(ts2)

    nb_ = 2
    dy1, bs1, wgp = call(
        functools.partial(k_train_back2, side, len(dyn), count, group_train, nb_),
        [(act, F32), st, ((images + 80, 128), F32)],
        [norm_flag, a2, mz, a1, vec2, vec1, t2w, info] + dyn,
        [wide(rows)] * nb_,
        smem=(0,),
        us=4.3,
    )
    bb1 = far(bs1, add)
    (d2,) = call(
        functools.partial(k_dw2, side, nb_, count),
        [((576, 128), F32)],
        [a1, vec1, a2, vec2, mz, wgp],
        [((384, 256), F32)] + [wide(rows)] * nb_,
        us=3.6,
    )
    piece = (SHARD_ROWS + 8, 128)
    even, odd = call(
        functools.partial(k_train_back1, side, len(bb1), nb_, count),
        [((4,) + piece, F32)] * 2,
        [me, dy1, a1, a0, mz, vec1, vec0, t1w, img, wgp, d2, bs1] + bb1,
        [((384, 256), F32), ((576, 128), F32), square, (act, F32)] + [wide(rows)] * (2 * nb_),
        smem=(0,),
        us=9.0,
    )

    k = SHARDS
    while k < dp:
        even, odd = even + swap(even, k, dp), odd + swap(odd, k, dp)
        k *= 2
    halves = call(k_halves, [(piece, F32)] * 4, [even, swap(odd, 1, dp)])
    parts = [halves[0]] + [swap(halves[k], 2 * k, dp) for k in range(1, 4)]
    grad, delta, rest = call(
        functools.partial(k_adam, count, len(b2)),
        [(piece, F32), (piece, F32), st],
        [me] + parts + b2 + list(packed[:3]) + [vec0],
        [square, square],
        smem=(0,),
    )
    groups = lax.axis_size("group")
    deltas = [delta] + [
        lax.ppermute(delta, "group", [(i, i ^ k) for i in range(groups)])
        for k in range(1, groups)
    ]
    pay, norm = call(
        functools.partial(k_total, groups),
        [((2 * SHARD_ROWS, 128), F32), ((16, 128), F32)],
        [grad] + deltas,
    )
    pays = []
    for k in range(4):
        x = swap(pay, 2 * k, dp) if k else pay
        pays += [x, swap(x, 1, dp)]
    p4 = [(3, 3, 3, 64), (2, 9, 64, 64), (3, 2, 64), (classes, head.shape[0])]
    g4 = [(3, 3, 3, 1, 64), (2, 9, 64, 64), (3, 2, 64), (classes, 1, head.shape[0])]
    outs = call(
        functools.partial(k_update, groups, classes),
        [(x, F32) for x in p4]
        + [(x, BF16) for x in p4]
        + [(x, F32) for x in g4 + g4 + p4]
        + [((1,), F32)],
        [me] + pays + [norm, rest] + list(packed),
        [(PACKED, F32)] * 2,
        smem=(0,),
    )

    def plain(stem, convs, norms, head):
        return [stem, convs.reshape(2, 3, 3, 64, 64), norms, head.T]

    def own(stem, convs, norms, head):
        return [
            jnp.transpose(stem, (3, 0, 1, 2, 4)),
            convs.reshape(1, 2, 3, 3, 64, 64),
            norms[None],
            jnp.transpose(head, (1, 2, 0)),
        ]

    return (
        *plain(*outs[0:4]),
        *plain(*outs[4:8]),
        *own(*outs[8:12]),
        *own(*outs[12:16]),
        *plain(*outs[16:20]),
        outs[20],
    )


def solution(mesh):
    split4 = P(("group", "dp"), None, None, None)
    split1 = P(("group", "dp"))
    group = P("group")
    whole = P()
    return jax.shard_map(
        body,
        mesh=mesh,
        in_specs=(split4, split1, split1, split1, split1, group, split4, split1)
        + (whole,) * 4
        + (group,) * 8
        + (whole,) * 4,
        out_specs=(whole,) * 8 + (group,) * 8 + (whole,) * 4 + (group,),
        check_vma=False,
    )
```

```python
import functools
import math

import jax
import jax.numpy as jnp
from jax import lax
from jax.experimental import pallas as pl
from jax.experimental.pallas import tpu as pltpu
from jax.sharding import PartitionSpec as P

STEP = 10
BN_EPS = 1e-05
ALPHA = 0.1
F32 = jnp.float32
BF16 = jnp.bfloat16
HIGH = lax.Precision.HIGHEST
VMEM_BYTES = 18 * 1024 * 1024
KEEP = 200000


TERMS = {
    1: ((0, 0),),
    2: ((1, 0), (0, 1), (0, 0)),
    3: ((2, 0), (1, 1), (0, 2), (1, 0), (0, 1), (0, 0)),
}


def mxu(a, b):
    return lax.dot_general(a, b, (((1,), (0,)), ((), ())), preferred_element_type=F32)


def mxu_t(a, b):
    return lax.dot_general(a, b, (((0,), (0,)), ((), ())), preferred_element_type=F32)


def split(x, n):
    parts = []
    for k in range(n):
        p = x.astype(BF16)
        parts.append(p)
        if k + 1 < n:
            x = x - p.astype(F32)
    return parts


def dup(v):
    return v + pltpu.roll(v, v.shape[-1] // 2, v.ndim - 1)


def low_half(shape):
    return lax.broadcasted_iota(jnp.int32, shape, len(shape) - 1) < shape[-1] // 2


def edges(rows, side):
    y = lax.rem(lax.broadcasted_iota(jnp.int32, (rows, 128), 0), side)
    return y == 0, y == side - 1


def down(x, top):
    return jnp.where(top, 0.0, pltpu.roll(x, 1, 0))


def up(x, bottom):
    return jnp.where(bottom, 0.0, pltpu.roll(x, x.shape[0] - 1, 0))


def row_sum(x):
    return jnp.sum(x, axis=0, keepdims=True)


def part(x):
    return jnp.sum(x.reshape(x.shape[0] // 8, 8, 128), axis=0)


def image_part(x, images):
    return jnp.sum(x.reshape(images, x.shape[0] // (8 * images), 8, 128), axis=1)


def zero_ends(wide):
    last, rows = wide.shape[0] - 1, wide.shape[1]
    wide[last, :, 128:192] = jnp.zeros((rows, 64), BF16)
    wide[0, :, 192:256] = jnp.zeros((rows, 64), BF16)


def put(wides, xp, parts):
    for wide, part in zip(wides, parts):
        wide[xp, :, 0:128] = part
        if xp > 0:
            wide[xp - 1, :, 128:192] = part[:, 0:64]
        if xp + 1 < wide.shape[0]:
            wide[xp + 1, :, 192:256] = part[:, 64:128]


def row_taps(z, top, bottom):
    return down(z[:, 0:128], top) + z[:, 128:256] + up(z[:, 256:384], bottom)


def conv_block(lhs, w, top, bottom):
    n = len(lhs)
    z = [mxu(x, w[:, 0 : 384 * (n - k)]) for k, x in enumerate(lhs)]
    total = None
    for rank in range(n - 1, -1, -1):
        for k in range(rank + 1):
            j = rank - k
            part = z[k][:, 384 * j : 384 * j + 384]
            total = part if total is None else total + part
    return row_taps(total, top, bottom)


def pair_form(t0, t1, t2):
    lt = low_half(t0.shape)
    return jnp.concatenate(
        [
            jnp.where(lt, t1, t0),
            jnp.where(lt, t2, t1),
            jnp.where(lt, 0.0, t2),
            jnp.where(lt, t0, 0.0),
        ],
        axis=0,
    )


def fold_pair(acc, out, base=0):
    for dy in range(3):
        b = acc[:, 128 * dy : 128 * dy + 128]
        even, odd, nxt, prv = b[0:64], b[64:128], b[128:192], b[192:256]
        lt = low_half(even.shape)
        taps = (jnp.where(lt, prv, even), jnp.where(lt, even, odd), jnp.where(lt, odd, nxt))
        for dx in range(3):
            r = base + 64 * (3 * dy + dx)
            out[r : r + 64] = dup(taps[dx])


def near_rows(side, xp):
    first, last = max(0, 2 * xp - 1) // 8, min(side - 1, 2 * xp + 2) // 8
    shape = (8, 128)
    parity = jnp.where(low_half(shape), 0, 1)
    rows = lax.broadcasted_iota(jnp.int32, shape, 0)
    return {b: rows + (8 * b + 1 - 2 * xp) - parity for b in range(first, last + 1)}


def stem_band(stem, side, xp):
    near = near_rows(side, xp)
    zero = jnp.zeros((8, 128), F32)
    blocks = []
    for dy in range(3):
        for c in range(3):
            s = [stem[12 * dx + 4 * dy + c : 12 * dx + 4 * dy + c + 1] for dx in range(3)]
            for b in range(side // 8):
                if b not in near:
                    blocks.append(zero)
                    continue
                d = near[b]
                blocks.append(
                    jnp.where(d == 0, s[0], jnp.where(d == 1, s[1], jnp.where(d == 2, s[2], 0.0)))
                )
    return jnp.concatenate(blocks, axis=0)


def stem_rows(img, top, bottom):
    return jnp.concatenate(
        [down(img, top)[:, 0:96], img[:, 0:96], up(img, bottom)[:, 0:96]], axis=1
    )


def image_mark(img, images, at):
    row = img.reshape(images, img.shape[0] // images, 128)[:, 0, :]
    lane = lax.broadcasted_iota(jnp.int32, (images, 128), 1)
    return jnp.sum(jnp.where(lane == at, row, 0.0), axis=1, keepdims=True)


def label_onehot(img, images, classes):
    lab = image_mark(img, images, 96)
    lane = lax.broadcasted_iota(jnp.int32, (images, 128), 1)
    return jnp.where((lane.astype(F32) == lab) & (lane < classes), 1.0, 0.0)


def tree(xs):
    xs = list(xs)
    while len(xs) > 1:
        xs = [xs[k] + xs[k + 1] if k + 1 < len(xs) else xs[k] for k in range(0, len(xs), 2)]
    return xs[0]


def combine(blocks, count):
    each = count / len(blocks)
    mean = tree(b[0:1] for b in blocks) / count
    m2 = tree(b[1:2] + each * jnp.square(b[0:1] / each - mean) for b in blocks)
    return mean, lax.rsqrt(m2 / count + BN_EPS)


def stack_rows(rows, n=8):
    rows = list(rows)
    return jnp.concatenate(rows + [jnp.zeros((n - len(rows), 128), F32)], axis=0)


def centred_sums(a, s, count):
    mean = s / count
    m2 = jnp.zeros((8, 128), F32)
    for xp in range(a.shape[0]):
        d = a[xp].astype(F32) - mean
        m2 = m2 + part(d * d)
    return dup(row_sum(m2))


def k_weights(convs, norms, head_t, w1, w2, t1, t2, nv, hp, hpt, hb, sq):
    for k, (out, back) in enumerate(((w1, t1), (w2, t2))):
        for dy in range(3):
            taps = [both(convs[k, 3 * dy + dx]) for dx in range(3)]
            turned = [both(jnp.transpose(convs[k, 8 - 3 * dy - dx])) for dx in range(3)]
            for src, dst, n in ((taps, out, 3), (turned, back, 2)):
                for i, p in enumerate(split(pair_form(*src), n)):
                    dst[:, 384 * i + 128 * dy : 384 * i + 128 * dy + 128] = p
    nv[...] = stack_rows([both(norms[k // 2, k % 2 : k % 2 + 1]) for k in range(6)])
    classes, depth = head_t.shape
    sq[...] = jnp.zeros(sq.shape, F32)
    sq[0:classes, 0:depth] = head_t[...]
    sqv = sq[...]
    turned = jnp.transpose(sqv)
    row = lax.broadcasted_iota(jnp.int32, turned.shape, 0)
    hp[...] = jnp.where(row < depth - 1, turned, 0.0)
    hb[...] = stack_rows([turned[depth - 1 : depth]])
    hpt[...] = dup(jnp.where(low_half(sqv.shape), sqv, 0.0))


def both(w):
    return jnp.concatenate([w, w], axis=1)


def pack_image(img, n, marks):
    side = img.shape[2]
    lane = lax.broadcasted_iota(jnp.int32, (side, 32), 1)
    tail = jnp.zeros((side, 32), F32)
    for k, m in enumerate(marks):
        tail = jnp.where(lane == k, m.astype(F32), tail)
    return jnp.concatenate([img[n, 0], img[n, 1], img[n, 2], tail], axis=1)


def k_first(n, side, classes, *refs):
    labels, flips, ids, clip, vlabels, raw, vraw, stem, a0, st, img, s40, vpack = refs
    for i in range(raw.shape[0]):
        lab = jnp.where(flips[i] == 1, ids[i], labels[i])
        img[side * i : side * i + side] = pack_image(raw, i, [lab, clip[i]])
    for i in range(vraw.shape[0]):
        vpack[side * i : side * i + side] = pack_image(vraw, i, [vlabels[i]])
    s40[...] = jnp.zeros(s40.shape, F32)
    for dy in range(3):
        for dx in range(3):
            r = 12 * dx + 4 * dy
            s40[r : r + 3] = both(stem[dy, dx])
    stem_conv(n, side, img, s40[...], a0, st)
    counts = row_sum(label_onehot(img[...], raw.shape[0], classes))
    st[2:3] = counts


def k_val_stem(side, each, s40, *refs):
    blocks, (a0, st, img) = refs[:-3], refs[-3:]
    for k, b in enumerate(blocks):
        img[each * k : each * k + each] = b[8 : 8 + each]
    stem_conv(1, side, img, s40[...], a0, st)


def stem_conv(n, side, img, stem, a0, st):
    rows = img.shape[0]
    pairs = a0.shape[0]
    top, bottom = edges(rows, side)
    parts = split(stem_rows(img[...], top, bottom), n)
    lhs = jnp.concatenate([parts[i] for i, _ in TERMS[n]], axis=1)
    s = jnp.zeros((8, 128), F32)
    for xp in range(0, pairs, 2):
        band = jnp.concatenate([stem_band(stem, side, xp), stem_band(stem, side, xp + 1)], axis=1)
        rhs = split(band, n)
        z = mxu(lhs, jnp.concatenate([rhs[j] for _, j in TERMS[n]], axis=0))
        a0[xp] = z[:, 0:128].astype(a0.dtype)
        a0[xp + 1] = z[:, 128:256].astype(a0.dtype)
        s = s + part(z[:, 0:128]) + part(z[:, 128:256])
    s = dup(row_sum(s))
    m2 = centred_sums(a0, s, rows * pairs * 2)
    st[...] = stack_rows([s, m2])


SHARDS, CONV_ROWS, SMALL_ROWS = 8, 72, 16
SHARD_ROWS = CONV_ROWS + SMALL_ROWS
NORM_AT = SHARDS * SHARD_ROWS
PACKED = (NORM_AT + 8, 128)


def pack_params(stem_of, convs, norm_of, head_of, out, sq, small):
    out[NORM_AT : NORM_AT + 8] = jnp.zeros((8, 128), F32)
    for k in range(3):
        out[NORM_AT + 2 * k : NORM_AT + 2 * k + 2, 0:64] = norm_of(k)
    sq[...] = jnp.zeros(sq.shape, F32)
    head_t = head_of()
    sq[64 : 64 + head_t.shape[0], 0 : head_t.shape[1]] = head_t
    small[...] = jnp.transpose(sq[...])
    for dx in range(3):
        for dy in range(3):
            r = 12 * dx + 4 * dy
            small[r : r + 3, 0:64] = stem_of(dy, dx)
    for s in range(SHARDS):
        at = SHARD_ROWS * s
        for t in range(9):
            out[at + 8 * t : at + 8 * t + 8] = jnp.concatenate(
                [convs[0, t, 8 * s : 8 * s + 8], convs[1, t, 8 * s : 8 * s + 8]], axis=1
            )
        out[at + CONV_ROWS : at + SHARD_ROWS] = small[SMALL_ROWS * s : SMALL_ROWS * s + SMALL_ROWS]


def k_params(*refs):
    ins, outs, sq, small = refs[:16], refs[16:20], refs[20], refs[21]
    for k in range(4):
        stem, convs, norms, head = ins[4 * k : 4 * k + 4]
        own = k in (1, 2)
        pack_params(
            (lambda dy, dx, r=stem: r[dy, dx, :, 0, :]) if own else (lambda dy, dx, r=stem: r[dy, dx]),
            convs,
            lambda i, r=norms: r[i],
            (lambda r=head: r[:, 0, :]) if own else (lambda r=head: r[...]),
            outs[k],
            sq,
            small,
        )


def k_halves(even, got, *outs):
    for k, out in enumerate(outs):
        out[...] = even[k] + got[k]


def adam(q, p, m, v):
    first = 0.9 * m + 0.1 * q
    second = 0.999 * v + 0.001 * q * q
    step = first / (1.0 - 0.9**STEP) / (jnp.sqrt(second / (1.0 - 0.999**STEP)) + 1e-08) + 0.01 * p
    return first, second, 0.05 * step


def k_adam(count, nb, me, *refs):
    parts, refs = refs[:4], refs[4:]
    stat, refs = refs[:nb], refs[nb:]
    pp, pm, pv, vec0, grad, delta, rest, px, ps = refs
    total = tree([r[...] for r in parts])
    r8 = total[SHARD_ROWS : SHARD_ROWS + 8]
    rest[...] = r8
    st = tree([r[...] for r in stat])
    px[...] = jnp.zeros(px.shape, F32)
    ps[...] = jnp.zeros(ps.shape, F32)
    px[0:40] = st[8:48]
    ps[0:40] = st[48:88]
    at = pl.ds(pl.multiple_of(SMALL_ROWS * me[0], 8), SMALL_ROWS)
    gain = vec0[2:3] * vec0[1:2]
    sm = total[CONV_ROWS:SHARD_ROWS]
    fixed = gain * (sm - ps[at] * (r8[0:1] / count) - px[at] * (r8[1:2] / count))
    sm = jnp.where(low_half(sm.shape), fixed, sm)
    q = jnp.concatenate([total[0:CONV_ROWS], sm], axis=0)
    qn = stack_rows([r8[k : k + 1] for k in (1, 0, 3, 2, 5, 4)])
    grad[0:SHARD_ROWS] = q
    grad[SHARD_ROWS : SHARD_ROWS + 8] = qn
    at = pl.ds(pl.multiple_of(SHARD_ROWS * me[0], 8), SHARD_ROWS)
    delta[0:SHARD_ROWS] = adam(q, pp[at], pm[at], pv[at])[2]
    at = slice(NORM_AT, NORM_AT + 8)
    delta[SHARD_ROWS : SHARD_ROWS + 8] = adam(qn, pp[at], pm[at], pv[at])[2]


def k_total(ng, grad, *refs):
    deltas, (pay, norm) = refs[:ng], refs[ng:]
    total = tree([d[...] for d in deltas])
    pay[0:SHARD_ROWS] = grad[0:SHARD_ROWS]
    pay[SHARD_ROWS : 2 * SHARD_ROWS] = total[0:SHARD_ROWS]
    norm[0:8] = grad[SHARD_ROWS : SHARD_ROWS + 8]
    norm[8:16] = total[SHARD_ROWS : SHARD_ROWS + 8]


def k_update(groups, classes, me, *refs):
    pays, (norm, rest, pp, pm, pv, mom), refs = refs[:8], refs[8:14], refs[14:]
    news, lows, firsts, seconds, outers, loss = (
        refs[0:4],
        refs[4:8],
        refs[8:12],
        refs[12:16],
        refs[16:20],
        refs[20],
    )
    grad, delta = refs[21:]
    for j, pay in enumerate(pays):
        s = jnp.bitwise_xor(me[0], j)
        at = pl.ds(pl.multiple_of(SHARD_ROWS * s, 8), SHARD_ROWS)
        grad[at] = pay[0:SHARD_ROWS]
        delta[at] = pay[SHARD_ROWS : 2 * SHARD_ROWS]
    grad[NORM_AT : NORM_AT + 8] = norm[0:8]
    delta[NORM_AT : NORM_AT + 8] = norm[8:16]
    p = pp[...]
    first, second, _ = adam(grad[...], p, pm[...], pv[...])
    average = delta[...] / groups
    outer = 0.9 * mom[...] + average
    new = p - 0.7 * (average + 0.9 * outer)
    unpack(new, news, False)
    unpack(new, lows, False)
    unpack(outer, outers, False)
    unpack(first, firsts, True)
    unpack(second, seconds, True)
    loss[...] = rest[6, 0:1]


def unpack(x, outs, own):
    stem, convs, norms, head = outs
    dt = convs.dtype
    smalls = []
    for s in range(SHARDS):
        at = SHARD_ROWS * s
        for t in range(9):
            blk = x[at + 8 * t : at + 8 * t + 8].astype(dt)
            convs[0, t, 8 * s : 8 * s + 8] = blk[:, 0:64]
            convs[1, t, 8 * s : 8 * s + 8] = blk[:, 64:128]
        smalls.append(x[at + CONV_ROWS : at + SHARD_ROWS])
    small = jnp.concatenate(smalls, axis=0)
    turned = jnp.transpose(small)
    classes, depth = head.shape[0], head.shape[-1]
    head_t = turned[64 : 64 + classes, 0:depth].astype(dt)
    if own:
        for k in range(classes):
            head[k] = head_t[k : k + 1]
    else:
        head[...] = head_t
    for dy in range(3):
        for dx in range(3):
            r = 12 * dx + 4 * dy
            if own:
                for c in range(3):
                    stem[dy, dx, c] = small[r + c : r + c + 1, 0:64].astype(dt)
            else:
                stem[dy, dx] = small[r : r + 3, 0:64].astype(dt)
    for k in range(3):
        norms[k] = x[NORM_AT + 2 * k : NORM_AT + 2 * k + 2, 0:64].astype(dt)


def k_conv(n, side, nb, layer, count, carried, *refs):
    a_in, nv = refs[0], refs[1]
    blocks, w = refs[2 : 2 + nb], refs[2 + nb]
    refs = refs[3 + nb :]
    riders, refs = refs[:carried], refs[carried:]
    a_out, st, vec = refs[:3]
    wides = refs[3:]
    pairs, rows = a_in.shape[0], a_in.shape[1]
    if riders:
        sums, vec0, s0 = riders
        ones = sums[40:80]
        local = s0[0:1] / (rows * pairs * 2)
        st[8:48] = vec0[1:2] * (sums[0:40] - (vec0[0:1] - local) * ones)
        st[48:88] = ones
    top, bottom = edges(rows, side)
    bl = [b[0:8] for b in blocks]
    mean, r = combine(bl, count)
    gain, bias = nv[2 * layer : 2 * layer + 1], nv[2 * layer + 1 : 2 * layer + 2]
    counts = tree(b[2:3] for b in bl)
    scale = gain * r
    vec[...] = stack_rows([mean, r, gain, bias, counts, scale])
    for wide in wides:
        zero_ends(wide)

    def prep(xp):
        h = jnp.maximum((a_in[xp].astype(F32) - mean) * scale + bias, 0.0)
        put(wides, xp, split(h, n))

    prep(0)
    s = jnp.zeros((8, 128), F32)
    for xp in range(pairs):
        if xp + 1 < pairs:
            prep(xp + 1)
        out = conv_block([wide[xp] for wide in wides], w, top, bottom)
        a_out[xp] = out.astype(a_out.dtype)
        s = s + part(out)
    s = dup(row_sum(s))
    m2 = centred_sums(a_out, s, rows * pairs * 2)
    st[0:8] = stack_rows([s, m2])


def bn(a, vec):
    d = a.astype(F32) - vec[0:1]
    return d * vec[1:2], d * vec[5:6] + vec[3:4]


def k_head(val, side, nb, count, classes, group_count, *refs):
    a2, a0, vec0r, nv, img, hp, hpt, hb = refs[:8]
    blocks = refs[8 : 8 + nb]
    mz, vec2r, info, extra = refs[8 + nb :]
    pairs, rows = a2.shape[0], a2.shape[1]
    images = rows // side
    mean, r = combine([b[0:8] for b in blocks], count)
    zero = jnp.zeros((1, 128), F32)
    vec2 = stack_rows([mean, r, nv[4:5], nv[5:6], zero, nv[4:5] * r])
    vec2r[...] = vec2
    vec0 = vec0r[...]
    zs = jnp.zeros((images, 8, 128), F32)
    ms = jnp.zeros((images, 8, 128), F32)
    xs = jnp.zeros((images, 8, 128), F32)
    for xp in range(pairs):
        xh2, y2 = bn(a2[xp], vec2)
        z = y2 + jnp.maximum(bn(a0[xp], vec0)[1], 0.0)
        on = z > 0
        m = jnp.where(on, 1.0, 0.0)
        mz[xp] = m.astype(BF16)
        zs = zs + image_part(jnp.maximum(z, 0.0), images)
        ms = ms + image_part(m, images)
        xs = xs + image_part(jnp.where(on, xh2, 0.0), images)
    zs, ms, xs = (jnp.sum(v, axis=1) for v in (zs, ms, xs))
    area = side * pairs * 2
    lt = low_half((images, 128))
    pooled, ms, xs = dup(zs) / area, dup(ms), dup(xs)
    logits = lax.dot(pooled, hp[...], precision=HIGH) + hb[0:1]
    lane = lax.broadcasted_iota(jnp.int32, (images, 128), 1)
    ok = lane < classes
    top = jnp.max(jnp.where(ok, logits, -3e38), axis=1, keepdims=True)
    e = jnp.where(ok, jnp.exp(jnp.where(ok, logits - top, 0.0)), 0.0)
    tot = jnp.sum(e, axis=1, keepdims=True)
    onehot = label_onehot(img[...], images, classes)
    pm = e / tot - onehot
    ce = jnp.log(tot) + top - jnp.sum(onehot * logits, axis=1, keepdims=True)
    g = lax.dot(pm, hpt[...], precision=HIGH)
    if val:
        n_val = group_count
        gp = g / (n_val * area)
        info[...] = gp
        head = lax.dot_general(
            pooled, pm / n_val, (((0,), (0,)), ((), ())), precision=HIGH
        )
        extra[0:64] = head[0:64]
        extra[64:72] = stack_rows([row_sum(pm) / n_val])
        extra[72:80] = stack_rows([row_sum(gp * ms), row_sum(gp * xs)])
    else:
        cw = group_count / (classes * (vec0[4:5] + 1.0))
        per = jnp.sum(onehot * cw, axis=1, keepdims=True)
        uw = jnp.where(lt, g * ms, g * xs)
        pc = jnp.where(lane == 0, per, jnp.where(lane == 1, image_mark(img[...], images, 97), 0.0))
        extra[0:images] = uw
        extra[images : 2 * images] = pc
        for k, v in enumerate((g, ms, xs, pooled, pm, jnp.broadcast_to(ce, (images, 128)))):
            info[k] = v


def k_static(side, img, a0, s0, out):
    pairs, rows = a0.shape[0], a0.shape[1]
    top, bottom = edges(rows, side)
    mean = s0[0:1] / (rows * pairs * 2)
    whole = stem_rows(img[...], top, bottom)
    lhs = turned_rows(split(whole, 2))
    out[0:40] = stem_grad(side, pairs, lhs, lambda xp: split(a0[xp] - mean, 2))[0]
    out[40:80] = patch_sums(side, whole)


def turned_rows(parts):
    return [jnp.transpose(p) for p in parts]


def stem_grad(side, pairs, lhs, *rhs_of):
    n = len(lhs)
    accs = [{} for _ in rhs_of]
    columns = [(q, xp) for xp in range(pairs) for q in range(len(rhs_of))]
    for at in range(0, len(columns), 2):
        two = columns[at : at + 2]
        parts = [rhs_of[q](xp) for q, xp in two]
        rhs = [jnp.concatenate([p[i] for p in parts], axis=1) for i in range(n)]
        f = None
        for i, j in TERMS[n]:
            t = mxu(lhs[i], rhs[j])
            f = t if f is None else f + t
        for place, (q, xp) in enumerate(two):
            near = near_rows(side, xp)
            for k in range(9):
                for b, d in near.items():
                    r = side * k + 8 * b
                    blk = f[r : r + 8, 128 * place : 128 * place + 128]
                    for dx in range(3):
                        v = jnp.where(d == dx, blk, 0.0)
                        key = (dx, k)
                        accs[q][key] = accs[q][key] + v if key in accs[q] else v
    outs = []
    zero = jnp.zeros((1, 128), F32)
    for acc in accs:
        rows = []
        for dx in range(3):
            for dy in range(3):
                rows += [dup(row_sum(acc[dx, 3 * dy + c])) for c in range(3)] + [zero]
        outs.append(jnp.concatenate(rows + [zero] * 4, axis=0))
    return outs


def patch_sums(side, whole):
    sums = row_sum(whole)
    col = jnp.transpose(jnp.broadcast_to(sums, (8, sums.shape[1])))[:, 0:1]
    xin = lax.rem(lax.broadcasted_iota(jnp.int32, col.shape, 0), side)
    rows = []
    for dx in range(3):
        keep = xin <= side - 2 if dx == 0 else (xin >= 1 if dx == 2 else xin >= 0)
        c = jnp.where(keep, col, 0.0)
        for k in range(12):
            if k % 4 == 3:
                rows.append(jnp.zeros((1, 128), F32))
                continue
            r = side * (3 * (k // 4) + k % 4)
            rows.append(jnp.broadcast_to(row_sum(c[r : r + side]), (1, 128)))
    return jnp.concatenate(rows + [jnp.zeros((4, 128), F32)], axis=0)


def back_of_norm2(gp, vec2, s1, s2, count, side, a2, mz):
    images, rows = gp.shape[0], a2.shape[1]
    k2 = vec2[2:3] * vec2[1:2]
    c0, c1 = k2 * s1 / count, k2 * s2 / count
    gk = jnp.broadcast_to((gp * k2)[:, None, :], (images, side, 128)).reshape(rows, 128)

    c1 = c1 * vec2[1:2]
    c0 = c0 - vec2[0:1] * c1

    def at(xp):
        return mz[xp].astype(F32) * gk - (a2[xp].astype(F32) * c1 + c0)

    return at


def back_of_norm1(vec1, s1, s2, count, dy1, a1):
    k1 = vec1[2:3] * vec1[1:2]
    c0, c1 = k1 * s1 / count, k1 * s2 / count

    c1 = c1 * vec1[1:2]
    c0 = c0 - vec1[0:1] * c1

    def at(xp):
        return dy1[xp].astype(F32) * k1 - (a1[xp].astype(F32) * c1 + c0)

    return at


def back_conv2(n, side, gp, vec2, s1, s2, count, a2, mz, a1, vec1, wt, wides, dy1, extra):
    pairs, rows = a2.shape[0], a2.shape[1]
    images = rows // side
    top, bottom = edges(rows, side)
    for wide in wides:
        zero_ends(wide)
    back_at = back_of_norm2(gp, vec2, s1, s2, count, side, a2, mz)

    def prep(xp):
        back = back_at(xp)
        parts = split(back, n)
        put(wides, xp, parts)
        if extra is not None:
            extra(xp, back, parts)

    prep(0)
    q1 = jnp.zeros((8, 128), F32)
    q2 = jnp.zeros((8, 128), F32)
    for xp in range(pairs):
        if xp + 1 < pairs:
            prep(xp + 1)
        dh = conv_block([wide[xp] for wide in wides], wt, top, bottom)
        xh1, y1 = bn(a1[xp], vec1)
        dy = jnp.where(y1 > 0, dh, 0.0)
        dy1[xp] = dy.astype(dy1.dtype)
        q1 = q1 + part(dy)
        q2 = q2 + part(dy * xh1)
    return dup(row_sum(q1)), dup(row_sum(q2))


def shifted(back, top, bottom):
    return jnp.concatenate([up(back, bottom), back, down(back, top)], axis=1)


def k_val_back2(side, nb, count, *refs):
    a2, mz, a1, vec2r, vec1r, gp, wt, wide1 = refs[:8]
    blocks = refs[8 : 8 + nb]
    dy1, st, g2 = refs[8 + nb : 11 + nb]
    wide, acc = refs[11 + nb :]
    wides = (wide,)
    rows = a2.shape[1]
    top, bottom = edges(rows, side)
    s1 = tree(b[72:73] for b in blocks)
    s2 = tree(b[73:74] for b in blocks)
    acc[...] = jnp.zeros(acc.shape, F32)

    def extra(xp, back, parts):
        acc[...] += mxu_t(shifted(back, top, bottom).astype(BF16), wide1[xp])

    q1, q2 = back_conv2(
        1, side, gp[...], vec2r[...], s1, s2, count, a2, mz, a1, vec1r[...], wt, wides, dy1, extra
    )
    fold_pair(jnp.transpose(acc[...]), g2)
    st[...] = stack_rows([q1, q2, s1, s2])


def back_conv1(n, side, gp, vec1, vec0, s1, s2, count, dy1, a1, a0, mz, wt, wides, dy0, extra):
    pairs, rows = a1.shape[0], a1.shape[1]
    images = rows // side
    top, bottom = edges(rows, side)
    for wide in wides:
        zero_ends(wide)
    back_at = back_of_norm1(vec1, s1, s2, count, dy1, a1)
    gpr = jnp.broadcast_to(gp[:, None, :], (images, side, 128)).reshape(rows, 128)

    def prep(xp):
        back = back_at(xp)
        parts = split(back, n)
        put(wides, xp, parts)
        if extra is not None:
            extra(xp, back, parts)

    prep(0)
    q1 = jnp.zeros((8, 128), F32)
    q2 = jnp.zeros((8, 128), F32)
    for xp in range(pairs):
        if xp + 1 < pairs:
            prep(xp + 1)
        dh = conv_block([wide[xp] for wide in wides], wt, top, bottom)
        xh0, y0 = bn(a0[xp], vec0)
        dy = jnp.where(y0 > 0, dh + mz[xp].astype(F32) * gpr, 0.0)
        dy0[xp] = dy.astype(dy0.dtype)
        q1 = q1 + part(dy)
        q2 = q2 + part(dy * xh0)
    return dup(row_sum(q1)), dup(row_sum(q2))


def k_val_back1(side, nb, count, *refs):
    dy1, a1, a0, mz, vec1r, vec0r, gp, wt, wide0, img = refs[:10]
    blocks = refs[10 : 10 + nb]
    g1, small = refs[10 + nb : 12 + nb]
    wide, acc, dy0 = refs[12 + nb :]
    wides = (wide,)
    pairs, rows = a1.shape[0], a1.shape[1]
    top, bottom = edges(rows, side)
    s1 = tree(b[0:1] for b in blocks)
    s2 = tree(b[1:2] for b in blocks)
    acc[...] = jnp.zeros(acc.shape, F32)
    vec0 = vec0r[...]

    def extra(xp, back, parts):
        acc[...] += mxu_t(shifted(back, top, bottom).astype(BF16), wide0[xp])

    q1, q2 = back_conv1(
        1, side, gp[...], vec1r[...], vec0, s1, s2, count, dy1, a1, a0, mz, wt, wides, dy0, extra
    )
    fold_pair(jnp.transpose(acc[...]), g1)
    whole = stem_rows(img[...], top, bottom)
    small[0:40], small[40:80] = stem_grad(
        side,
        pairs,
        turned_rows([whole.astype(BF16)]),
        lambda xp: [dy0[xp]],
        lambda xp: [((a0[xp].astype(F32) - vec0[0:1]) * vec0[1:2]).astype(BF16)],
    )
    small[80:120] = patch_sums(side, whole)
    small[120:128] = stack_rows([q1, q2])


def k_tan1(side, nb, nv_blocks, count, count_val, *refs):
    img, a0, a1, vec0r, vec1r, w1, vvec0r = refs[:7]
    refs = refs[7:]
    stat = refs[:nb]
    refs = refs[nb:]
    smalls, g1s, sts = refs[:nv_blocks], refs[nv_blocks : 2 * nv_blocks], refs[2 * nv_blocks : 3 * nv_blocks]
    t1, th0, st, wide, wide0, v1 = refs[3 * nv_blocks :]
    pairs, rows = a1.shape[0], a1.shape[1]
    top, bottom = edges(rows, side)
    vec0, vec1, vv0 = vec0r[...], vec1r[...], vvec0r[...]
    small = sum(b[...] for b in smalls)
    q1, q2 = small[120:121], small[121:122]
    v0 = (
        vv0[2:3]
        * vv0[1:2]
        * (small[0:40] - small[80:120] * (q1 / count_val) - small[40:80] * (q2 / count_val))
    )
    static = tree(b[...] for b in stat)
    u1 = row_sum(v0 * static[48:88])
    u2 = row_sum(v0 * static[8:48])
    k0 = vec0[2:3] * vec0[1:2]
    e0 = q1 - k0 * u1 / count
    e1 = q2 - k0 * u2 / count
    for dy in range(3):
        taps = []
        for dx in range(3):
            r = 64 * (3 * dy + dx)
            taps.append(sum(g[r : r + 64] for g in g1s))
        v1[:, 128 * dy : 128 * dy + 128] = pair_form(*taps).astype(BF16)
    zero_ends(wide)
    zero_ends(wide0)
    lhs = stem_rows(img[...], top, bottom).astype(BF16)
    tang = {}

    def prep(xp):
        if xp % 2 == 0:
            band = jnp.concatenate(
                [stem_band(v0, side, xp), stem_band(v0, side, xp + 1)], axis=1
            ).astype(BF16)
            z = mxu(lhs, band)
            tang[xp], tang[xp + 1] = z[:, 0:128], z[:, 128:256]
        xh0, y0 = bn(a0[xp], vec0)
        th = jnp.where(y0 > 0, k0 * tang.pop(xp) + e1 * xh0 + e0, 0.0).astype(BF16)
        th0[xp] = th
        put((wide, wide0), xp, [th, jnp.maximum(y0, 0.0).astype(BF16)])

    prep(0)
    p1 = jnp.zeros((8, 128), F32)
    p2 = jnp.zeros((8, 128), F32)
    for xp in range(pairs):
        if xp + 1 < pairs:
            prep(xp + 1)
        t = row_taps(mxu(wide[xp], w1[:, 0:384]) + mxu(wide0[xp], v1[...]), top, bottom)
        t1[xp] = t
        xh1 = (a1[xp] - vec1[0:1]) * vec1[1:2]
        p1 = p1 + part(t)
        p2 = p2 + part(t * xh1)
    vs = [sum(b[k : k + 1] for b in sts) for k in range(2)]
    st[...] = stack_rows([dup(row_sum(p1)), dup(row_sum(p2)), vs[0], vs[1], sts[0][2:3], sts[0][3:4]])


def k_tan2(side, nb, nv_blocks, count, *refs):
    t1, th0, a1, a2, mz, vec1r, vec2r, w2, info, own, gather = refs[:11]
    refs = refs[11:]
    blocks = refs[:nb]
    refs = refs[nb:]
    g2s, heads = refs[:nv_blocks], refs[nv_blocks : 2 * nv_blocks]
    st, wide, wide1, v2 = refs[2 * nv_blocks :]
    pairs, rows = a1.shape[0], a1.shape[1]
    images = rows // side
    top, bottom = edges(rows, side)
    vec1, vec2 = vec1r[...], vec2r[...]
    u1 = tree(b[0:1] for b in blocks)
    u2 = tree(b[1:2] for b in blocks)
    k1 = vec1[2:3] * vec1[1:2]
    e0 = own[2:3] - k1 * u1 / count
    e1 = own[3:4] - k1 * u2 / count
    for dy in range(3):
        taps = []
        for dx in range(3):
            r = 64 * (3 * dy + dx)
            taps.append(sum(g[r : r + 64] for g in g2s))
        v2[:, 128 * dy : 128 * dy + 128] = pair_form(*taps).astype(BF16)
    zero_ends(wide)
    zero_ends(wide1)

    def prep(xp):
        xh1, y1 = bn(a1[xp], vec1)
        th = jnp.where(y1 > 0, k1 * t1[xp] + e1 * xh1 + e0, 0.0).astype(BF16)
        put((wide, wide1), xp, [th, jnp.maximum(y1, 0.0).astype(BF16)])

    prep(0)
    p1 = jnp.zeros((8, 128), F32)
    p2 = jnp.zeros((8, 128), F32)
    asum = jnp.zeros((images, 8, 128), F32)
    k2 = vec2[2:3] * vec2[1:2]
    for xp in range(pairs):
        if xp + 1 < pairs:
            prep(xp + 1)
        t = row_taps(mxu(wide[xp], w2[:, 0:384]) + mxu(wide1[xp], v2[...]), top, bottom)
        xh2 = (a2[xp] - vec2[0:1]) * vec2[1:2]
        p1 = p1 + part(t)
        p2 = p2 + part(t * xh2)
        m = mz[xp].astype(F32)
        asum = asum + image_part(m * (k2 * t + th0[xp].astype(F32)), images)
    asum = dup(jnp.sum(asum, axis=1))
    area = side * pairs * 2
    g, ms, xs, pooled, pm = (info[k] for k in range(5))
    inner = g * (asum + own[5:6] * xs + own[4:5] * ms)
    base = jnp.sum(jnp.where(low_half(inner.shape), inner, 0.0), axis=1, keepdims=True) / area
    vhead = sum(h[0:72] for h in heads)
    vh = jnp.concatenate([vhead[0:64], jnp.zeros((64, 128), F32)], axis=0)
    lin = lax.dot(pooled, vh, precision=HIGH) + vhead[64:65]
    base = base + jnp.sum(pm * lin, axis=1, keepdims=True)
    st[0:images] = jnp.broadcast_to(base, (images, 128))
    p1, p2 = dup(row_sum(p1)), dup(row_sum(p2))
    st[images : images + 8] = stack_rows([jnp.where(low_half(p1.shape), p1, p2)])
    st[images + 8 :] = gather[...]


def k_train_back2(side, nb, count, group_count, n, *refs):
    flag, a2, mz, a1, vec2r, vec1r, wt, info = refs[:8]
    refs = refs[8:]
    dyn = refs[:nb]
    dy1, st, wgp = refs[nb : nb + 3]
    wides = refs[nb + 3 :]
    pairs, rows = a2.shape[0], a2.shape[1]
    images = rows // side
    area = side * pairs * 2
    vec2 = vec2r[...]
    k2 = vec2[2:3] * vec2[1:2]
    each = dyn[0].shape[0]
    at = images + 8
    tsum = 0.0
    for b in range(nb):
        for j in range(each):
            tsum = tsum + dyn[b][j, images : images + 1]
    tt = tsum * k2 / (count * area)
    raws, pers = [], []
    total = jnp.zeros((1, 1), F32)
    mag = jnp.zeros((1, 1), F32)
    for b in range(nb):
        for j in range(each):
            uw = dyn[b][j, at : at + images]
            pc = dyn[b][j, at + images : at + 2 * images]
            per, clip = pc[:, 0:1], pc[:, 1:2]
            tan = dyn[b][j, 0:images, 0:1] - jnp.sum(uw * tt, axis=1, keepdims=True)
            score = -ALPHA * per * tan
            raw = clip * jnp.maximum(-score, 0.0)
            total = total + row_sum(raw)
            mag = mag + row_sum(clip * jnp.abs(score))
            raws.append(raw)
            pers.append(per)
    on = flag[0] == 1
    denom = jnp.maximum(total, 0.25 * mag) + 1e-06
    ssum = jnp.zeros((1, 128), F32)
    k = 0
    own = None
    for b in range(nb):
        for j in range(each):
            w = jnp.where(on, raws[k] / denom, 1.0 / group_count) * pers[k]
            own = w if own is None else own
            ssum = ssum + row_sum(w * dyn[b][j, at : at + images])
            k += 1
    ssum = ssum / area
    lt = low_half(ssum.shape)
    s1, s2 = dup(jnp.where(lt, ssum, 0.0)), dup(jnp.where(lt, 0.0, ssum))
    g, pooled, pm, ce = info[0], info[3], info[4], info[5]
    gp = own * g / area
    wgp[0:images] = gp
    head = lax.dot_general(pooled, own * pm, (((0,), (0,)), ((), ())), precision=HIGH)
    wgp[images : images + 64] = head[0:64]
    mine = row_sum(own * dyn[0][0, at : at + images]) / area
    o1, o2 = dup(jnp.where(lt, mine, 0.0)), dup(jnp.where(lt, 0.0, mine))
    wgp[images + 64 : images + 72] = stack_rows([row_sum(own * pm), row_sum(own * ce), o1, o2])

    wgp[images + 72 : images + 80] = stack_rows([s1, s2])
    q1, q2 = back_conv2(
        n, side, gp, vec2, s1, s2, count, a2, mz, a1, vec1r[...], wt, wides, dy1, None
    )
    st[...] = stack_rows([q1, q2])


def k_train_back1(side, nb, n, count, me, *refs):
    dy1, a1, a0, mz, vec1r, vec0r, wt, img, wgp, d2, st1 = refs[:11]
    blocks = refs[11 : 11 + nb]
    even, odd, acc, d1, small, dy0 = refs[11 + nb : 17 + nb]
    wides, inputs = refs[17 + nb : 17 + nb + n], refs[17 + nb + n :]
    pairs, rows = a1.shape[0], a1.shape[1]
    images = rows // side
    top, bottom = edges(rows, side)
    s1 = tree(b[0:1] for b in blocks)
    s2 = tree(b[1:2] for b in blocks)
    vec0 = vec0r[...]
    acc[...] = jnp.zeros(acc.shape, F32)
    for wide in inputs:
        zero_ends(wide)
    held = {}

    def gradient(xp):
        lhs = split(shifted(held.pop(xp), top, bottom), n)
        t = None
        for i, j in TERMS[n]:
            d = mxu_t(lhs[i], inputs[j][xp])
            t = d if t is None else t + d
        acc[...] += t

    def extra(xp, back, parts):
        put(inputs, xp, split(jnp.maximum(bn(a0[xp], vec0)[1], 0.0), n))
        held[xp] = back
        if xp > 0:
            gradient(xp - 1)

    q1, q2 = back_conv1(
        n, side, wgp[0:images], vec1r[...], vec0, s1, s2, count, dy1, a1, a0, mz, wt, wides, dy0, extra
    )
    gradient(pairs - 1)
    fold_pair(jnp.transpose(acc[...]), d1)
    lhs = turned_rows(split(stem_rows(img[...], top, bottom), n))
    stem = stem_grad(side, pairs, lhs, lambda xp: split(dy0[xp], n))[0]
    small[...] = jnp.zeros((128, 128), F32)
    small[0:65] = wgp[images : images + 65]
    right = pltpu.roll(small[...], 64, 1)
    small[...] = jnp.zeros((128, 128), F32)
    small[0:40] = stem
    small[...] = jnp.where(low_half((128, 128)), small[...], right)
    rest = stack_rows(
        [q1, q2, st1[0:1], st1[1:2]] + [wgp[images + k : images + k + 1] for k in (66, 67, 65)]
    )
    lt8 = low_half((8, 128))
    for j in range(SHARDS):
        s = jnp.bitwise_xor(me[0], j)
        dst = (even, odd)[j % 2]
        k = j // 2
        for t in range(9):
            at = pl.ds(pl.multiple_of(64 * t + 8 * s, 8), 8)
            dst[k, 8 * t : 8 * t + 8] = jnp.where(lt8, d1[at], d2[at])
        dst[k, CONV_ROWS:SHARD_ROWS] = small[pl.ds(pl.multiple_of(SMALL_ROWS * s, 8), SMALL_ROWS)]
        dst[k, SHARD_ROWS : SHARD_ROWS + 8] = rest


def weight_gradient(side, n, a, vec, back_at, wides, acc, g):
    pairs, rows = a.shape[0], a.shape[1]
    top, bottom = edges(rows, side)
    acc[...] = jnp.zeros(acc.shape, F32)
    for wide in wides:
        zero_ends(wide)

    def prep(xp):
        put(wides, xp, split(jnp.maximum(bn(a[xp], vec)[1], 0.0), n))

    prep(0)
    for xp in range(pairs):
        if xp + 1 < pairs:
            prep(xp + 1)
        lhs = split(shifted(back_at(xp), top, bottom), n)
        t = None
        for i, j in TERMS[n]:
            d = mxu_t(lhs[i], wides[j][xp])
            t = d if t is None else t + d
        acc[...] += t
    fold_pair(jnp.transpose(acc[...]), g)


def k_dw2(side, n, count, a1, vec1, a2, vec2, mz, wgp, g, acc, *wides):
    images = a1.shape[1] // side
    at = images + 72
    back_at = back_of_norm2(
        wgp[0:images], vec2[...], wgp[at : at + 1], wgp[at + 1 : at + 2], count, side, a2, mz
    )
    weight_gradient(side, n, a1, vec1[...], back_at, wides, acc, g)


VM = pl.BlockSpec(memory_space=pltpu.VMEM)
SM = pl.BlockSpec(memory_space=pltpu.SMEM)


def call(kernel, outs, args, scratch=(), smem=(), raw=(), us=1.0, after=()):
    count = len(args)

    def run(*refs):
        kernel(*refs[:count], *refs[count + len(after) :])

    def placed(i, x):
        if i in raw:
            return pltpu.with_memory_space_constraint(x, pltpu.HBM)
        return pltpu.with_memory_space_constraint(x, pltpu.VMEM) if x.size >= KEEP else x

    return pl.pallas_call(
        run,
        out_shape=[
            pltpu.VMEM(s, d) if math.prod(s) >= KEEP else jax.ShapeDtypeStruct(s, d)
            for s, d in outs
        ],
        in_specs=[SM if i in smem else VM for i in range(count)]
        + [pl.BlockSpec(memory_space=pl.ANY)] * len(after),
        out_specs=[VM] * len(outs),
        scratch_shapes=[pltpu.VMEM(s, d) for s, d in scratch],
        compiler_params=pltpu.CompilerParams(vmem_limit_bytes=VMEM_BYTES),
        cost_estimate=pl.CostEstimate(
            flops=int(us * 1.1e9), bytes_accessed=1 << 16, transcendentals=0
        ),
    )(*[placed(i, x) for i, x in enumerate(args)], *[placed(-1, x) for x in after])


def swap(x, k, n):
    return lax.ppermute(x, "dp", [(i, i ^ k) for i in range(n)])


def add(a, b, step):
    return a + b


def chan(count, a, b, step):
    d = a[0:1] - b[0:1]
    cross = d * d / (2.0 * count * step)
    return a + b + jnp.pad(cross, ((1, a.shape[0] - 2), (0, 0)))


def near(x, team, merge):
    n = lax.axis_size("dp")
    k = 1
    while k < team // 2:
        x = merge(x, swap(x, k, n), k)
        k *= 2
    return [x, swap(x, k, n)] if team > 1 else [x]


def far(x, merge, rider=None):
    n = lax.axis_size("dp")
    k = 1
    while k < n // 4:
        x = merge(x, swap(x, k, n), k)
        k *= 2
    if rider is not None:
        x = jnp.concatenate([x, rider], axis=0)
    return [x] + [swap(x, j * k + 1, n) for j in range(1, n // k)]


def far_list(x):
    n = lax.axis_size("dp")
    x = x[None]
    k = 1
    while k < n // 4:
        x = jnp.concatenate([x, swap(x, k, n)], axis=0)
        k *= 2
    return [x] + [swap(x, j * k + 1, n) for j in range(1, n // k)]


def body(
    train_images,
    train_labels,
    flip_flags,
    class_ids,
    clip_mask,
    norm_flag,
    val_images,
    val_labels,
    stem,
    convs,
    norms,
    head,
    m_stem,
    v_stem,
    m_convs,
    v_convs,
    m_norms,
    v_norms,
    m_head,
    v_head,
    mom_stem,
    mom_convs,
    mom_norms,
    mom_head,
):
    dp = lax.axis_size("dp")
    classes = head.shape[1]
    side, pairs = train_images.shape[1], train_images.shape[2] // 2
    images, val_each = train_images.shape[0], val_images.shape[0]
    group_train, group_val = dp * images, dp * val_each
    team = max(2, group_val // 16)
    rows, vrows = images * side, side * group_val // team
    vimages = group_val // team
    count, count_val = group_train * side * pairs * 2, group_val * side * pairs * 2
    nt, nval = 3, 1

    act = (pairs, rows, 128)
    st = ((8, 128), F32)
    square = ((128, 128), F32)

    def planes(img):
        return jnp.transpose(img, (0, 3, 1, 2))

    me = lax.rem(lax.axis_index("dp"), SHARDS).astype(jnp.int32).reshape(1)
    a0, s0, img, s40, vpack = call(
        functools.partial(k_first, nt, side, classes),
        [(act, F32), st, ((rows, 128), F32), ((40, 128), F32), ((val_each * side, 128), F32)],
        [train_labels, flip_flags, class_ids, clip_mask, val_labels]
        + [planes(train_images), planes(val_images), stem],
        smem=range(5),
        raw=range(8),
        us=4.5,
        after=[me],
    )
    b0 = far(s0, functools.partial(chan, rows * pairs * 2), vpack)
    (static,) = call(
        functools.partial(k_static, side), [((80, 128), F32)], [img, a0, s0], us=2.0, after=b0[:1]
    )
    forms = [((256, 384 * n), BF16) for n in (3, 3, 2, 2)]
    w1, w2, t1w, t2w, nv, hp, hpt, hb = call(
        k_weights,
        forms + [st, square, square, st],
        [convs.reshape(2, 9, 64, 64), norms, head.T],
        [square],
        raw=range(3),
        us=2.0,
    )
    moment_views = [
        (
            jnp.transpose(x[0], (1, 2, 3, 0, 4)),
            x[1].reshape(2, 9, 64, 64),
            x[2][0],
            jnp.transpose(x[3], (2, 0, 1)),
        )
        for x in ((m_stem, m_convs, m_norms, m_head), (v_stem, v_convs, v_norms, v_head))
    ]
    packed = call(
        k_params,
        [(PACKED, F32)] * 4,
        [stem, convs.reshape(2, 9, 64, 64), norms, head.T]
        + [x for views in moment_views for x in views]
        + [mom_stem, mom_convs.reshape(2, 9, 64, 64), mom_norms, mom_head.T],
        [square, square],
        raw=range(16),
        us=2.0,
    )

    act = (pairs, rows, 128)
    vact = (pairs, vrows, 128)

    def wide(r):
        return ((pairs, r, 256), BF16)

    va0, vs0, vimg = call(
        functools.partial(k_val_stem, side, val_each * side),
        [(vact, BF16), st, ((vrows, 128), F32)],
        [s40] + b0,
        us=2.4,
    )
    vchan = functools.partial(chan, vrows * pairs * 2)
    vb0 = near(vs0, team, vchan)

    def conv(n, layer, r, total, a, blocks, w, rider=(), after=()):
        pay = ((8 + (rider[0].shape[0] if rider else 0), 128), F32)
        return call(
            functools.partial(k_conv, n, side, len(blocks), layer, total, len(rider)),
            [((pairs, r, 128), F32 if n > 1 else BF16), pay, st] + [wide(r)] * (n == 1),
            [a, nv] + blocks + [w] + list(rider),
            [wide(r)] * n * (n > 1),
            us=6.7 if n > 1 else 3.3,
            after=after,
        )

    a1, s1, vec0 = conv(nt, 0, rows, count, a0, b0, w1, after=[static])
    b1 = far(s1, functools.partial(chan, rows * pairs * 2))
    va1, vs1, vvec0, vwide0 = conv(nval, 0, vrows, count_val, va0, vb0, w1, after=[s1])
    vb1 = near(vs1, team, vchan)
    va2, vs2, vvec1, vwide1 = conv(nval, 1, vrows, count_val, va1, vb1, w2, after=b1[:1])
    vb2 = near(vs2, team, vchan)
    a2, s2, vec1 = conv(nt, 1, rows, count, a1, b1, w2, [static, vec0, s0])
    b2 = far(s2, functools.partial(chan, rows * pairs * 2))

    vmz, vvec2, vgp, vextra = call(
        functools.partial(k_head, True, side, len(vb2), count_val, classes, group_val),
        [(vact, BF16), st, ((vimages, 128), F32), ((80, 128), F32)],
        [va2, va0, vvec0, nv, vimg, hp, hpt, hb] + vb2,
        us=4.0,
        after=[s2],
    )
    vextras = near(vextra, team, add)
    vdy1, vst1, g2 = call(
        functools.partial(k_val_back2, side, len(vextras), count_val),
        [(vact, BF16), st, ((576, 128), F32)],
        [va2, vmz, va1, vvec2, vvec1, vgp, t2w, vwide1] + vextras,
        [wide(vrows), ((384, 256), F32)],
        us=6.0,
        after=b2[:1],
    )
    vst1s = near(vst1, team, add)
    g2s = near(g2, team, add)
    g1, small = call(
        functools.partial(k_val_back1, side, len(vst1s), count_val),
        [((576, 128), F32), ((128, 128), F32)],
        [vdy1, va1, va0, vmz, vvec1, vvec0, vgp, t1w, vwide0, vimg] + vst1s,
        [wide(vrows), ((384, 256), F32), (vact, BF16)],
        us=7.0,
        after=b2[1:],
    )
    smalls = near(small, team, add)
    g1s = near(g1, team, add)

    tan1, th0, ts1 = call(
        functools.partial(k_tan1, side, len(b2), len(g1s), count, count_val),
        [(act, F32), (act, BF16), st],
        [img, a0, a1, vec0, vec1, w1, vvec0] + b2 + smalls + g1s + vst1s,
        [wide(rows), wide(rows), ((256, 384), BF16)],
        us=4.0,
    )
    tb1 = far(ts1, add)
    mz, vec2, info, gather = call(
        functools.partial(k_head, False, side, len(b2), count, classes, group_train),
        [(act, BF16), st, ((6, images, 128), F32), ((2 * images, 128), F32)],
        [a2, a0, vec0, nv, img, hp, hpt, hb] + b2,
        us=2.2,
        after=[ts1],
    )
    (ts2,) = call(
        functools.partial(k_tan2, side, len(tb1), len(g2s), count),
        [((3 * images + 8, 128), F32)],
        [tan1, th0, a1, a2, mz, vec1, vec2, w2, info, ts1, gather] + tb1 + g2s + vextras,
        [wide(rows), wide(rows), ((256, 384), BF16)],
        us=4.0,
    )
    dyn = far_list(ts2)

    nb_ = 2
    dy1, bs1, wgp = call(
        functools.partial(k_train_back2, side, len(dyn), count, group_train, nb_),
        [(act, F32), st, ((images + 80, 128), F32)],
        [norm_flag, a2, mz, a1, vec2, vec1, t2w, info] + dyn,
        [wide(rows)] * nb_,
        smem=(0,),
        us=4.3,
    )
    bb1 = far(bs1, add)
    (d2,) = call(
        functools.partial(k_dw2, side, nb_, count),
        [((576, 128), F32)],
        [a1, vec1, a2, vec2, mz, wgp],
        [((384, 256), F32)] + [wide(rows)] * nb_,
        us=3.6,
    )
    piece = (SHARD_ROWS + 8, 128)
    even, odd = call(
        functools.partial(k_train_back1, side, len(bb1), nb_, count),
        [((4,) + piece, F32)] * 2,
        [me, dy1, a1, a0, mz, vec1, vec0, t1w, img, wgp, d2, bs1] + bb1,
        [((384, 256), F32), ((576, 128), F32), square, (act, F32)] + [wide(rows)] * (2 * nb_),
        smem=(0,),
        us=9.0,
    )

    k = SHARDS
    while k < dp:
        even, odd = even + swap(even, k, dp), odd + swap(odd, k, dp)
        k *= 2
    halves = call(k_halves, [(piece, F32)] * 4, [even, swap(odd, 1, dp)])
    parts = [halves[0]] + [swap(halves[k], 2 * k, dp) for k in range(1, 4)]
    grad, delta, rest = call(
        functools.partial(k_adam, count, len(b2)),
        [(piece, F32), (piece, F32), st],
        [me] + parts + b2 + list(packed[:3]) + [vec0],
        [square, square],
        smem=(0,),
    )
    groups = lax.axis_size("group")
    deltas = [delta] + [
        lax.ppermute(delta, "group", [(i, i ^ k) for i in range(groups)])
        for k in range(1, groups)
    ]
    pay, norm = call(
        functools.partial(k_total, groups),
        [((2 * SHARD_ROWS, 128), F32), ((16, 128), F32)],
        [grad] + deltas,
    )
    pays = []
    for k in range(4):
        x = swap(pay, 2 * k, dp) if k else pay
        pays += [x, swap(x, 1, dp)]
    p4 = [(3, 3, 3, 64), (2, 9, 64, 64), (3, 2, 64), (classes, head.shape[0])]
    g4 = [(3, 3, 3, 1, 64), (2, 9, 64, 64), (3, 2, 64), (classes, 1, head.shape[0])]
    outs = call(
        functools.partial(k_update, groups, classes),
        [(x, F32) for x in p4]
        + [(x, BF16) for x in p4]
        + [(x, F32) for x in g4 + g4 + p4]
        + [((1,), F32)],
        [me] + pays + [norm, rest] + list(packed),
        [(PACKED, F32)] * 2,
        smem=(0,),
    )

    def plain(stem, convs, norms, head):
        return [stem, convs.reshape(2, 3, 3, 64, 64), norms, head.T]

    def own(stem, convs, norms, head):
        return [
            jnp.transpose(stem, (3, 0, 1, 2, 4)),
            convs.reshape(1, 2, 3, 3, 64, 64),
            norms[None],
            jnp.transpose(head, (1, 2, 0)),
        ]

    return (
        *plain(*outs[0:4]),
        *plain(*outs[4:8]),
        *own(*outs[8:12]),
        *own(*outs[12:16]),
        *plain(*outs[16:20]),
        outs[20],
    )


def solution(mesh):
    split4 = P(("group", "dp"), None, None, None)
    split1 = P(("group", "dp"))
    group = P("group")
    whole = P()
    return jax.shard_map(
        body,
        mesh=mesh,
        in_specs=(split4, split1, split1, split1, split1, group, split4, split1)
        + (whole,) * 4
        + (group,) * 8
        + (whole,) * 4,
        out_specs=(whole,) * 8 + (group,) * 8 + (whole,) * 4 + (group,),
        check_vma=False,
    )
```

```python
import functools
import math

import jax
import jax.numpy as jnp
from jax import lax
from jax.experimental import pallas as pl
from jax.experimental.pallas import tpu as pltpu
from jax.sharding import PartitionSpec as P

STEP = 10
BN_EPS = 1e-05
ALPHA = 0.1
F32 = jnp.float32
BF16 = jnp.bfloat16
HIGH = lax.Precision.HIGHEST
VMEM_BYTES = 18 * 1024 * 1024
KEEP = 200000


TERMS = {
    1: ((0, 0),),
    2: ((1, 0), (0, 1), (0, 0)),
    3: ((2, 0), (1, 1), (0, 2), (1, 0), (0, 1), (0, 0)),
}


def mxu(a, b):
    return lax.dot_general(a, b, (((1,), (0,)), ((), ())), preferred_element_type=F32)


def mxu_t(a, b):
    return lax.dot_general(a, b, (((0,), (0,)), ((), ())), preferred_element_type=F32)


def split(x, n):
    parts = []
    for k in range(n):
        p = x.astype(BF16)
        parts.append(p)
        if k + 1 < n:
            x = x - p.astype(F32)
    return parts


def dup(v):
    return v + pltpu.roll(v, v.shape[-1] // 2, v.ndim - 1)


def low_half(shape):
    return lax.broadcasted_iota(jnp.int32, shape, len(shape) - 1) < shape[-1] // 2


def edges(rows, side):
    y = lax.rem(lax.broadcasted_iota(jnp.int32, (rows, 128), 0), side)
    return y == 0, y == side - 1


def down(x, top):
    return jnp.where(top, 0.0, pltpu.roll(x, 1, 0))


def up(x, bottom):
    return jnp.where(bottom, 0.0, pltpu.roll(x, x.shape[0] - 1, 0))


def row_sum(x):
    return jnp.sum(x, axis=0, keepdims=True)


def part(x):
    return jnp.sum(x.reshape(x.shape[0] // 8, 8, 128), axis=0)


def image_part(x, images):
    return jnp.sum(x.reshape(images, x.shape[0] // (8 * images), 8, 128), axis=1)


def zero_ends(wide):
    last, rows = wide.shape[0] - 1, wide.shape[1]
    wide[last, :, 128:192] = jnp.zeros((rows, 64), BF16)
    wide[0, :, 192:256] = jnp.zeros((rows, 64), BF16)


def put(wides, xp, parts):
    for wide, part in zip(wides, parts):
        wide[xp, :, 0:128] = part
        if xp > 0:
            wide[xp - 1, :, 128:192] = part[:, 0:64]
        if xp + 1 < wide.shape[0]:
            wide[xp + 1, :, 192:256] = part[:, 64:128]


def row_taps(z, top, bottom):
    return down(z[:, 0:128], top) + z[:, 128:256] + up(z[:, 256:384], bottom)


def conv_block(lhs, w, top, bottom):
    n = len(lhs)
    z = [mxu(x, w[:, 0 : 384 * (n - k)]) for k, x in enumerate(lhs)]
    total = None
    for rank in range(n - 1, -1, -1):
        for k in range(rank + 1):
            j = rank - k
            part = z[k][:, 384 * j : 384 * j + 384]
            total = part if total is None else total + part
    return row_taps(total, top, bottom)


def pair_form(t0, t1, t2):
    lt = low_half(t0.shape)
    return jnp.concatenate(
        [
            jnp.where(lt, t1, t0),
            jnp.where(lt, t2, t1),
            jnp.where(lt, 0.0, t2),
            jnp.where(lt, t0, 0.0),
        ],
        axis=0,
    )


def fold_pair(acc, out, base=0):
    for dy in range(3):
        b = acc[:, 128 * dy : 128 * dy + 128]
        even, odd, nxt, prv = b[0:64], b[64:128], b[128:192], b[192:256]
        lt = low_half(even.shape)
        taps = (jnp.where(lt, prv, even), jnp.where(lt, even, odd), jnp.where(lt, odd, nxt))
        for dx in range(3):
            r = base + 64 * (3 * dy + dx)
            out[r : r + 64] = dup(taps[dx])


def near_rows(side, xp):
    first, last = max(0, 2 * xp - 1) // 8, min(side - 1, 2 * xp + 2) // 8
    shape = (8, 128)
    parity = jnp.where(low_half(shape), 0, 1)
    rows = lax.broadcasted_iota(jnp.int32, shape, 0)
    return {b: rows + (8 * b + 1 - 2 * xp) - parity for b in range(first, last + 1)}


def stem_band(stem, side, xp):
    near = near_rows(side, xp)
    zero = jnp.zeros((8, 128), F32)
    blocks = []
    for dy in range(3):
        for c in range(3):
            s = [stem[12 * dx + 4 * dy + c : 12 * dx + 4 * dy + c + 1] for dx in range(3)]
            for b in range(side // 8):
                if b not in near:
                    blocks.append(zero)
                    continue
                d = near[b]
                blocks.append(
                    jnp.where(d == 0, s[0], jnp.where(d == 1, s[1], jnp.where(d == 2, s[2], 0.0)))
                )
    return jnp.concatenate(blocks, axis=0)


def stem_rows(img, top, bottom):
    return jnp.concatenate(
        [down(img, top)[:, 0:96], img[:, 0:96], up(img, bottom)[:, 0:96]], axis=1
    )


def image_mark(img, images, at):
    row = img.reshape(images, img.shape[0] // images, 128)[:, 0, :]
    lane = lax.broadcasted_iota(jnp.int32, (images, 128), 1)
    return jnp.sum(jnp.where(lane == at, row, 0.0), axis=1, keepdims=True)


def label_onehot(img, images, classes):
    lab = image_mark(img, images, 96)
    lane = lax.broadcasted_iota(jnp.int32, (images, 128), 1)
    return jnp.where((lane.astype(F32) == lab) & (lane < classes), 1.0, 0.0)


def tree(xs):
    xs = list(xs)
    while len(xs) > 1:
        xs = [xs[k] + xs[k + 1] if k + 1 < len(xs) else xs[k] for k in range(0, len(xs), 2)]
    return xs[0]


def combine(blocks, count):
    each = count / len(blocks)
    mean = tree(b[0:1] for b in blocks) / count
    m2 = tree(b[1:2] + each * jnp.square(b[0:1] / each - mean) for b in blocks)
    return mean, lax.rsqrt(m2 / count + BN_EPS)


def stack_rows(rows, n=8):
    rows = list(rows)
    return jnp.concatenate(rows + [jnp.zeros((n - len(rows), 128), F32)], axis=0)


class Moments:
    def __init__(self):
        self.pivot, self.count = None, 0

    def add(self, x):
        if self.pivot is None:
            self.pivot = dup(row_sum(x)) / (2 * x.shape[0])
            self.first = jnp.zeros((8, 128), F32)
            self.second = jnp.zeros((8, 128), F32)
        d = x - self.pivot
        self.first = self.first + part(d)
        self.second = self.second + part(d * d)
        self.count += 2 * x.shape[0]

    def rows(self):
        off = dup(row_sum(self.first))
        return [
            off + self.pivot * self.count,
            dup(row_sum(self.second)) - off * off / self.count,
        ]


def k_weights(convs, norms, head_t, w1, w2, t1, t2, nv, hp, hpt, hb, sq):
    for k, (out, back) in enumerate(((w1, t1), (w2, t2))):
        for dy in range(3):
            taps = [both(convs[k, 3 * dy + dx]) for dx in range(3)]
            turned = [both(jnp.transpose(convs[k, 8 - 3 * dy - dx])) for dx in range(3)]
            for src, dst, n in ((taps, out, 3), (turned, back, 2)):
                for i, p in enumerate(split(pair_form(*src), n)):
                    dst[:, 384 * i + 128 * dy : 384 * i + 128 * dy + 128] = p
    nv[...] = stack_rows([both(norms[k // 2, k % 2 : k % 2 + 1]) for k in range(6)])
    classes, depth = head_t.shape
    sq[...] = jnp.zeros(sq.shape, F32)
    sq[0:classes, 0:depth] = head_t[...]
    sqv = sq[...]
    turned = jnp.transpose(sqv)
    row = lax.broadcasted_iota(jnp.int32, turned.shape, 0)
    hp[...] = jnp.where(row < depth - 1, turned, 0.0)
    hb[...] = stack_rows([turned[depth - 1 : depth]])
    hpt[...] = dup(jnp.where(low_half(sqv.shape), sqv, 0.0))


def both(w):
    return jnp.concatenate([w, w], axis=1)


def pack_image(img, n, marks):
    side = img.shape[2]
    lane = lax.broadcasted_iota(jnp.int32, (side, 32), 1)
    tail = jnp.zeros((side, 32), F32)
    for k, m in enumerate(marks):
        tail = jnp.where(lane == k, m.astype(F32), tail)
    return jnp.concatenate([img[n, 0], img[n, 1], img[n, 2], tail], axis=1)


def k_first(n, side, classes, *refs):
    labels, flips, ids, clip, vlabels, raw, vraw, stem, a0, st, img, s40, vpack = refs
    for i in range(raw.shape[0]):
        lab = jnp.where(flips[i] == 1, ids[i], labels[i])
        img[side * i : side * i + side] = pack_image(raw, i, [lab, clip[i]])
    for i in range(vraw.shape[0]):
        vpack[side * i : side * i + side] = pack_image(vraw, i, [vlabels[i]])
    s40[...] = jnp.zeros(s40.shape, F32)
    for dy in range(3):
        for dx in range(3):
            r = 12 * dx + 4 * dy
            s40[r : r + 3] = both(stem[dy, dx])
    stem_conv(n, side, img, s40[...], a0, st)
    counts = row_sum(label_onehot(img[...], raw.shape[0], classes))
    st[2:3] = counts


def k_val_stem(side, each, s40, *refs):
    blocks, (a0, st, img) = refs[:-3], refs[-3:]
    for k, b in enumerate(blocks):
        img[each * k : each * k + each] = b[8 : 8 + each]
    stem_conv(1, side, img, s40[...], a0, st)


def stem_conv(n, side, img, stem, a0, st):
    rows = img.shape[0]
    pairs = a0.shape[0]
    top, bottom = edges(rows, side)
    parts = split(stem_rows(img[...], top, bottom), n)
    lhs = jnp.concatenate([parts[i] for i, _ in TERMS[n]], axis=1)
    moments = Moments()
    for xp in range(0, pairs, 2):
        band = jnp.concatenate([stem_band(stem, side, xp), stem_band(stem, side, xp + 1)], axis=1)
        rhs = split(band, n)
        z = mxu(lhs, jnp.concatenate([rhs[j] for _, j in TERMS[n]], axis=0))
        a0[xp] = z[:, 0:128].astype(a0.dtype)
        a0[xp + 1] = z[:, 128:256].astype(a0.dtype)
        moments.add(z[:, 0:128])
        moments.add(z[:, 128:256])
    st[...] = stack_rows(moments.rows())


SHARDS, CONV_ROWS, SMALL_ROWS = 8, 72, 16
SHARD_ROWS = CONV_ROWS + SMALL_ROWS
NORM_AT = SHARDS * SHARD_ROWS
PACKED = (NORM_AT + 8, 128)


def pack_params(stem_of, convs, norm_of, head_of, out, sq, small):
    out[NORM_AT : NORM_AT + 8] = jnp.zeros((8, 128), F32)
    for k in range(3):
        out[NORM_AT + 2 * k : NORM_AT + 2 * k + 2, 0:64] = norm_of(k)
    sq[...] = jnp.zeros(sq.shape, F32)
    head_t = head_of()
    sq[64 : 64 + head_t.shape[0], 0 : head_t.shape[1]] = head_t
    small[...] = jnp.transpose(sq[...])
    for dx in range(3):
        for dy in range(3):
            r = 12 * dx + 4 * dy
            small[r : r + 3, 0:64] = stem_of(dy, dx)
    for s in range(SHARDS):
        at = SHARD_ROWS * s
        for t in range(9):
            out[at + 8 * t : at + 8 * t + 8] = jnp.concatenate(
                [convs[0, t, 8 * s : 8 * s + 8], convs[1, t, 8 * s : 8 * s + 8]], axis=1
            )
        out[at + CONV_ROWS : at + SHARD_ROWS] = small[SMALL_ROWS * s : SMALL_ROWS * s + SMALL_ROWS]


def k_params(*refs):
    ins, outs, sq, small = refs[:16], refs[16:20], refs[20], refs[21]
    for k in range(4):
        stem, convs, norms, head = ins[4 * k : 4 * k + 4]
        own = k in (1, 2)
        pack_params(
            (lambda dy, dx, r=stem: r[dy, dx, :, 0, :]) if own else (lambda dy, dx, r=stem: r[dy, dx]),
            convs,
            lambda i, r=norms: r[i],
            (lambda r=head: r[:, 0, :]) if own else (lambda r=head: r[...]),
            outs[k],
            sq,
            small,
        )


def k_halves(even, got, *outs):
    for k, out in enumerate(outs):
        out[...] = even[k] + got[k]


def adam(q, p, m, v):
    first = 0.9 * m + 0.1 * q
    second = 0.999 * v + 0.001 * q * q
    step = first / (1.0 - 0.9**STEP) / (jnp.sqrt(second / (1.0 - 0.999**STEP)) + 1e-08) + 0.01 * p
    return first, second, 0.05 * step


def k_adam(count, nb, me, *refs):
    parts, refs = refs[:4], refs[4:]
    stat, refs = refs[:nb], refs[nb:]
    pp, pm, pv, vec0, grad, delta, rest, px, ps = refs
    total = tree([r[...] for r in parts])
    r8 = total[SHARD_ROWS : SHARD_ROWS + 8]
    rest[...] = r8
    st = tree([r[...] for r in stat])
    px[...] = jnp.zeros(px.shape, F32)
    ps[...] = jnp.zeros(ps.shape, F32)
    px[0:40] = st[8:48]
    ps[0:40] = st[48:88]
    at = pl.ds(pl.multiple_of(SMALL_ROWS * me[0], 8), SMALL_ROWS)
    gain = vec0[2:3] * vec0[1:2]
    sm = total[CONV_ROWS:SHARD_ROWS]
    fixed = gain * (sm - ps[at] * (r8[0:1] / count) - px[at] * (r8[1:2] / count))
    sm = jnp.where(low_half(sm.shape), fixed, sm)
    q = jnp.concatenate([total[0:CONV_ROWS], sm], axis=0)
    qn = stack_rows([r8[k : k + 1] for k in (1, 0, 3, 2, 5, 4)])
    grad[0:SHARD_ROWS] = q
    grad[SHARD_ROWS : SHARD_ROWS + 8] = qn
    at = pl.ds(pl.multiple_of(SHARD_ROWS * me[0], 8), SHARD_ROWS)
    delta[0:SHARD_ROWS] = adam(q, pp[at], pm[at], pv[at])[2]
    at = slice(NORM_AT, NORM_AT + 8)
    delta[SHARD_ROWS : SHARD_ROWS + 8] = adam(qn, pp[at], pm[at], pv[at])[2]


def k_total(ng, grad, *refs):
    deltas, (pay, norm) = refs[:ng], refs[ng:]
    total = tree([d[...] for d in deltas])
    pay[0:SHARD_ROWS] = grad[0:SHARD_ROWS]
    pay[SHARD_ROWS : 2 * SHARD_ROWS] = total[0:SHARD_ROWS]
    norm[0:8] = grad[SHARD_ROWS : SHARD_ROWS + 8]
    norm[8:16] = total[SHARD_ROWS : SHARD_ROWS + 8]


def k_update(groups, classes, me, *refs):
    pays, (norm, rest, pp, pm, pv, mom), refs = refs[:8], refs[8:14], refs[14:]
    news, lows, firsts, seconds, outers, loss = (
        refs[0:4],
        refs[4:8],
        refs[8:12],
        refs[12:16],
        refs[16:20],
        refs[20],
    )
    grad, delta = refs[21:]
    for j, pay in enumerate(pays):
        s = jnp.bitwise_xor(me[0], j)
        at = pl.ds(pl.multiple_of(SHARD_ROWS * s, 8), SHARD_ROWS)
        grad[at] = pay[0:SHARD_ROWS]
        delta[at] = pay[SHARD_ROWS : 2 * SHARD_ROWS]
    grad[NORM_AT : NORM_AT + 8] = norm[0:8]
    delta[NORM_AT : NORM_AT + 8] = norm[8:16]
    p = pp[...]
    first, second, _ = adam(grad[...], p, pm[...], pv[...])
    average = delta[...] / groups
    outer = 0.9 * mom[...] + average
    new = p - 0.7 * (average + 0.9 * outer)
    unpack(new, news, False)
    unpack(new, lows, False)
    unpack(outer, outers, False)
    unpack(first, firsts, True)
    unpack(second, seconds, True)
    loss[...] = rest[6, 0:1]


def unpack(x, outs, own):
    stem, convs, norms, head = outs
    dt = convs.dtype
    smalls = []
    for s in range(SHARDS):
        at = SHARD_ROWS * s
        for t in range(9):
            blk = x[at + 8 * t : at + 8 * t + 8].astype(dt)
            convs[0, t, 8 * s : 8 * s + 8] = blk[:, 0:64]
            convs[1, t, 8 * s : 8 * s + 8] = blk[:, 64:128]
        smalls.append(x[at + CONV_ROWS : at + SHARD_ROWS])
    small = jnp.concatenate(smalls, axis=0)
    turned = jnp.transpose(small)
    classes, depth = head.shape[0], head.shape[-1]
    head_t = turned[64 : 64 + classes, 0:depth].astype(dt)
    if own:
        for k in range(classes):
            head[k] = head_t[k : k + 1]
    else:
        head[...] = head_t
    for dy in range(3):
        for dx in range(3):
            r = 12 * dx + 4 * dy
            if own:
                for c in range(3):
                    stem[dy, dx, c] = small[r + c : r + c + 1, 0:64].astype(dt)
            else:
                stem[dy, dx] = small[r : r + 3, 0:64].astype(dt)
    for k in range(3):
        norms[k] = x[NORM_AT + 2 * k : NORM_AT + 2 * k + 2, 0:64].astype(dt)


def k_conv(n, side, nb, layer, count, carried, *refs):
    a_in, nv = refs[0], refs[1]
    blocks, w = refs[2 : 2 + nb], refs[2 + nb]
    refs = refs[3 + nb :]
    riders, refs = refs[:carried], refs[carried:]
    a_out, st, vec = refs[:3]
    wides = refs[3:]
    pairs, rows = a_in.shape[0], a_in.shape[1]
    if riders:
        sums, vec0, s0 = riders
        ones = sums[40:80]
        local = s0[0:1] / (rows * pairs * 2)
        st[8:48] = vec0[1:2] * (sums[0:40] - (vec0[0:1] - local) * ones)
        st[48:88] = ones
    top, bottom = edges(rows, side)
    bl = [b[0:8] for b in blocks]
    mean, r = combine(bl, count)
    gain, bias = nv[2 * layer : 2 * layer + 1], nv[2 * layer + 1 : 2 * layer + 2]
    counts = tree(b[2:3] for b in bl)
    scale = gain * r
    vec[...] = stack_rows([mean, r, gain, bias, counts, scale])
    for wide in wides:
        zero_ends(wide)

    def prep(xp):
        h = jnp.maximum((a_in[xp].astype(F32) - mean) * scale + bias, 0.0)
        put(wides, xp, split(h, n))

    prep(0)
    moments = Moments()
    for xp in range(pairs):
        if xp + 1 < pairs:
            prep(xp + 1)
        out = conv_block([wide[xp] for wide in wides], w, top, bottom)
        a_out[xp] = out.astype(a_out.dtype)
        moments.add(out)
    st[0:8] = stack_rows(moments.rows())


def bn(a, vec):
    d = a.astype(F32) - vec[0:1]
    return d * vec[1:2], d * vec[5:6] + vec[3:4]


def k_head(val, side, nb, count, classes, group_count, *refs):
    a2, a0, vec0r, nv, img, hp, hpt, hb = refs[:8]
    blocks = refs[8 : 8 + nb]
    mz, vec2r, info, extra = refs[8 + nb :]
    pairs, rows = a2.shape[0], a2.shape[1]
    images = rows // side
    mean, r = combine([b[0:8] for b in blocks], count)
    zero = jnp.zeros((1, 128), F32)
    vec2 = stack_rows([mean, r, nv[4:5], nv[5:6], zero, nv[4:5] * r])
    vec2r[...] = vec2
    vec0 = vec0r[...]
    zs = jnp.zeros((images, 8, 128), F32)
    ms = jnp.zeros((images, 8, 128), F32)
    xs = jnp.zeros((images, 8, 128), F32)
    for xp in range(pairs):
        xh2, y2 = bn(a2[xp], vec2)
        z = y2 + jnp.maximum(bn(a0[xp], vec0)[1], 0.0)
        on = z > 0
        m = jnp.where(on, 1.0, 0.0)
        mz[xp] = m.astype(BF16)
        zs = zs + image_part(jnp.maximum(z, 0.0), images)
        ms = ms + image_part(m, images)
        xs = xs + image_part(jnp.where(on, xh2, 0.0), images)
    zs, ms, xs = (jnp.sum(v, axis=1) for v in (zs, ms, xs))
    area = side * pairs * 2
    lt = low_half((images, 128))
    pooled, ms, xs = dup(zs) / area, dup(ms), dup(xs)
    logits = lax.dot(pooled, hp[...], precision=HIGH) + hb[0:1]
    lane = lax.broadcasted_iota(jnp.int32, (images, 128), 1)
    ok = lane < classes
    top = jnp.max(jnp.where(ok, logits, -3e38), axis=1, keepdims=True)
    e = jnp.where(ok, jnp.exp(jnp.where(ok, logits - top, 0.0)), 0.0)
    tot = jnp.sum(e, axis=1, keepdims=True)
    onehot = label_onehot(img[...], images, classes)
    pm = e / tot - onehot
    ce = jnp.log(tot) + top - jnp.sum(onehot * logits, axis=1, keepdims=True)
    g = lax.dot(pm, hpt[...], precision=HIGH)
    if val:
        n_val = group_count
        gp = g / (n_val * area)
        info[...] = gp
        head = lax.dot_general(
            pooled, pm / n_val, (((0,), (0,)), ((), ())), precision=HIGH
        )
        extra[0:64] = head[0:64]
        extra[64:72] = stack_rows([row_sum(pm) / n_val])
        extra[72:80] = stack_rows([row_sum(gp * ms), row_sum(gp * xs)])
    else:
        cw = group_count / (classes * (vec0[4:5] + 1.0))
        per = jnp.sum(onehot * cw, axis=1, keepdims=True)
        uw = jnp.where(lt, g * ms, g * xs)
        pc = jnp.where(lane == 0, per, jnp.where(lane == 1, image_mark(img[...], images, 97), 0.0))
        extra[0:images] = uw
        extra[images : 2 * images] = pc
        for k, v in enumerate((g, ms, xs, pooled, pm, jnp.broadcast_to(ce, (images, 128)))):
            info[k] = v


def k_static(side, img, a0, s0, out):
    pairs, rows = a0.shape[0], a0.shape[1]
    top, bottom = edges(rows, side)
    mean = s0[0:1] / (rows * pairs * 2)
    whole = stem_rows(img[...], top, bottom)
    lhs = turned_rows(split(whole, 2))
    out[0:40] = stem_grad(side, pairs, lhs, lambda xp: split(a0[xp] - mean, 2))[0]
    out[40:80] = patch_sums(side, whole)


def turned_rows(parts):
    return [jnp.transpose(p) for p in parts]


def stem_grad(side, pairs, lhs, *rhs_of):
    n = len(lhs)
    accs = [{} for _ in rhs_of]
    columns = [(q, xp) for xp in range(pairs) for q in range(len(rhs_of))]
    for at in range(0, len(columns), 2):
        two = columns[at : at + 2]
        parts = [rhs_of[q](xp) for q, xp in two]
        rhs = [jnp.concatenate([p[i] for p in parts], axis=1) for i in range(n)]
        f = None
        for i, j in TERMS[n]:
            t = mxu(lhs[i], rhs[j])
            f = t if f is None else f + t
        for place, (q, xp) in enumerate(two):
            near = near_rows(side, xp)
            for k in range(9):
                for b, d in near.items():
                    r = side * k + 8 * b
                    blk = f[r : r + 8, 128 * place : 128 * place + 128]
                    for dx in range(3):
                        v = jnp.where(d == dx, blk, 0.0)
                        key = (dx, k)
                        accs[q][key] = accs[q][key] + v if key in accs[q] else v
    outs = []
    zero = jnp.zeros((1, 128), F32)
    for acc in accs:
        rows = []
        for dx in range(3):
            for dy in range(3):
                rows += [dup(row_sum(acc[dx, 3 * dy + c])) for c in range(3)] + [zero]
        outs.append(jnp.concatenate(rows + [zero] * 4, axis=0))
    return outs


def patch_sums(side, whole):
    sums = row_sum(whole)
    col = jnp.transpose(jnp.broadcast_to(sums, (8, sums.shape[1])))[:, 0:1]
    xin = lax.rem(lax.broadcasted_iota(jnp.int32, col.shape, 0), side)
    rows = []
    for dx in range(3):
        keep = xin <= side - 2 if dx == 0 else (xin >= 1 if dx == 2 else xin >= 0)
        c = jnp.where(keep, col, 0.0)
        for k in range(12):
            if k % 4 == 3:
                rows.append(jnp.zeros((1, 128), F32))
                continue
            r = side * (3 * (k // 4) + k % 4)
            rows.append(jnp.broadcast_to(row_sum(c[r : r + side]), (1, 128)))
    return jnp.concatenate(rows + [jnp.zeros((4, 128), F32)], axis=0)


def back_of_norm2(gp, vec2, s1, s2, count, side, a2, mz):
    images, rows = gp.shape[0], a2.shape[1]
    k2 = vec2[2:3] * vec2[1:2]
    c0, c1 = k2 * s1 / count, k2 * s2 / count
    gk = jnp.broadcast_to((gp * k2)[:, None, :], (images, side, 128)).reshape(rows, 128)

    c1 = c1 * vec2[1:2]
    c0 = c0 - vec2[0:1] * c1

    def at(xp):
        return mz[xp].astype(F32) * gk - (a2[xp].astype(F32) * c1 + c0)

    return at


def back_of_norm1(vec1, s1, s2, count, dy1, a1):
    k1 = vec1[2:3] * vec1[1:2]
    c0, c1 = k1 * s1 / count, k1 * s2 / count

    c1 = c1 * vec1[1:2]
    c0 = c0 - vec1[0:1] * c1

    def at(xp):
        return dy1[xp].astype(F32) * k1 - (a1[xp].astype(F32) * c1 + c0)

    return at


def back_conv2(n, side, gp, vec2, s1, s2, count, a2, mz, a1, vec1, wt, wides, dy1, extra):
    pairs, rows = a2.shape[0], a2.shape[1]
    images = rows // side
    top, bottom = edges(rows, side)
    for wide in wides:
        zero_ends(wide)
    back_at = back_of_norm2(gp, vec2, s1, s2, count, side, a2, mz)

    def prep(xp):
        back = back_at(xp)
        parts = split(back, n)
        put(wides, xp, parts)
        if extra is not None:
            extra(xp, back, parts)

    prep(0)
    q1 = jnp.zeros((8, 128), F32)
    q2 = jnp.zeros((8, 128), F32)
    for xp in range(pairs):
        if xp + 1 < pairs:
            prep(xp + 1)
        dh = conv_block([wide[xp] for wide in wides], wt, top, bottom)
        xh1, y1 = bn(a1[xp], vec1)
        dy = jnp.where(y1 > 0, dh, 0.0)
        dy1[xp] = dy.astype(dy1.dtype)
        q1 = q1 + part(dy)
        q2 = q2 + part(dy * xh1)
    return dup(row_sum(q1)), dup(row_sum(q2))


def shifted(back, top, bottom):
    return jnp.concatenate([up(back, bottom), back, down(back, top)], axis=1)


def k_val_back2(side, nb, count, *refs):
    a2, mz, a1, vec2r, vec1r, gp, wt, wide1 = refs[:8]
    blocks = refs[8 : 8 + nb]
    dy1, st, g2 = refs[8 + nb : 11 + nb]
    wide, acc = refs[11 + nb :]
    wides = (wide,)
    rows = a2.shape[1]
    top, bottom = edges(rows, side)
    s1 = tree(b[72:73] for b in blocks)
    s2 = tree(b[73:74] for b in blocks)
    acc[...] = jnp.zeros(acc.shape, F32)

    def extra(xp, back, parts):
        acc[...] += mxu_t(shifted(back, top, bottom).astype(BF16), wide1[xp])

    q1, q2 = back_conv2(
        1, side, gp[...], vec2r[...], s1, s2, count, a2, mz, a1, vec1r[...], wt, wides, dy1, extra
    )
    fold_pair(jnp.transpose(acc[...]), g2)
    st[...] = stack_rows([q1, q2, s1, s2])


def back_conv1(n, side, gp, vec1, vec0, s1, s2, count, dy1, a1, a0, mz, wt, wides, dy0, extra):
    pairs, rows = a1.shape[0], a1.shape[1]
    images = rows // side
    top, bottom = edges(rows, side)
    for wide in wides:
        zero_ends(wide)
    back_at = back_of_norm1(vec1, s1, s2, count, dy1, a1)
    gpr = jnp.broadcast_to(gp[:, None, :], (images, side, 128)).reshape(rows, 128)

    def prep(xp):
        back = back_at(xp)
        parts = split(back, n)
        put(wides, xp, parts)
        if extra is not None:
            extra(xp, back, parts)

    prep(0)
    q1 = jnp.zeros((8, 128), F32)
    q2 = jnp.zeros((8, 128), F32)
    for xp in range(pairs):
        if xp + 1 < pairs:
            prep(xp + 1)
        dh = conv_block([wide[xp] for wide in wides], wt, top, bottom)
        xh0, y0 = bn(a0[xp], vec0)
        dy = jnp.where(y0 > 0, dh + mz[xp].astype(F32) * gpr, 0.0)
        dy0[xp] = dy.astype(dy0.dtype)
        q1 = q1 + part(dy)
        q2 = q2 + part(dy * xh0)
    return dup(row_sum(q1)), dup(row_sum(q2))


def k_val_back1(side, nb, count, *refs):
    dy1, a1, a0, mz, vec1r, vec0r, gp, wt, wide0, img = refs[:10]
    blocks = refs[10 : 10 + nb]
    g1, small = refs[10 + nb : 12 + nb]
    wide, acc, dy0 = refs[12 + nb :]
    wides = (wide,)
    pairs, rows = a1.shape[0], a1.shape[1]
    top, bottom = edges(rows, side)
    s1 = tree(b[0:1] for b in blocks)
    s2 = tree(b[1:2] for b in blocks)
    acc[...] = jnp.zeros(acc.shape, F32)
    vec0 = vec0r[...]

    def extra(xp, back, parts):
        acc[...] += mxu_t(shifted(back, top, bottom).astype(BF16), wide0[xp])

    q1, q2 = back_conv1(
        1, side, gp[...], vec1r[...], vec0, s1, s2, count, dy1, a1, a0, mz, wt, wides, dy0, extra
    )
    fold_pair(jnp.transpose(acc[...]), g1)
    whole = stem_rows(img[...], top, bottom)
    small[0:40], small[40:80] = stem_grad(
        side,
        pairs,
        turned_rows([whole.astype(BF16)]),
        lambda xp: [dy0[xp]],
        lambda xp: [((a0[xp].astype(F32) - vec0[0:1]) * vec0[1:2]).astype(BF16)],
    )
    small[80:120] = patch_sums(side, whole)
    small[120:128] = stack_rows([q1, q2])


def k_tan1(side, nb, nv_blocks, count, count_val, *refs):
    img, a0, a1, vec0r, vec1r, w1, vvec0r = refs[:7]
    refs = refs[7:]
    stat = refs[:nb]
    refs = refs[nb:]
    smalls, g1s, sts = refs[:nv_blocks], refs[nv_blocks : 2 * nv_blocks], refs[2 * nv_blocks : 3 * nv_blocks]
    t1, th0, st, wide, wide0, v1 = refs[3 * nv_blocks :]
    pairs, rows = a1.shape[0], a1.shape[1]
    top, bottom = edges(rows, side)
    vec0, vec1, vv0 = vec0r[...], vec1r[...], vvec0r[...]
    small = sum(b[...] for b in smalls)
    q1, q2 = small[120:121], small[121:122]
    v0 = (
        vv0[2:3]
        * vv0[1:2]
        * (small[0:40] - small[80:120] * (q1 / count_val) - small[40:80] * (q2 / count_val))
    )
    static = tree(b[...] for b in stat)
    u1 = row_sum(v0 * static[48:88])
    u2 = row_sum(v0 * static[8:48])
    k0 = vec0[2:3] * vec0[1:2]
    e0 = q1 - k0 * u1 / count
    e1 = q2 - k0 * u2 / count
    for dy in range(3):
        taps = []
        for dx in range(3):
            r = 64 * (3 * dy + dx)
            taps.append(sum(g[r : r + 64] for g in g1s))
        v1[:, 128 * dy : 128 * dy + 128] = pair_form(*taps).astype(BF16)
    zero_ends(wide)
    zero_ends(wide0)
    lhs = stem_rows(img[...], top, bottom).astype(BF16)
    tang = {}

    def prep(xp):
        if xp % 2 == 0:
            band = jnp.concatenate(
                [stem_band(v0, side, xp), stem_band(v0, side, xp + 1)], axis=1
            ).astype(BF16)
            z = mxu(lhs, band)
            tang[xp], tang[xp + 1] = z[:, 0:128], z[:, 128:256]
        xh0, y0 = bn(a0[xp], vec0)
        th = jnp.where(y0 > 0, k0 * tang.pop(xp) + e1 * xh0 + e0, 0.0).astype(BF16)
        th0[xp] = th
        put((wide, wide0), xp, [th, jnp.maximum(y0, 0.0).astype(BF16)])

    prep(0)
    p1 = jnp.zeros((8, 128), F32)
    p2 = jnp.zeros((8, 128), F32)
    for xp in range(pairs):
        if xp + 1 < pairs:
            prep(xp + 1)
        t = row_taps(mxu(wide[xp], w1[:, 0:384]) + mxu(wide0[xp], v1[...]), top, bottom)
        t1[xp] = t
        xh1 = (a1[xp] - vec1[0:1]) * vec1[1:2]
        p1 = p1 + part(t)
        p2 = p2 + part(t * xh1)
    vs = [sum(b[k : k + 1] for b in sts) for k in range(2)]
    st[...] = stack_rows([dup(row_sum(p1)), dup(row_sum(p2)), vs[0], vs[1], sts[0][2:3], sts[0][3:4]])


def k_tan2(side, nb, nv_blocks, count, *refs):
    t1, th0, a1, a2, mz, vec1r, vec2r, w2, info, own, gather = refs[:11]
    refs = refs[11:]
    blocks = refs[:nb]
    refs = refs[nb:]
    g2s, heads = refs[:nv_blocks], refs[nv_blocks : 2 * nv_blocks]
    st, wide, wide1, v2 = refs[2 * nv_blocks :]
    pairs, rows = a1.shape[0], a1.shape[1]
    images = rows // side
    top, bottom = edges(rows, side)
    vec1, vec2 = vec1r[...], vec2r[...]
    u1 = tree(b[0:1] for b in blocks)
    u2 = tree(b[1:2] for b in blocks)
    k1 = vec1[2:3] * vec1[1:2]
    e0 = own[2:3] - k1 * u1 / count
    e1 = own[3:4] - k1 * u2 / count
    for dy in range(3):
        taps = []
        for dx in range(3):
            r = 64 * (3 * dy + dx)
            taps.append(sum(g[r : r + 64] for g in g2s))
        v2[:, 128 * dy : 128 * dy + 128] = pair_form(*taps).astype(BF16)
    zero_ends(wide)
    zero_ends(wide1)

    def prep(xp):
        xh1, y1 = bn(a1[xp], vec1)
        th = jnp.where(y1 > 0, k1 * t1[xp] + e1 * xh1 + e0, 0.0).astype(BF16)
        put((wide, wide1), xp, [th, jnp.maximum(y1, 0.0).astype(BF16)])

    prep(0)
    p1 = jnp.zeros((8, 128), F32)
    p2 = jnp.zeros((8, 128), F32)
    asum = jnp.zeros((images, 8, 128), F32)
    k2 = vec2[2:3] * vec2[1:2]
    for xp in range(pairs):
        if xp + 1 < pairs:
            prep(xp + 1)
        t = row_taps(mxu(wide[xp], w2[:, 0:384]) + mxu(wide1[xp], v2[...]), top, bottom)
        xh2 = (a2[xp] - vec2[0:1]) * vec2[1:2]
        p1 = p1 + part(t)
        p2 = p2 + part(t * xh2)
        m = mz[xp].astype(F32)
        asum = asum + image_part(m * (k2 * t + th0[xp].astype(F32)), images)
    asum = dup(jnp.sum(asum, axis=1))
    area = side * pairs * 2
    g, ms, xs, pooled, pm = (info[k] for k in range(5))
    inner = g * (asum + own[5:6] * xs + own[4:5] * ms)
    base = jnp.sum(jnp.where(low_half(inner.shape), inner, 0.0), axis=1, keepdims=True) / area
    vhead = sum(h[0:72] for h in heads)
    vh = jnp.concatenate([vhead[0:64], jnp.zeros((64, 128), F32)], axis=0)
    lin = lax.dot(pooled, vh, precision=HIGH) + vhead[64:65]
    base = base + jnp.sum(pm * lin, axis=1, keepdims=True)
    st[0:images] = jnp.broadcast_to(base, (images, 128))
    p1, p2 = dup(row_sum(p1)), dup(row_sum(p2))
    st[images : images + 8] = stack_rows([jnp.where(low_half(p1.shape), p1, p2)])
    st[images + 8 :] = gather[...]


def k_train_back2(side, nb, count, group_count, n, *refs):
    flag, a2, mz, a1, vec2r, vec1r, wt, info = refs[:8]
    refs = refs[8:]
    dyn = refs[:nb]
    dy1, st, wgp = refs[nb : nb + 3]
    wides = refs[nb + 3 :]
    pairs, rows = a2.shape[0], a2.shape[1]
    images = rows // side
    area = side * pairs * 2
    vec2 = vec2r[...]
    k2 = vec2[2:3] * vec2[1:2]
    each = dyn[0].shape[0]
    at = images + 8
    tsum = 0.0
    for b in range(nb):
        for j in range(each):
            tsum = tsum + dyn[b][j, images : images + 1]
    tt = tsum * k2 / (count * area)
    raws, pers = [], []
    total = jnp.zeros((1, 1), F32)
    mag = jnp.zeros((1, 1), F32)
    for b in range(nb):
        for j in range(each):
            uw = dyn[b][j, at : at + images]
            pc = dyn[b][j, at + images : at + 2 * images]
            per, clip = pc[:, 0:1], pc[:, 1:2]
            tan = dyn[b][j, 0:images, 0:1] - jnp.sum(uw * tt, axis=1, keepdims=True)
            score = -ALPHA * per * tan
            raw = clip * jnp.maximum(-score, 0.0)
            total = total + row_sum(raw)
            mag = mag + row_sum(clip * jnp.abs(score))
            raws.append(raw)
            pers.append(per)
    on = flag[0] == 1
    denom = jnp.maximum(total, 0.25 * mag) + 1e-06
    ssum = jnp.zeros((1, 128), F32)
    k = 0
    own = None
    for b in range(nb):
        for j in range(each):
            w = jnp.where(on, raws[k] / denom, 1.0 / group_count) * pers[k]
            own = w if own is None else own
            ssum = ssum + row_sum(w * dyn[b][j, at : at + images])
            k += 1
    ssum = ssum / area
    lt = low_half(ssum.shape)
    s1, s2 = dup(jnp.where(lt, ssum, 0.0)), dup(jnp.where(lt, 0.0, ssum))
    g, pooled, pm, ce = info[0], info[3], info[4], info[5]
    gp = own * g / area
    wgp[0:images] = gp
    head = lax.dot_general(pooled, own * pm, (((0,), (0,)), ((), ())), precision=HIGH)
    wgp[images : images + 64] = head[0:64]
    mine = row_sum(own * dyn[0][0, at : at + images]) / area
    o1, o2 = dup(jnp.where(lt, mine, 0.0)), dup(jnp.where(lt, 0.0, mine))
    wgp[images + 64 : images + 72] = stack_rows([row_sum(own * pm), row_sum(own * ce), o1, o2])

    wgp[images + 72 : images + 80] = stack_rows([s1, s2])
    q1, q2 = back_conv2(
        n, side, gp, vec2, s1, s2, count, a2, mz, a1, vec1r[...], wt, wides, dy1, None
    )
    st[...] = stack_rows([q1, q2])


def k_train_back1(side, nb, n, count, me, *refs):
    dy1, a1, a0, mz, vec1r, vec0r, wt, img, wgp, d2, st1 = refs[:11]
    blocks = refs[11 : 11 + nb]
    even, odd, acc, d1, small, dy0 = refs[11 + nb : 17 + nb]
    wides, inputs = refs[17 + nb : 17 + nb + n], refs[17 + nb + n :]
    pairs, rows = a1.shape[0], a1.shape[1]
    images = rows // side
    top, bottom = edges(rows, side)
    s1 = tree(b[0:1] for b in blocks)
    s2 = tree(b[1:2] for b in blocks)
    vec0 = vec0r[...]
    acc[...] = jnp.zeros(acc.shape, F32)
    for wide in inputs:
        zero_ends(wide)
    held = {}

    def gradient(xp):
        lhs = split(shifted(held.pop(xp), top, bottom), n)
        t = None
        for i, j in TERMS[n]:
            d = mxu_t(lhs[i], inputs[j][xp])
            t = d if t is None else t + d
        acc[...] += t

    def extra(xp, back, parts):
        put(inputs, xp, split(jnp.maximum(bn(a0[xp], vec0)[1], 0.0), n))
        held[xp] = back
        if xp > 0:
            gradient(xp - 1)

    q1, q2 = back_conv1(
        n, side, wgp[0:images], vec1r[...], vec0, s1, s2, count, dy1, a1, a0, mz, wt, wides, dy0, extra
    )
    gradient(pairs - 1)
    fold_pair(jnp.transpose(acc[...]), d1)
    lhs = turned_rows(split(stem_rows(img[...], top, bottom), n))
    stem = stem_grad(side, pairs, lhs, lambda xp: split(dy0[xp], n))[0]
    small[...] = jnp.zeros((128, 128), F32)
    small[0:65] = wgp[images : images + 65]
    right = pltpu.roll(small[...], 64, 1)
    small[...] = jnp.zeros((128, 128), F32)
    small[0:40] = stem
    small[...] = jnp.where(low_half((128, 128)), small[...], right)
    rest = stack_rows(
        [q1, q2, st1[0:1], st1[1:2]] + [wgp[images + k : images + k + 1] for k in (66, 67, 65)]
    )
    lt8 = low_half((8, 128))
    for j in range(SHARDS):
        s = jnp.bitwise_xor(me[0], j)
        dst = (even, odd)[j % 2]
        k = j // 2
        for t in range(9):
            at = pl.ds(pl.multiple_of(64 * t + 8 * s, 8), 8)
            dst[k, 8 * t : 8 * t + 8] = jnp.where(lt8, d1[at], d2[at])
        dst[k, CONV_ROWS:SHARD_ROWS] = small[pl.ds(pl.multiple_of(SMALL_ROWS * s, 8), SMALL_ROWS)]
        dst[k, SHARD_ROWS : SHARD_ROWS + 8] = rest


def weight_gradient(side, n, a, vec, back_at, wides, acc, g):
    pairs, rows = a.shape[0], a.shape[1]
    top, bottom = edges(rows, side)
    acc[...] = jnp.zeros(acc.shape, F32)
    for wide in wides:
        zero_ends(wide)

    def prep(xp):
        put(wides, xp, split(jnp.maximum(bn(a[xp], vec)[1], 0.0), n))

    prep(0)
    for xp in range(pairs):
        if xp + 1 < pairs:
            prep(xp + 1)
        lhs = split(shifted(back_at(xp), top, bottom), n)
        t = None
        for i, j in TERMS[n]:
            d = mxu_t(lhs[i], wides[j][xp])
            t = d if t is None else t + d
        acc[...] += t
    fold_pair(jnp.transpose(acc[...]), g)


def k_dw2(side, n, count, a1, vec1, a2, vec2, mz, wgp, g, acc, *wides):
    images = a1.shape[1] // side
    at = images + 72
    back_at = back_of_norm2(
        wgp[0:images], vec2[...], wgp[at : at + 1], wgp[at + 1 : at + 2], count, side, a2, mz
    )
    weight_gradient(side, n, a1, vec1[...], back_at, wides, acc, g)


VM = pl.BlockSpec(memory_space=pltpu.VMEM)
SM = pl.BlockSpec(memory_space=pltpu.SMEM)


def call(kernel, outs, args, scratch=(), smem=(), raw=(), us=1.0, after=()):
    count = len(args)

    def run(*refs):
        kernel(*refs[:count], *refs[count + len(after) :])

    def placed(i, x):
        if i in raw:
            return pltpu.with_memory_space_constraint(x, pltpu.HBM)
        return pltpu.with_memory_space_constraint(x, pltpu.VMEM) if x.size >= KEEP else x

    return pl.pallas_call(
        run,
        out_shape=[
            pltpu.VMEM(s, d) if math.prod(s) >= KEEP else jax.ShapeDtypeStruct(s, d)
            for s, d in outs
        ],
        in_specs=[SM if i in smem else VM for i in range(count)]
        + [pl.BlockSpec(memory_space=pl.ANY)] * len(after),
        out_specs=[VM] * len(outs),
        scratch_shapes=[pltpu.VMEM(s, d) for s, d in scratch],
        compiler_params=pltpu.CompilerParams(vmem_limit_bytes=VMEM_BYTES),
        cost_estimate=pl.CostEstimate(
            flops=int(us * 1.1e9), bytes_accessed=1 << 16, transcendentals=0
        ),
    )(*[placed(i, x) for i, x in enumerate(args)], *[placed(-1, x) for x in after])


def swap(x, k, n):
    return lax.ppermute(x, "dp", [(i, i ^ k) for i in range(n)])


def add(a, b, step):
    return a + b


def chan(count, a, b, step):
    d = a[0:1] - b[0:1]
    cross = d * d / (2.0 * count * step)
    return a + b + jnp.pad(cross, ((1, a.shape[0] - 2), (0, 0)))


def near(x, team, merge):
    n = lax.axis_size("dp")
    k = 1
    while k < team // 2:
        x = merge(x, swap(x, k, n), k)
        k *= 2
    return [x, swap(x, k, n)] if team > 1 else [x]


def far(x, merge, rider=None):
    n = lax.axis_size("dp")
    k = 1
    while k < n // 4:
        x = merge(x, swap(x, k, n), k)
        k *= 2
    if rider is not None:
        x = jnp.concatenate([x, rider], axis=0)
    return [x] + [swap(x, j * k + 1, n) for j in range(1, n // k)]


def far_list(x):
    n = lax.axis_size("dp")
    x = x[None]
    k = 1
    while k < n // 4:
        x = jnp.concatenate([x, swap(x, k, n)], axis=0)
        k *= 2
    return [x] + [swap(x, j * k + 1, n) for j in range(1, n // k)]


def body(
    train_images,
    train_labels,
    flip_flags,
    class_ids,
    clip_mask,
    norm_flag,
    val_images,
    val_labels,
    stem,
    convs,
    norms,
    head,
    m_stem,
    v_stem,
    m_convs,
    v_convs,
    m_norms,
    v_norms,
    m_head,
    v_head,
    mom_stem,
    mom_convs,
    mom_norms,
    mom_head,
):
    dp = lax.axis_size("dp")
    classes = head.shape[1]
    side, pairs = train_images.shape[1], train_images.shape[2] // 2
    images, val_each = train_images.shape[0], val_images.shape[0]
    group_train, group_val = dp * images, dp * val_each
    team = max(2, group_val // 16)
    rows, vrows = images * side, side * group_val // team
    vimages = group_val // team
    count, count_val = group_train * side * pairs * 2, group_val * side * pairs * 2
    nt, nval = 3, 1

    act = (pairs, rows, 128)
    st = ((8, 128), F32)
    square = ((128, 128), F32)

    def planes(img):
        return jnp.transpose(img, (0, 3, 1, 2))

    me = lax.rem(lax.axis_index("dp"), SHARDS).astype(jnp.int32).reshape(1)
    a0, s0, img, s40, vpack = call(
        functools.partial(k_first, nt, side, classes),
        [(act, F32), st, ((rows, 128), F32), ((40, 128), F32), ((val_each * side, 128), F32)],
        [train_labels, flip_flags, class_ids, clip_mask, val_labels]
        + [planes(train_images), planes(val_images), stem],
        smem=range(5),
        raw=range(8),
        us=4.5,
        after=[me],
    )
    b0 = far(s0, functools.partial(chan, rows * pairs * 2), vpack)
    (static,) = call(
        functools.partial(k_static, side), [((80, 128), F32)], [img, a0, s0], us=2.0, after=b0[:1]
    )
    forms = [((256, 384 * n), BF16) for n in (3, 3, 2, 2)]
    w1, w2, t1w, t2w, nv, hp, hpt, hb = call(
        k_weights,
        forms + [st, square, square, st],
        [convs.reshape(2, 9, 64, 64), norms, head.T],
        [square],
        raw=range(3),
        us=2.0,
    )
    moment_views = [
        (
            jnp.transpose(x[0], (1, 2, 3, 0, 4)),
            x[1].reshape(2, 9, 64, 64),
            x[2][0],
            jnp.transpose(x[3], (2, 0, 1)),
        )
        for x in ((m_stem, m_convs, m_norms, m_head), (v_stem, v_convs, v_norms, v_head))
    ]
    packed = call(
        k_params,
        [(PACKED, F32)] * 4,
        [stem, convs.reshape(2, 9, 64, 64), norms, head.T]
        + [x for views in moment_views for x in views]
        + [mom_stem, mom_convs.reshape(2, 9, 64, 64), mom_norms, mom_head.T],
        [square, square],
        raw=range(16),
        us=2.0,
    )

    act = (pairs, rows, 128)
    vact = (pairs, vrows, 128)

    def wide(r):
        return ((pairs, r, 256), BF16)

    va0, vs0, vimg = call(
        functools.partial(k_val_stem, side, val_each * side),
        [(vact, BF16), st, ((vrows, 128), F32)],
        [s40] + b0,
        us=2.4,
    )
    vchan = functools.partial(chan, vrows * pairs * 2)
    vb0 = near(vs0, team, vchan)

    def conv(n, layer, r, total, a, blocks, w, rider=(), after=()):
        pay = ((8 + (rider[0].shape[0] if rider else 0), 128), F32)
        return call(
            functools.partial(k_conv, n, side, len(blocks), layer, total, len(rider)),
            [((pairs, r, 128), F32 if n > 1 else BF16), pay, st] + [wide(r)] * (n == 1),
            [a, nv] + blocks + [w] + list(rider),
            [wide(r)] * n * (n > 1),
            us=6.7 if n > 1 else 3.3,
            after=after,
        )

    a1, s1, vec0 = conv(nt, 0, rows, count, a0, b0, w1, after=[static])
    b1 = far(s1, functools.partial(chan, rows * pairs * 2))
    va1, vs1, vvec0, vwide0 = conv(nval, 0, vrows, count_val, va0, vb0, w1, after=[s1])
    vb1 = near(vs1, team, vchan)
    va2, vs2, vvec1, vwide1 = conv(nval, 1, vrows, count_val, va1, vb1, w2, after=b1[:1])
    vb2 = near(vs2, team, vchan)
    a2, s2, vec1 = conv(nt, 1, rows, count, a1, b1, w2, [static, vec0, s0])
    b2 = far(s2, functools.partial(chan, rows * pairs * 2))

    vmz, vvec2, vgp, vextra = call(
        functools.partial(k_head, True, side, len(vb2), count_val, classes, group_val),
        [(vact, BF16), st, ((vimages, 128), F32), ((80, 128), F32)],
        [va2, va0, vvec0, nv, vimg, hp, hpt, hb] + vb2,
        us=4.0,
        after=[s2],
    )
    vextras = near(vextra, team, add)
    vdy1, vst1, g2 = call(
        functools.partial(k_val_back2, side, len(vextras), count_val),
        [(vact, BF16), st, ((576, 128), F32)],
        [va2, vmz, va1, vvec2, vvec1, vgp, t2w, vwide1] + vextras,
        [wide(vrows), ((384, 256), F32)],
        us=6.0,
        after=b2[:1],
    )
    vst1s = near(vst1, team, add)
    g2s = near(g2, team, add)
    g1, small = call(
        functools.partial(k_val_back1, side, len(vst1s), count_val),
        [((576, 128), F32), ((128, 128), F32)],
        [vdy1, va1, va0, vmz, vvec1, vvec0, vgp, t1w, vwide0, vimg] + vst1s,
        [wide(vrows), ((384, 256), F32), (vact, BF16)],
        us=7.0,
        after=b2[1:],
    )
    smalls = near(small, team, add)
    g1s = near(g1, team, add)

    tan1, th0, ts1 = call(
        functools.partial(k_tan1, side, len(b2), len(g1s), count, count_val),
        [(act, F32), (act, BF16), st],
        [img, a0, a1, vec0, vec1, w1, vvec0] + b2 + smalls + g1s + vst1s,
        [wide(rows), wide(rows), ((256, 384), BF16)],
        us=4.0,
    )
    tb1 = far(ts1, add)
    mz, vec2, info, gather = call(
        functools.partial(k_head, False, side, len(b2), count, classes, group_train),
        [(act, BF16), st, ((6, images, 128), F32), ((2 * images, 128), F32)],
        [a2, a0, vec0, nv, img, hp, hpt, hb] + b2,
        us=2.2,
        after=[ts1],
    )
    (ts2,) = call(
        functools.partial(k_tan2, side, len(tb1), len(g2s), count),
        [((3 * images + 8, 128), F32)],
        [tan1, th0, a1, a2, mz, vec1, vec2, w2, info, ts1, gather] + tb1 + g2s + vextras,
        [wide(rows), wide(rows), ((256, 384), BF16)],
        us=4.0,
    )
    dyn = far_list(ts2)

    nb_ = 2
    dy1, bs1, wgp = call(
        functools.partial(k_train_back2, side, len(dyn), count, group_train, nb_),
        [(act, F32), st, ((images + 80, 128), F32)],
        [norm_flag, a2, mz, a1, vec2, vec1, t2w, info] + dyn,
        [wide(rows)] * nb_,
        smem=(0,),
        us=4.3,
    )
    bb1 = far(bs1, add)
    (d2,) = call(
        functools.partial(k_dw2, side, nb_, count),
        [((576, 128), F32)],
        [a1, vec1, a2, vec2, mz, wgp],
        [((384, 256), F32)] + [wide(rows)] * nb_,
        us=3.6,
    )
    piece = (SHARD_ROWS + 8, 128)
    even, odd = call(
        functools.partial(k_train_back1, side, len(bb1), nb_, count),
        [((4,) + piece, F32)] * 2,
        [me, dy1, a1, a0, mz, vec1, vec0, t1w, img, wgp, d2, bs1] + bb1,
        [((384, 256), F32), ((576, 128), F32), square, (act, F32)] + [wide(rows)] * (2 * nb_),
        smem=(0,),
        us=9.0,
    )

    k = SHARDS
    while k < dp:
        even, odd = even + swap(even, k, dp), odd + swap(odd, k, dp)
        k *= 2
    halves = call(k_halves, [(piece, F32)] * 4, [even, swap(odd, 1, dp)])
    parts = [halves[0]] + [swap(halves[k], 2 * k, dp) for k in range(1, 4)]
    grad, delta, rest = call(
        functools.partial(k_adam, count, len(b2)),
        [(piece, F32), (piece, F32), st],
        [me] + parts + b2 + list(packed[:3]) + [vec0],
        [square, square],
        smem=(0,),
    )
    groups = lax.axis_size("group")
    deltas = [delta] + [
        lax.ppermute(delta, "group", [(i, i ^ k) for i in range(groups)])
        for k in range(1, groups)
    ]
    pay, norm = call(
        functools.partial(k_total, groups),
        [((2 * SHARD_ROWS, 128), F32), ((16, 128), F32)],
        [grad] + deltas,
    )
    pays = []
    for k in range(4):
        x = swap(pay, 2 * k, dp) if k else pay
        pays += [x, swap(x, 1, dp)]
    p4 = [(3, 3, 3, 64), (2, 9, 64, 64), (3, 2, 64), (classes, head.shape[0])]
    g4 = [(3, 3, 3, 1, 64), (2, 9, 64, 64), (3, 2, 64), (classes, 1, head.shape[0])]
    outs = call(
        functools.partial(k_update, groups, classes),
        [(x, F32) for x in p4]
        + [(x, BF16) for x in p4]
        + [(x, F32) for x in g4 + g4 + p4]
        + [((1,), F32)],
        [me] + pays + [norm, rest] + list(packed),
        [(PACKED, F32)] * 2,
        smem=(0,),
    )

    def plain(stem, convs, norms, head):
        return [stem, convs.reshape(2, 3, 3, 64, 64), norms, head.T]

    def own(stem, convs, norms, head):
        return [
            jnp.transpose(stem, (3, 0, 1, 2, 4)),
            convs.reshape(1, 2, 3, 3, 64, 64),
            norms[None],
            jnp.transpose(head, (1, 2, 0)),
        ]

    return (
        *plain(*outs[0:4]),
        *plain(*outs[4:8]),
        *own(*outs[8:12]),
        *own(*outs[12:16]),
        *plain(*outs[16:20]),
        outs[20],
    )


def solution(mesh):
    split4 = P(("group", "dp"), None, None, None)
    split1 = P(("group", "dp"))
    group = P("group")
    whole = P()
    return jax.shard_map(
        body,
        mesh=mesh,
        in_specs=(split4, split1, split1, split1, split1, group, split4, split1)
        + (whole,) * 4
        + (group,) * 8
        + (whole,) * 4,
        out_specs=(whole,) * 8 + (group,) * 8 + (whole,) * 4 + (group,),
        check_vma=False,
    )
```
